256 devices in a mesh: lon: 64 (over y_lo, z, x), lat: 2 (over y_hi), head: 2 (over core).
Axes of the slice: x: 4, y: 4 (y_hi: 2, y_lo: 2; y = y_hi * 2 + y_lo), z: 8, core: 2. Of those that a mesh axis runs over, the one named last changes fastest.
Arguments:
- tokens: bfloat16 [2, 24, 384, 1024], P(None, 'lat', 'lon', 'head')
- grad_out: bfloat16 [2, 24, 384, 1024], P(None, 'lat', 'lon', 'head'), may hold values from -16 to 16
- w_qkv: bfloat16 [3, 1024, 1024], P(None, None, 'head')
- w_out: bfloat16 [1024, 1024], P('head'), may hold values from -0.1875 to 0.1875
- band_count: int32 [24], replicated, may hold values from 96 to 384
- lat_shift: int32 [1], replicated, may hold values from 1 to 11
- lon_shift: int32 [1], replicated, may hold values from 1 to 5
Outputs:
- grad_tokens: bfloat16 [2, 24, 384, 1024], P(None, 'lat', 'lon', 'head')
- grad_qkv: float32 [3, 1024, 1024], P(None, ('lon', 'lat'), 'head')
The draws below stay inside these ranges and needn't reach their ends.
All inputs are finite; a program needn't handle non-finite values.
Results may differ from the reference program's by a relative error of at most 0.012.
The reference program's roundings to bfloat16 on the way (of `probs_b`, `grad_attended`, `grad_values` and `grad_scores`) count: a program that leaves them out, or rounds other values in their place, can miss the bound.
Values may be sent and summed in bfloat16 or wider, within the bound.
A program may use at most 448 MiB of HBM per device.

```python
import jax
import jax.numpy as jnp
from jax import lax

D = 1024
HEAD_DIM = 64
LEV = 2
WLAT = 12
WLON = 6
CLON = 6
NLAT = 24
NLON = 384
N_LON = 64


def draw_tokens(key, part):
    key = jax.random.fold_in(key, 11)
    value_key = jax.random.fold_in(key, 1)
    full_shape = (LEV, NLAT, NLON, D)
    values = jnp.clip(jax.random.normal(value_key, full_shape, jnp.float32), -6.0, 6.0)
    return values.astype(jnp.bfloat16)


def draw_w_qkv(key, part):
    key = jax.random.fold_in(key, 23)
    main_key = jax.random.fold_in(key, 0)
    initial = jax.random.normal(main_key, (3, D, D), jnp.float32) * D ** (-0.5)
    return initial.astype(jnp.bfloat16)


def touch_ends(entries, key, least, top_value):
    longest = entries.shape.index(max(entries.shape))
    spots = []
    for shift in (0, 1):
        where = [jax.random.randint(jax.random.fold_in(key, axis), (), 0, length) for axis, length in enumerate(entries.shape)]
        where[longest] = (where[longest] + shift) % entries.shape[longest]
        spots.append(tuple(where))
    return entries.at[spots[0]].set(least).at[spots[1]].set(top_value)


def strengthened(result, stream_key, source, target, shards_of, factor):
    def block_of(position):
        return (jnp.arange(result.shape[position]) // (result.shape[position] // shards_of)).reshape((-1,) + (1,) * (result.ndim - 1 - position))

    one_side = jax.random.permutation(stream_key, shards_of)[block_of(target)]
    other_side = (block_of(target) + shards_of // 2) % shards_of
    return jnp.where((block_of(source) == one_side) | (block_of(source) == other_side), factor * result, result)


def shard_levels(stream_key, dims, cuts, least, high):
    def one(axis_at, shards_of):
        steps = jax.random.uniform(jax.random.fold_in(jax.random.fold_in(stream_key, 6), axis_at), (shards_of,), jnp.float32, least / len(cuts), high / len(cuts))
        return jnp.repeat(jnp.exp(steps), dims[axis_at] // shards_of).reshape((-1,) + (1,) * (len(dims) - axis_at - 1))

    loudness = one(*cuts[0])
    for cut in cuts[1:]:
        loudness = loudness * one(*cut)
    return loudness


def scatter_about(own_key, shape, spread, limit, cuts=(), kind=jnp.bfloat16):
    entries = spread * jax.random.normal(own_key, shape, jnp.float32)
    if cuts:
        entries = entries * shard_levels(own_key, shape, cuts, -0.22, 0.18)
    return jnp.clip(entries, -limit, limit).astype(kind)


def gaussian_with(key, extent, spread, reach, pieces, heavy, kind=jnp.bfloat16):
    entries = spread * jax.random.normal(key, extent, jnp.float32)
    if pieces:
        entries = entries * shard_levels(key, extent, pieces, -0.22, 0.18)
    return jnp.clip(strengthened(entries, jax.random.fold_in(key, 3), *heavy), -reach, reach).astype(kind)


def setup_inputs(seed: int = 0) -> dict:
    key_list = jax.random.split(jax.random.key(seed), 8)
    tokens = draw_tokens(jax.random.fold_in(key_list[7], 71), 0)
    grad_out = gaussian_with(key_list[1], (LEV, NLAT, NLON, D), 1.0, 16.0, ((1, 2), (2, 64), (3, 2)), (2, 3, 64, 4.0))
    w_qkv = draw_w_qkv(jax.random.fold_in(key_list[7], 71), 0)
    w_out = scatter_about(key_list[3], (D, D), D ** -0.5, 0.1875, ((0, 2),))
    band_count = touch_ends(jax.random.randint(key_list[4], (NLAT,), NLON // 4, NLON + 1), jax.random.fold_in(key_list[4], 1), NLON // 4, NLON).astype(jnp.int32)
    lat_shift = jax.random.randint(key_list[5], (1,), 1, WLAT).astype(jnp.int32)
    lon_shift = jax.random.randint(key_list[6], (1,), 1, WLON).astype(jnp.int32)
    return {"tokens": tokens, "grad_out": grad_out, "w_qkv": w_qkv, "w_out": w_out, "band_count": band_count, "lat_shift": lat_shift, "lon_shift": lon_shift}


def rounded(array):
    return lax.optimization_barrier(array.astype(jnp.bfloat16))


def window_backward(shifted, grad_shifted, is_valid, seam_side, w_query, w_keys, w_values, w_out):
    windows, window, model_width = shifted.shape
    flat_in = shifted.reshape(-1, model_width)
    flat_grad = grad_shifted.reshape(-1, model_width)
    query = rounded(jnp.dot(flat_in, w_query, preferred_element_type=jnp.float32))
    keys = rounded(jnp.dot(flat_in, w_keys, preferred_element_type=jnp.float32))
    values = rounded(jnp.dot(flat_in, w_values, preferred_element_type=jnp.float32))
    columns = w_query.shape[1]
    head_count = columns // HEAD_DIM
    score_scale = HEAD_DIM ** -0.5

    def per_head(array):
        return array.reshape(windows, window, head_count, HEAD_DIM).astype(jnp.float32)

    scores = jnp.einsum('pqhe,pkhe->phqk', per_head(query), per_head(keys)) * score_scale
    itself = jnp.eye(window, dtype=bool)
    allowed = (is_valid[:, None, :] | itself[None]) & (seam_side[:, :, None] == seam_side[:, None, :])
    scores = jnp.where(allowed[:, None], scores, jnp.float32(-1e30))
    highest = jnp.max(scores, -1, keepdims=True)
    raised = jnp.exp(scores - highest)
    attn_probs = raised / jnp.sum(raised, -1, keepdims=True)
    probs_b = rounded(attn_probs).astype(jnp.float32)
    grad_attended = rounded(jnp.dot(flat_grad, w_out.T, preferred_element_type=jnp.float32))
    grad_heads = per_head(grad_attended)
    grad_values = rounded(jnp.einsum('phqk,pqhe->pkhe', probs_b, grad_heads)).reshape(-1, columns)
    grad_probs = jnp.einsum('pqhe,pkhe->phqk', grad_heads, per_head(values))
    inner = jnp.sum(attn_probs * grad_probs, -1, keepdims=True)
    grad_scores = rounded(attn_probs * (grad_probs - inner) * score_scale).astype(jnp.float32)
    grad_query = rounded(jnp.einsum('phqk,pkhe->pqhe', grad_scores, per_head(keys))).reshape(-1, columns)
    grad_keys = rounded(jnp.einsum('phqk,pqhe->pkhe', grad_scores, per_head(query))).reshape(-1, columns)
    grad_in = jnp.dot(grad_query, w_query.T, preferred_element_type=jnp.float32)
    grad_in = grad_in + jnp.dot(grad_keys, w_keys.T, preferred_element_type=jnp.float32)
    grad_in = grad_in + jnp.dot(grad_values, w_values.T, preferred_element_type=jnp.float32)
    weight_terms = jnp.stack([jnp.dot(flat_in.T, grad_query, preferred_element_type=jnp.float32),
                              jnp.dot(flat_in.T, grad_keys, preferred_element_type=jnp.float32),
                              jnp.dot(flat_in.T, grad_values, preferred_element_type=jnp.float32)])
    return grad_in, weight_terms


def to_groups(array):
    features = array.shape[-1]
    shaped = array.reshape(LEV, NLAT // WLAT, WLAT, NLON // WLON, WLON, features)
    shaped = shaped.transpose(1, 3, 0, 2, 4, 5)
    return shaped.reshape((NLAT // WLAT) * N_LON, CLON // WLON, LEV * WLAT * WLON, features)


def reference(tokens, grad_out, w_qkv, w_out, band_count, lat_shift, lon_shift):
    row_shift = lat_shift[0]
    col_shift = lon_shift[0]
    shifted = jnp.roll(tokens, (-row_shift, -col_shift), axis=(1, 2))
    grad_shifted = jnp.roll(grad_out, (-row_shift, -col_shift), axis=(1, 2))
    raw_rows = jnp.arange(NLAT, dtype=jnp.int32) + row_shift
    glob_rows = raw_rows % NLAT
    glob_cols = (jnp.arange(NLON, dtype=jnp.int32) + col_shift) % NLON
    is_valid = glob_cols[None, :] < band_count[glob_rows][:, None]
    seam_side = jnp.broadcast_to((raw_rows >= NLAT)[:, None], (NLAT, NLON))
    masks = jnp.stack([is_valid, seam_side], -1).astype(jnp.int32)
    masks = jnp.broadcast_to(masks[None], (LEV, NLAT, NLON, 2))
    inputs = (to_groups(shifted), to_groups(grad_shifted), to_groups(masks))

    def scan_step(totals, group):
        group_in, group_grad, group_mask = group
        grad_in, weight_terms = window_backward(
            group_in, group_grad, group_mask[..., 0] > 0, group_mask[..., 1],
            w_qkv[0], w_qkv[1], w_qkv[2], w_out)
        return totals + weight_terms, grad_in.reshape(group_in.shape[0], group_in.shape[1], D)

    initial = jnp.zeros((3, D, D), jnp.float32)
    totals, grad_windows = lax.scan(scan_step, initial, inputs)
    grid = grad_windows.reshape(NLAT // WLAT, NLON // WLON, LEV, WLAT, WLON, D)
    grid = grid.transpose(2, 0, 3, 1, 4, 5).reshape(LEV, NLAT, NLON, D)
    grad_tokens = jnp.roll(grid, (row_shift, col_shift), axis=(1, 2)).astype(jnp.bfloat16)
    return grad_tokens, totals
```

```python
import functools

import jax
import jax.numpy as jnp
from jax import lax
from jax.experimental import pallas as pl
from jax.experimental.pallas import tpu as pltpu
from jax.sharding import PartitionSpec as P

MESH = pl.DeviceIdType.MESH
HEAD_DIM = 64
LEV = 2
WLAT = 12
WLON = 6
NX = 4
NZ = 8
TOK = LEV * WLAT * WLON
COL = LEV * WLAT
EDGE = 80
SLOTS = 80
HALF_ROWS = WLAT // 2
EXT = TOK + 2 * EDGE
F32 = jnp.float32
BF16 = jnp.bfloat16


def nn(a, b):
    return lax.dot_general(a, b, (((1,), (0,)), ((), ())), preferred_element_type=F32)


def nt(a, b):
    return lax.dot_general(a, b, (((1,), (1,)), ((), ())), preferred_element_type=F32)


def tn(a, b):
    return lax.dot_general(a, b, (((0,), (0,)), ((), ())), preferred_element_type=F32)


def iota(shape, axis):
    return lax.broadcasted_iota(jnp.int32, shape, axis)


def by24(t):
    return (t * 171) >> 12


def by12(t):
    return (t * 342) >> 12


def by6(t):
    return (t * 43) >> 8


def one_hot(cond):
    return jnp.where(cond, 1.0, 0.0).astype(BF16)


def kernel(
    sizes,
    band_ref,
    lat_ref,
    lon_ref,
    tok_ref,
    gout_ref,
    wqkv_hbm,
    wout_hbm,
    gtok_ref,
    gw_ref,
    wqkv,
    wout,
    ext,
    lat_send,
    lat_recv,
    xg,
    go,
    bias,
    qkv,
    ga,
    gall,
    gsend,
    grecv,
    gin,
    gin_recv,
    back_send,
    back_recv,
    side_send,
    side_recv,
    pfull,
    ysend,
    yrecv,
    rz,
    zsend,
    zrecv,
    rx,
    xrecv,
    w_sem,
    halo_send_sem,
    halo_recv_sem,
    lat_send_sem,
    lat_recv_sem,
    core_send_sem,
    core_recv_sem,
    xg_send_sem,
    xg_recv_sem,
    relay_send_sem,
    relay_recv_sem,
    g_send_sem,
    g_recv_sem,
    y_send_sem,
    y_recv_sem,
    z_send_sem,
    z_recv_sem,
    x_send_sem,
    x_recv_sem,
):
    n_lon, n_lat, width, half = sizes
    n_ylo = n_lon // (NX * NZ)
    n_y = n_lat * n_ylo
    cut = half // NX
    lon = lax.axis_index("lon")
    lat = lax.axis_index("lat")
    core = lax.axis_index("head")
    x = lon % NX
    z = (lon // NX) % NZ
    ylo = lon // (NX * NZ)
    y = lat * n_ylo + ylo

    right = ((lon + 1) % n_lon, lat, core)
    left = ((lon + n_lon - 1) % n_lon, lat, core)
    across = (lon, (lat + 1) % n_lat, core)
    sibling = (lon, lat, 1 - core)

    def x_peer(d):
        return (lon - x + (x + d) % NX, lat, core)

    def y_peer(d):
        other = (y + d) % n_y
        return (lon + (other % n_ylo - ylo) * (NX * NZ), other // n_ylo, core)

    def z_peer(d):
        return (lon + ((z + d) % NZ - z) * NX, lat, core)

    partners = [right, left, across, sibling]
    partners += [x_peer(d) for d in range(1, NX)]
    partners += [y_peer(d) for d in range(1, n_y)]
    partners += [z_peer(d) for d in range(1, NZ)]

    def remote(src, dst, send_sem, recv_sem, device):
        return pltpu.make_async_remote_copy(
            src_ref=src,
            dst_ref=dst,
            send_sem=send_sem,
            recv_sem=recv_sem,
            device_id=device,
            device_id_type=MESH,
        )

    barrier = pltpu.get_barrier_semaphore()
    for partner in partners:
        pl.semaphore_signal(barrier, inc=1, device_id=partner, device_id_type=MESH)

    load_qkv = pltpu.make_async_copy(wqkv_hbm, wqkv, w_sem.at[0])
    load_out = pltpu.make_async_copy(wout_hbm, wout, w_sem.at[1])
    load_qkv.start()
    load_out.start()

    row_shift = lat_ref[0]
    col_shift = lon_ref[0]
    row_swap = jnp.where(row_shift > HALF_ROWS, 1, 0)
    col_swap = jnp.where(col_shift > WLON // 2, 1, 0)
    f = row_shift - WLAT * row_swap
    e = col_shift - WLON * col_swap

    ext[0, EDGE : EDGE + TOK] = tok_ref[...]
    ext[1, EDGE : EDGE + TOK] = gout_ref[...]

    t = iota((TOK, EXT), 0)
    u = iota((TOK, EXT), 1)
    row = t - WLAT * by12(t) + f
    stays = (row >= 0) & (row < WLAT)
    keep_hot = one_hot(stays & (u == t + (EDGE + COL * e + f)))

    s = iota((SLOTS, EXT), 0)
    u = iota((SLOTS, EXT), 1)
    send_hot = one_hot(
        (u == s + HALF_ROWS * by6(s) + (EDGE + COL * e + HALF_ROWS * row_swap))
        & (s < TOK // 2)
    )

    t = iota((TOK, SLOTS), 0)
    s = iota((TOK, SLOTS), 1)
    group = by12(t)
    row = t - WLAT * group + f
    leaves = (row < 0) | (row >= WLAT)
    wrapped = jnp.where(row < 0, row + WLAT, row - WLAT)
    take_hot = one_hot(leaves & (s == HALF_ROWS * group + wrapped - HALF_ROWS * row_swap))

    k_at = iota((TOK, TOK), 0)
    q_at = iota((TOK, TOK), 1)
    first_row = WLAT * ((lat + row_swap) % n_lat) + row_shift
    k_row = k_at - WLAT * by12(k_at)
    q_row = q_at - WLAT * by12(q_at)
    n_rows = WLAT * n_lat
    counts = jnp.zeros((TOK, TOK), jnp.int32)
    for r in range(WLAT):
        raw = first_row + r
        counts = jnp.where(k_row == r, band_ref[jnp.where(raw >= n_rows, raw - n_rows, raw)], counts)
    n_cols = WLON * n_lon
    k_col = by24(k_at) + (WLON * lon + e)
    k_col = jnp.where(k_col < 0, k_col + n_cols, k_col)
    k_col = jnp.where(k_col >= n_cols, k_col - n_cols, k_col)
    same_side = (k_row + first_row >= n_rows) == (q_row + first_row >= n_rows)
    allowed = ((k_col < counts) | (k_at == q_at)) & same_side
    bias[...] = jnp.where(allowed, 0.0, -1e30)

    pl.semaphore_wait(barrier, len(partners))

    halo = []
    for a in range(2):
        to_left = remote(
            ext.at[a, EDGE : 2 * EDGE],
            ext.at[a, EDGE + TOK : EXT],
            halo_send_sem.at[a, 0],
            halo_recv_sem.at[a, 0],
            left,
        )
        to_right = remote(
            ext.at[a, TOK : TOK + EDGE],
            ext.at[a, 0:EDGE],
            halo_send_sem.at[a, 1],
            halo_recv_sem.at[a, 1],
            right,
        )
        to_left.start()
        to_right.start()
        halo.append((to_left, to_right))

    sends = []
    over_lat = []
    kept = []
    for a in range(2):
        for copy in halo[a]:
            copy.wait_recv()
        wide = ext[a]
        lat_send[a] = nn(send_hot, wide).astype(BF16)
        copy = remote(
            lat_send.at[a], lat_recv.at[a], lat_send_sem.at[a], lat_recv_sem.at[a], across
        )
        copy.start()
        over_lat.append(copy)
        kept.append(nn(keep_hot, wide))
    sends += [copy for pair in halo for copy in pair]
    sends += over_lat

    over_core = []
    over_x = []
    for a in range(2):
        over_lat[a].wait_recv()
        window = (kept[a] + nn(take_hot, lat_recv[a])).astype(BF16)
        if a == 0:
            xg[0, core] = window
            mine = xg.at[0, core]
        else:
            go[core] = window
            mine = go.at[core]
        copy = remote(mine, mine, core_send_sem.at[a], core_recv_sem.at[a], sibling)
        copy.start()
        over_core.append(copy)
        if a == 0:
            for d in range(1, NX):
                copy = remote(
                    xg.at[0, core],
                    xg.at[d, core],
                    xg_send_sem.at[d],
                    xg_recv_sem.at[d],
                    x_peer(d),
                )
                copy.start()
                over_x.append(copy)
    sends += over_core + over_x

    load_qkv.wait()
    over_core[0].wait_recv()
    for j in range(3):
        total = nn(xg[0, 0], wqkv[j, :half]) + nn(xg[0, 1], wqkv[j, half:])
        qkv[j] = total.astype(BF16)
    load_out.wait()
    over_core[1].wait_recv()
    ga[...] = (nt(go[0], wout[:, :half]) + nt(go[1], wout[:, half:])).astype(BF16)

    relays = []
    for d in range(1, NX):
        over_x[d - 1].wait_recv()
        copy = remote(
            xg.at[d, core],
            xg.at[d, core],
            relay_send_sem.at[d],
            relay_recv_sem.at[d],
            sibling,
        )
        copy.start()
        relays.append(copy)
    sends += relays

    scale = HEAD_DIM ** (-0.5)
    over_g = {}
    for n in range(NX):
        d = (n + 1) % NX
        part = pl.ds(pl.multiple_of(((x + d) % NX) * cut, cut), cut)
        q_part, k_part, v_part = (qkv[j, :, part] for j in range(3))
        g_part = ga[:, part]
        outs = [[], [], []]
        for head in range(cut // HEAD_DIM):
            at = slice(head * HEAD_DIM, (head + 1) * HEAD_DIM)
            q, k, v, g = q_part[:, at], k_part[:, at], v_part[:, at], g_part[:, at]
            scores = jnp.where(bias[...] == 0.0, nt(k, q) * scale, -1e30)
            raised = jnp.exp(scores - jnp.max(scores, 0, keepdims=True))
            probs = raised * (1.0 / jnp.sum(raised, 0, keepdims=True))
            grad_probs = nt(v, g)
            inner = jnp.sum(probs * grad_probs, 0, keepdims=True)
            grad_scores = (probs * (grad_probs - inner) * scale).astype(BF16)
            outs[0].append(tn(grad_scores, k).astype(BF16))
            outs[1].append(nn(grad_scores, q).astype(BF16))
            outs[2].append(nn(probs.astype(BF16), g).astype(BF16))
        for j in range(3):
            joined = jnp.concatenate(outs[j], 1)
            gall[j, :, part] = joined
            gsend[d, :, j * cut : (j + 1) * cut] = joined
        if d:
            copy = remote(
                gsend.at[d], grecv.at[d], g_send_sem.at[d], g_recv_sem.at[d], x_peer(d)
            )
            copy.start()
            over_g[d] = copy
    sends += list(over_g.values())

    def grad_in(which):
        rows = pl.ds(pl.multiple_of(which * half, half), half)
        return (
            nt(gall[0], wqkv[0, rows]) + nt(gall[1], wqkv[1, rows]) + nt(gall[2], wqkv[2, rows])
        )

    gin[0] = grad_in(1 - core)
    to_sibling = remote(gin.at[0], gin_recv, core_send_sem.at[2], core_recv_sem.at[2], sibling)
    to_sibling.start()
    gin[1] = grad_in(core)

    for copy in relays:
        copy.wait_recv()
    for d in range(1, NX):
        over_g[d].wait_recv()
    blocks = pfull.shape[0]
    own = pfull.shape[2]
    for side in range(2):
        total = tn(xg[0, side], gsend[0])
        for d in range(1, NX):
            total = total + tn(xg[d, side], grecv[d])
        pfull[side * (blocks // 2) : (side + 1) * (blocks // 2)] = total.reshape(
            blocks // 2, n_lat, own, 3 * cut
        )

    def y_rows(which):
        lo = which % n_ylo
        return pfull[pl.ds(lo * (NZ * NX), NZ * NX), which // n_ylo]

    over_y = []
    for d in range(1, n_y):
        ysend[d] = y_rows((y + d) % n_y).reshape(NZ * NX * own, 3 * cut).astype(BF16)
        copy = remote(
            ysend.at[d], yrecv.at[d], y_send_sem.at[d], y_recv_sem.at[d], y_peer(d)
        )
        copy.start()
        over_y.append(copy)
    sends += over_y

    to_sibling.wait_recv()
    window = (gin[1] + gin_recv[...]).astype(BF16)
    s = iota((SLOTS, TOK), 0)
    t = iota((SLOTS, TOK), 1)
    group = by12(t)
    row = t - WLAT * group + f
    leaves = (row < 0) | (row >= WLAT)
    wrapped = jnp.where(row < 0, row + WLAT, row - WLAT)
    give_hot = one_hot(leaves & (s == HALF_ROWS * group + wrapped - HALF_ROWS * row_swap))
    back_send[...] = nn(give_hot, window).astype(BF16)
    over_lat_back = remote(
        back_send, back_recv, lat_send_sem.at[2], lat_recv_sem.at[2], across
    )
    over_lat_back.start()
    b = iota((TOK, TOK), 0)
    t = iota((TOK, TOK), 1)
    row = b - WLAT * by12(b) - f
    stay_hot = one_hot((row >= 0) & (row < WLAT) & (t == b - f))
    kept = nn(stay_hot, window)
    b = iota((TOK, SLOTS), 0)
    s = iota((TOK, SLOTS), 1)
    group = by12(b)
    row = b - WLAT * group
    was = row - f
    came = (was < 0) | (was >= WLAT)
    back_hot = one_hot(came & (s == HALF_ROWS * group + row - HALF_ROWS * row_swap))
    over_lat_back.wait_recv()
    grid = (kept + nn(back_hot, back_recv[...])).astype(BF16)
    s = iota((EDGE, TOK), 0)
    t = iota((EDGE, TOK), 1)
    place = t + COL * e
    side_send[0] = nn(one_hot((place < 0) & (s == place + EDGE)), grid).astype(BF16)
    side_send[1] = nn(one_hot((place >= TOK) & (s == place - TOK)), grid).astype(BF16)
    side_left = remote(
        side_send.at[0], side_recv.at[0], halo_send_sem.at[2, 0], halo_recv_sem.at[2, 0], left
    )
    side_right = remote(
        side_send.at[1], side_recv.at[1], halo_send_sem.at[2, 1], halo_recv_sem.at[2, 1], right
    )
    side_left.start()
    side_right.start()
    sends += [to_sibling, over_lat_back, side_left, side_right]
    b = iota((TOK, TOK), 0)
    t = iota((TOK, TOK), 1)
    home = nn(one_hot(b == t + COL * e), grid)

    total = y_rows(y).reshape(NZ * NX * own, 3 * cut)
    for d in range(1, n_y):
        over_y[d - 1].wait_recv()
        total = total + yrecv[d].astype(F32)
    rz[...] = total.reshape(NZ, NX * own, 3 * cut)
    over_z = []
    for d in range(1, NZ):
        zsend[d] = rz[(z + d) % NZ].astype(BF16)
        copy = remote(
            zsend.at[d], zrecv.at[d], z_send_sem.at[d], z_recv_sem.at[d], z_peer(d)
        )
        copy.start()
        over_z.append(copy)
    sends += over_z

    side_left.wait_recv()
    side_right.wait_recv()
    b = iota((TOK, EDGE), 0)
    s = iota((TOK, EDGE), 1)
    from_right = nn(one_hot(b == s + (TOK - EDGE)), side_recv[0])
    from_left = nn(one_hot(b == s), side_recv[1])
    gtok_ref[...] = (home + from_right + from_left).astype(BF16)

    total = rz[z]
    for d in range(1, NZ):
        over_z[d - 1].wait_recv()
        total = total + zrecv[d].astype(F32)
    rx[...] = total.reshape(NX, own, 3 * cut)
    last = []
    for d in range(1, NX):
        copy = remote(
            rx.at[(x + d) % NX], xrecv.at[d], x_send_sem.at[d], x_recv_sem.at[d], x_peer(d)
        )
        copy.start()
        last.append(copy)
    for d in range(NX):
        if d:
            last[d - 1].wait_recv()
            piece = xrecv[d]
        else:
            piece = rx[x]
        part = pl.ds(pl.multiple_of(((x + NX - d) % NX) * cut, cut), cut)
        for j in range(3):
            gw_ref[j, :, part] = piece[:, j * cut : (j + 1) * cut]
    sends += last

    for copy in sends:
        copy.wait_send()


def solution(mesh):
    n_lon, n_lat = mesh.shape["lon"], mesh.shape["lat"]

    def flat(array):
        return array.transpose(2, 0, 1, 3).reshape(TOK, array.shape[-1])

    def shards(tokens, grad_out, w_qkv, w_out, band_count, lat_shift, lon_shift):
        half = tokens.shape[-1]
        width = w_qkv.shape[1]
        own = width // (n_lon * n_lat)
        n_y = n_lon // (NX * NZ) * n_lat
        cut = half // NX
        vmem = pl.BlockSpec(memory_space=pltpu.VMEM)
        smem = pl.BlockSpec(memory_space=pltpu.SMEM)
        hbm = pl.BlockSpec(memory_space=pl.ANY)
        dma = pltpu.SemaphoreType.DMA
        gtok, gw = pl.pallas_call(
            functools.partial(kernel, (n_lon, n_lat, width, half)),
            out_shape=(
                jax.ShapeDtypeStruct((TOK, half), BF16),
                jax.ShapeDtypeStruct((3, own, half), F32),
            ),
            in_specs=[smem, smem, smem, vmem, vmem, hbm, hbm],
            out_specs=(vmem, vmem),
            scratch_shapes=[
                pltpu.VMEM((3, width, half), BF16),
                pltpu.VMEM((half, width), BF16),
                pltpu.VMEM((2, EXT, half), BF16),
                pltpu.VMEM((2, SLOTS, half), BF16),
                pltpu.VMEM((2, SLOTS, half), BF16),
                pltpu.VMEM((NX, 2, TOK, half), BF16),
                pltpu.VMEM((2, TOK, half), BF16),
                pltpu.VMEM((TOK, TOK), F32),
                pltpu.VMEM((3, TOK, half), BF16),
                pltpu.VMEM((TOK, half), BF16),
                pltpu.VMEM((3, TOK, half), BF16),
                pltpu.VMEM((NX, TOK, 3 * cut), BF16),
                pltpu.VMEM((NX, TOK, 3 * cut), BF16),
                pltpu.VMEM((2, TOK, half), F32),
                pltpu.VMEM((TOK, half), F32),
                pltpu.VMEM((SLOTS, half), BF16),
                pltpu.VMEM((SLOTS, half), BF16),
                pltpu.VMEM((2, EDGE, half), BF16),
                pltpu.VMEM((2, EDGE, half), BF16),
                pltpu.VMEM((n_lon, n_lat, own, 3 * cut), F32),
                pltpu.VMEM((n_y, NZ * NX * own, 3 * cut), BF16),
                pltpu.VMEM((n_y, NZ * NX * own, 3 * cut), BF16),
                pltpu.VMEM((NZ, NX * own, 3 * cut), F32),
                pltpu.VMEM((NZ, NX * own, 3 * cut), BF16),
                pltpu.VMEM((NZ, NX * own, 3 * cut), BF16),
                pltpu.VMEM((NX, own, 3 * cut), F32),
                pltpu.VMEM((NX, own, 3 * cut), F32),
                dma((2,)),
                dma((3, 2)),
                dma((3, 2)),
                dma((3,)),
                dma((3,)),
                dma((3,)),
                dma((3,)),
                dma((NX,)),
                dma((NX,)),
                dma((NX,)),
                dma((NX,)),
                dma((NX,)),
                dma((NX,)),
                dma((n_y,)),
                dma((n_y,)),
                dma((NZ,)),
                dma((NZ,)),
                dma((NX,)),
                dma((NX,)),
            ],
            compiler_params=pltpu.CompilerParams(
                collective_id=0, has_side_effects=True, vmem_limit_bytes=48 * 2**20
            ),
        )(band_count, lat_shift, lon_shift, flat(tokens), flat(grad_out), w_qkv, w_out)
        gtok = gtok.reshape(WLON, LEV, WLAT, half).transpose(1, 2, 0, 3)
        return gtok, gw

    in_specs = (
        P(None, "lat", "lon", "head"),
        P(None, "lat", "lon", "head"),
        P(None, None, "head"),
        P("head", None),
        P(),
        P(),
        P(),
    )
    out_specs = (P(None, "lat", "lon", "head"), P(None, ("lon", "lat"), "head"))
    return jax.shard_map(shards, mesh=mesh, in_specs=in_specs, out_specs=out_specs, check_vma=False)
```

```python
import functools

import jax
import jax.numpy as jnp
from jax import lax
from jax.experimental import pallas as pl
from jax.experimental.pallas import tpu as pltpu
from jax.sharding import PartitionSpec as P

MESH = pl.DeviceIdType.MESH
HEAD_DIM = 64
LEV = 2
WLAT = 12
WLON = 6
NX = 4
NZ = 8
TOK = LEV * WLAT * WLON
ROW = LEV * WLON
HALF_ROWS = WLAT // 2
HALF_COLS = WLON // 2
F32 = jnp.float32
BF16 = jnp.bfloat16


def nn(a, b):
    return lax.dot_general(a, b, (((1,), (0,)), ((), ())), preferred_element_type=F32)


def nt(a, b):
    return lax.dot_general(a, b, (((1,), (1,)), ((), ())), preferred_element_type=F32)


def tn(a, b):
    return lax.dot_general(a, b, (((0,), (0,)), ((), ())), preferred_element_type=F32)


def iota(shape, axis):
    return lax.broadcasted_iota(jnp.int32, shape, axis)


def by12(t):
    return (t * 342) >> 12


def kernel(
    sizes,
    band_ref,
    lat_ref,
    lon_ref,
    tok_hbm,
    gout_hbm,
    wqkv_hbm,
    wout_hbm,
    gtok_ref,
    gw_ref,
    wqkv,
    wout,
    tok_wide,
    gout_wide,
    tok_rows,
    gout_rows,
    lat_send,
    xo,
    xg,
    go,
    bias,
    qkv,
    ga,
    gall,
    own_qk,
    own_v,
    qk_recv,
    v_recv,
    gin,
    gin_recv,
    back_own,
    back_rows,
    back_send,
    side_own,
    side_cols,
    side_send,
    pw,
    pn,
    wsend,
    wrecv,
    nsend,
    nrecv,
    rz,
    zsend,
    zrecv,
    rw,
    rn,
    fw,
    fn,
    load_sem,
    halo_send_sem,
    halo_recv_sem,
    lat_send_sem,
    lat_recv_sem,
    core_send_sem,
    core_recv_sem,
    xg_send_sem,
    xg_recv_sem,
    relay_send_sem,
    relay_recv_sem,
    g_send_sem,
    g_recv_sem,
    p_send_sem,
    p_recv_sem,
    z_send_sem,
    z_recv_sem,
    f_send_sem,
    f_recv_sem,
):
    n_lon, n_lat, width, half = sizes
    n_ylo = n_lon // (NX * NZ)
    n_y = n_lat * n_ylo
    assert n_y == NX
    cut = half // NX
    lon = lax.axis_index("lon")
    lat = lax.axis_index("lat")
    core = lax.axis_index("head")
    x = lon % NX
    z = (lon // NX) % NZ
    ylo = lon // (NX * NZ)
    y = lat * n_ylo + ylo

    right = ((lon + 1) % n_lon, lat, core)
    left = ((lon + n_lon - 1) % n_lon, lat, core)
    across = (lon, (lat + 1) % n_lat, core)
    sibling = (lon, lat, 1 - core)

    def x_peer(d):
        return (lon - x + (x + d) % NX, lat, core)

    def y_peer(d):
        other = (y + d) % n_y
        return (lon + (other % n_ylo - ylo) * (NX * NZ), other // n_ylo, core)

    def z_peer(d):
        return (lon + ((z + d) % NZ - z) * NX, lat, core)

    def either(for_first, for_second):
        return for_first + core * (for_second - for_first)

    def wide_peer(d):
        return tuple(either(a, b) for a, b in zip(x_peer(d)[:2], y_peer(d)[:2])) + (core,)

    def slim_peer(d):
        return tuple(either(a, b) for a, b in zip(y_peer(d)[:2], x_peer(d)[:2])) + (core,)

    wide_at = either(x, y)
    slim_at = either(y, x)

    def x_block(i):
        return i * n_lat

    def y_block(i):
        return (i % n_ylo) * (NZ * NX * n_lat) + i // n_ylo

    def wide_block(i):
        return either(x_block(i), y_block(i))

    def slim_block(i):
        return either(y_block(i), x_block(i))

    partners = [right, left, across, sibling]
    partners += [x_peer(d) for d in range(1, NX)]
    partners += [y_peer(d) for d in range(1, n_y)]
    partners += [z_peer(d) for d in range(1, NZ)]

    def remote(src, dst, send_sem, recv_sem, device):
        return pltpu.make_async_remote_copy(
            src_ref=src,
            dst_ref=dst,
            send_sem=send_sem,
            recv_sem=recv_sem,
            device_id=device,
            device_id_type=MESH,
        )

    barrier = pltpu.get_barrier_semaphore()
    for partner in partners:
        pl.semaphore_signal(barrier, inc=1, device_id=partner, device_id_type=MESH)

    inputs = (tok_hbm, gout_hbm)
    wides = (tok_wide, gout_wide)
    rows_of = (tok_rows, gout_rows)
    loads = []
    for a in range(2):
        middle = wides[a].at[:, HALF_COLS : HALF_COLS + WLON]
        loads.append(pltpu.make_async_copy(inputs[a], middle, load_sem.at[a]))
    loads.append(pltpu.make_async_copy(wqkv_hbm, wqkv, load_sem.at[2]))
    loads.append(pltpu.make_async_copy(wout_hbm, wout, load_sem.at[3]))
    for load in loads:
        load.start()

    row_shift = lat_ref[0]
    col_shift = lon_ref[0]
    row_swap = jnp.where(row_shift > HALF_ROWS, 1, 0)
    col_swap = jnp.where(col_shift > HALF_COLS, 1, 0)
    f = row_shift - WLAT * row_swap
    e = col_shift - WLON * col_swap

    k_at = iota((TOK, TOK), 0)
    q_at = iota((TOK, TOK), 1)
    first_row = WLAT * ((lat + row_swap) % n_lat) + row_shift
    k_row = by12(k_at)
    q_row = by12(q_at)
    n_rows = WLAT * n_lat
    counts = jnp.zeros((TOK, TOK), jnp.int32)
    for r in range(WLAT):
        raw = first_row + r
        counts = jnp.where(k_row == r, band_ref[jnp.where(raw >= n_rows, raw - n_rows, raw)], counts)
    n_cols = WLON * n_lon
    k_col = ((k_at - ROW * k_row) >> 1) + (WLON * lon + e)
    k_col = jnp.where(k_col < 0, k_col + n_cols, k_col)
    k_col = jnp.where(k_col >= n_cols, k_col - n_cols, k_col)
    same_side = (k_row + first_row >= n_rows) == (q_row + first_row >= n_rows)
    allowed = ((k_col < counts) | (k_at == q_at)) & same_side
    bias[...] = jnp.where(allowed, 0.0, -1e30)

    pl.semaphore_wait(barrier, len(partners))

    halo = []
    for a in range(2):
        to_left = remote(
            inputs[a].at[:, 0:HALF_COLS],
            wides[a].at[:, HALF_COLS + WLON : 2 * WLON],
            halo_send_sem.at[a, 0],
            halo_recv_sem.at[a, 0],
            left,
        )
        to_right = remote(
            inputs[a].at[:, HALF_COLS:WLON],
            wides[a].at[:, 0:HALF_COLS],
            halo_send_sem.at[a, 1],
            halo_recv_sem.at[a, 1],
            right,
        )
        to_left.start()
        to_right.start()
        halo.append((to_left, to_right))

    sends = [copy for pair in halo for copy in pair]
    over_lat = []
    for a in range(2):
        loads[a].wait()
        for copy in halo[a]:
            copy.wait_recv()
        columns = pl.ds(e + HALF_COLS, WLON)
        lat_send[a] = wides[a][pl.ds(HALF_ROWS * row_swap, HALF_ROWS), columns]
        copy = remote(
            lat_send.at[a],
            rows_of[a].at[WLAT : WLAT + HALF_ROWS],
            lat_send_sem.at[a],
            lat_recv_sem.at[a],
            across,
        )
        copy.start()
        over_lat.append(copy)
        rows_of[a][0:WLAT] = wides[a][:, columns]
    sends += over_lat

    over_core = []
    over_plane = {}
    for a in range(2):
        over_lat[a].wait_recv()
        picked = []
        for r in range(WLAT):
            q = f + r
            place = jnp.where(q < 0, q + (WLAT + HALF_ROWS), q)
            picked.append(rows_of[a][place])
        window = jnp.stack(picked).reshape(TOK, half)
        if a == 0:
            xo[core] = window
            mine = xo.at[core]
        else:
            go[core] = window
            mine = go.at[core]
        copy = remote(mine, mine, core_send_sem.at[a], core_recv_sem.at[a], sibling)
        copy.start()
        over_core.append(copy)
        if a == 0:
            for d in range(1, NX):
                for axis, peer in ((0, x_peer(d)), (1, y_peer(d))):
                    copy = remote(
                        xo.at[core],
                        xg.at[axis, d, core],
                        xg_send_sem.at[axis, d],
                        xg_recv_sem.at[axis, d],
                        peer,
                    )
                    copy.start()
                    over_plane[axis, d] = copy
    sends += over_core + list(over_plane.values())

    loads[2].wait()
    over_core[0].wait_recv()
    for j in range(3):
        total = nn(xo[0], wqkv[j, :half]) + nn(xo[1], wqkv[j, half:])
        qkv[j] = total.astype(BF16)
    loads[3].wait()
    over_core[1].wait_recv()
    ga[...] = (nt(go[0], wout[:, :half]) + nt(go[1], wout[:, half:])).astype(BF16)

    scale = HEAD_DIM ** (-0.5)
    over_qk = {}
    for n in range(NX):
        d = (n + 1) % NX
        pair = (wide_at + d) % NX
        part = pl.ds(pl.multiple_of(pair * cut, cut), cut)
        q_part, k_part, v_part = (qkv[j, :, part] for j in range(3))
        g_part = ga[:, part]
        outs = [[], [], []]
        for head in range(cut // HEAD_DIM):
            at = slice(head * HEAD_DIM, (head + 1) * HEAD_DIM)
            q, k, v, g = q_part[:, at], k_part[:, at], v_part[:, at], g_part[:, at]
            scores = jnp.where(bias[...] == 0.0, nt(k, q) * scale, -1e30)
            raised = jnp.exp(scores - jnp.max(scores, 0, keepdims=True))
            probs = raised * (1.0 / jnp.sum(raised, 0, keepdims=True))
            grad_probs = nt(v, g)
            inner = jnp.sum(probs * grad_probs, 0, keepdims=True)
            grad_scores = (probs * (grad_probs - inner) * scale).astype(BF16)
            outs[0].append(tn(grad_scores, k).astype(BF16))
            outs[1].append(nn(grad_scores, q).astype(BF16))
            outs[2].append(nn(probs.astype(BF16), g).astype(BF16))
        for j in range(3):
            joined = jnp.concatenate(outs[j], 1)
            gall[j, :, part] = joined
            if j < 2:
                own_qk[d, :, j * cut : (j + 1) * cut] = joined
            else:
                own_v[pair] = joined
        if d:
            copy = remote(
                own_qk.at[d], qk_recv.at[d], g_send_sem.at[0, d], g_recv_sem.at[0, d], wide_peer(d)
            )
            copy.start()
            over_qk[d] = copy
    over_v = {}
    for d in range(1, NX):
        copy = remote(
            own_v.at[(slim_at + d) % NX],
            v_recv.at[d],
            g_send_sem.at[1, d],
            g_recv_sem.at[1, d],
            slim_peer(d),
        )
        copy.start()
        over_v[d] = copy
    sends += list(over_qk.values()) + list(over_v.values())

    def grad_in(which):
        rows = pl.ds(pl.multiple_of(which * half, half), half)
        return (
            nt(gall[0], wqkv[0, rows]) + nt(gall[1], wqkv[1, rows]) + nt(gall[2], wqkv[2, rows])
        )

    gin[0] = grad_in(1 - core)
    to_sibling = remote(gin.at[0], gin_recv, core_send_sem.at[2], core_recv_sem.at[2], sibling)
    to_sibling.start()
    relays = {}
    for key, copy in over_plane.items():
        axis, d = key
        copy.wait_recv()
        mine = xg.at[axis, d, core]
        relay = remote(mine, mine, relay_send_sem.at[axis, d], relay_recv_sem.at[axis, d], sibling)
        relay.start()
        relays[key] = relay
    gin[1] = grad_in(core)

    to_sibling.wait_recv()
    window = (gin[1] + gin_recv[...]).astype(BF16).reshape(WLAT, WLON, LEV, half)
    back_own[...] = window
    back_rows[0:WLAT] = window
    for k in range(HALF_ROWS):
        from_row = k + jnp.where(f > 0, WLAT, -HALF_ROWS) - f
        back_send[k] = back_own[jnp.clip(from_row, 0, WLAT - 1)]
    over_lat_back = remote(
        back_send,
        back_rows.at[WLAT : WLAT + HALF_ROWS],
        lat_send_sem.at[2],
        lat_recv_sem.at[2],
        across,
    )
    over_lat_back.start()

    for copy in relays.values():
        copy.wait_recv()
    for d in range(1, NX):
        over_qk[d].wait_recv()
        over_v[d].wait_recv()
    blocks = pw.shape[0]
    own = pw.shape[1]
    for side in range(2):
        rows = slice(side * (blocks // 2), (side + 1) * (blocks // 2))
        total = tn(xo[side], own_qk[0])
        for d in range(1, NX):
            total = total + tn(xg[core, d, side], qk_recv[d])
        pw[rows] = total.reshape(blocks // 2, own, 2 * cut)
        total = tn(xo[side], own_v[slim_at])
        for d in range(1, NX):
            total = total + tn(xg[1 - core, d, side], v_recv[d])
        pn[rows] = total.reshape(blocks // 2, own, cut)

    def wide_rows(i):
        picked = [
            pw[slim_block(i) + k * (NX * n_lat) + wide_block(s)] for k in range(NZ) for s in range(NX)
        ]
        return jnp.concatenate(picked, 0)

    def slim_rows(i):
        picked = [
            pn[wide_block(i) + k * (NX * n_lat) + slim_block(s)] for k in range(NZ) for s in range(NX)
        ]
        return jnp.concatenate(picked, 0)

    over_p = []
    for d in range(1, NX):
        wsend[d] = wide_rows((slim_at + d) % NX).astype(BF16)
        to_wide = remote(
            wsend.at[d], wrecv.at[d], p_send_sem.at[0, d], p_recv_sem.at[0, d], slim_peer(d)
        )
        to_wide.start()
        nsend[d] = slim_rows((wide_at + d) % NX).astype(BF16)
        to_slim = remote(
            nsend.at[d], nrecv.at[d], p_send_sem.at[1, d], p_recv_sem.at[1, d], wide_peer(d)
        )
        to_slim.start()
        over_p.append((to_wide, to_slim))
    sends += [copy for pair in over_p for copy in pair]

    over_lat_back.wait_recv()
    for b in range(WLAT):
        was = b - f
        home = (was >= 0) & (was < WLAT)
        row = back_rows[jnp.where(home, was, b + WLAT - HALF_ROWS * row_swap)]
        side_own[b] = row
        side_cols[b, 0:WLON] = row
    for s in range(HALF_COLS):
        side_send[0, :, s] = side_own[:, jnp.clip(s - HALF_COLS - e, 0, WLON - 1)]
        side_send[1, :, s] = side_own[:, jnp.clip(s + WLON - e, 0, WLON - 1)]
    side_left = remote(
        side_send.at[0],
        side_cols.at[:, WLON + HALF_COLS : 2 * WLON],
        halo_send_sem.at[2, 0],
        halo_recv_sem.at[2, 0],
        left,
    )
    side_right = remote(
        side_send.at[1],
        side_cols.at[:, WLON : WLON + HALF_COLS],
        halo_send_sem.at[2, 1],
        halo_recv_sem.at[2, 1],
        right,
    )
    side_left.start()
    side_right.start()
    sends += [to_sibling, over_lat_back, side_left, side_right] + list(relays.values())

    total_w = wide_rows(slim_at)
    total_n = slim_rows(wide_at)
    for d in range(1, NX):
        over_p[d - 1][0].wait_recv()
        total_w = total_w + wrecv[d].astype(F32)
        over_p[d - 1][1].wait_recv()
        total_n = total_n + nrecv[d].astype(F32)
    rz[:, :, : 2 * cut] = total_w.reshape(NZ, NX * own, 2 * cut)
    rz[:, :, 2 * cut :] = total_n.reshape(NZ, NX * own, cut)
    over_z = []
    for d in range(1, NZ):
        zsend[d] = rz[(z + d) % NZ].astype(BF16)
        copy = remote(
            zsend.at[d], zrecv.at[d], z_send_sem.at[d], z_recv_sem.at[d], z_peer(d)
        )
        copy.start()
        over_z.append(copy)
    sends += over_z

    side_left.wait_recv()
    side_right.wait_recv()
    for q in range(WLON):
        c = q - e
        home = (c >= 0) & (c < WLON)
        gtok_ref[:, q] = side_cols[:, jnp.where(home, c, q + WLON)]

    total = rz[z]
    for d in range(1, NZ):
        over_z[d - 1].wait_recv()
        total = total + zrecv[d].astype(F32)
    rw[...] = total[:, : 2 * cut].reshape(NX, own, 2 * cut)
    rn[...] = total[:, 2 * cut :].reshape(NX, own, cut)
    last = []
    for d in range(1, NX):
        to_wide = remote(
            rw.at[(wide_at + d) % NX],
            fw.at[d],
            f_send_sem.at[0, d],
            f_recv_sem.at[0, d],
            wide_peer(d),
        )
        to_wide.start()
        to_slim = remote(
            rn.at[(slim_at + d) % NX],
            fn.at[d],
            f_send_sem.at[1, d],
            f_recv_sem.at[1, d],
            slim_peer(d),
        )
        to_slim.start()
        last.append((to_wide, to_slim))
    for d in range(NX):
        if d:
            last[d - 1][0].wait_recv()
            last[d - 1][1].wait_recv()
            qk, v = fw[d], fn[d]
        else:
            qk, v = rw[wide_at], rn[slim_at]
        part = pl.ds(pl.multiple_of(((wide_at + NX - d) % NX) * cut, cut), cut)
        gw_ref[0, :, part] = qk[:, :cut]
        gw_ref[1, :, part] = qk[:, cut:]
        part = pl.ds(pl.multiple_of(((slim_at + NX - d) % NX) * cut, cut), cut)
        gw_ref[2, :, part] = v
    sends += [copy for pair in last for copy in pair]

    for copy in sends:
        copy.wait_send()


def solution(mesh):
    n_lon, n_lat = mesh.shape["lon"], mesh.shape["lat"]

    def shards(tokens, grad_out, w_qkv, w_out, band_count, lat_shift, lon_shift):
        half = tokens.shape[-1]
        width = w_qkv.shape[1]
        own = width // (n_lon * n_lat)
        cut = half // NX
        rest = NZ * NX * own
        vmem = pl.BlockSpec(memory_space=pltpu.VMEM)
        smem = pl.BlockSpec(memory_space=pltpu.SMEM)
        hbm = pl.BlockSpec(memory_space=pltpu.HBM)
        dma = pltpu.SemaphoreType.DMA
        gtok, gw = pl.pallas_call(
            functools.partial(kernel, (n_lon, n_lat, width, half)),
            out_shape=(
                jax.ShapeDtypeStruct((WLAT, WLON, LEV, half), BF16),
                jax.ShapeDtypeStruct((3, own, half), F32),
            ),
            in_specs=[smem, smem, smem, hbm, hbm, hbm, hbm],
            out_specs=(vmem, vmem),
            scratch_shapes=[
                pltpu.VMEM((3, width, half), BF16),
                pltpu.VMEM((half, width), BF16),
                pltpu.VMEM((WLAT, 2 * WLON, LEV, half), BF16),
                pltpu.VMEM((WLAT, 2 * WLON, LEV, half), BF16),
                pltpu.VMEM((WLAT + HALF_ROWS, WLON, LEV, half), BF16),
                pltpu.VMEM((WLAT + HALF_ROWS, WLON, LEV, half), BF16),
                pltpu.VMEM((2, HALF_ROWS, WLON, LEV, half), BF16),
                pltpu.VMEM((2, TOK, half), BF16),
                pltpu.VMEM((2, NX, 2, TOK, half), BF16),
                pltpu.VMEM((2, TOK, half), BF16),
                pltpu.VMEM((TOK, TOK), F32),
                pltpu.VMEM((3, TOK, half), BF16),
                pltpu.VMEM((TOK, half), BF16),
                pltpu.VMEM((3, TOK, half), BF16),
                pltpu.VMEM((NX, TOK, 2 * cut), BF16),
                pltpu.VMEM((NX, TOK, cut), BF16),
                pltpu.VMEM((NX, TOK, 2 * cut), BF16),
                pltpu.VMEM((NX, TOK, cut), BF16),
                pltpu.VMEM((2, TOK, half), F32),
                pltpu.VMEM((TOK, half), F32),
                pltpu.VMEM((WLAT, WLON, LEV, half), BF16),
                pltpu.VMEM((WLAT + HALF_ROWS, WLON, LEV, half), BF16),
                pltpu.VMEM((HALF_ROWS, WLON, LEV, half), BF16),
                pltpu.VMEM((WLAT, WLON, LEV, half), BF16),
                pltpu.VMEM((WLAT, 2 * WLON, LEV, half), BF16),
                pltpu.VMEM((2, WLAT, HALF_COLS, LEV, half), BF16),
                pltpu.VMEM((n_lon * n_lat, own, 2 * cut), F32),
                pltpu.VMEM((n_lon * n_lat, own, cut), F32),
                pltpu.VMEM((NX, rest, 2 * cut), BF16),
                pltpu.VMEM((NX, rest, 2 * cut), BF16),
                pltpu.VMEM((NX, rest, cut), BF16),
                pltpu.VMEM((NX, rest, cut), BF16),
                pltpu.VMEM((NZ, NX * own, 3 * cut), F32),
                pltpu.VMEM((NZ, NX * own, 3 * cut), BF16),
                pltpu.VMEM((NZ, NX * own, 3 * cut), BF16),
                pltpu.VMEM((NX, own, 2 * cut), F32),
                pltpu.VMEM((NX, own, cut), F32),
                pltpu.VMEM((NX, own, 2 * cut), F32),
                pltpu.VMEM((NX, own, cut), F32),
                dma((4,)),
                dma((3, 2)),
                dma((3, 2)),
                dma((3,)),
                dma((3,)),
                dma((3,)),
                dma((3,)),
                dma((2, NX)),
                dma((2, NX)),
                dma((2, NX)),
                dma((2, NX)),
                dma((2, NX)),
                dma((2, NX)),
                dma((2, NX)),
                dma((2, NX)),
                dma((NZ,)),
                dma((NZ,)),
                dma((2, NX)),
                dma((2, NX)),
            ],
            compiler_params=pltpu.CompilerParams(
                collective_id=0, has_side_effects=True, vmem_limit_bytes=48 * 2**20
            ),
        )(
            band_count,
            lat_shift,
            lon_shift,
            tokens.transpose(1, 2, 0, 3),
            grad_out.transpose(1, 2, 0, 3),
            w_qkv,
            w_out,
        )
        return gtok.transpose(2, 0, 1, 3), gw

    in_specs = (
        P(None, "lat", "lon", "head"),
        P(None, "lat", "lon", "head"),
        P(None, None, "head"),
        P("head", None),
        P(),
        P(),
        P(),
    )
    out_specs = (P(None, "lat", "lon", "head"), P(None, ("lon", "lat"), "head"))
    return jax.shard_map(shards, mesh=mesh, in_specs=in_specs, out_specs=out_specs, check_vma=False)
```

```python
import functools

import jax
import jax.numpy as jnp
from jax import lax
from jax.experimental import pallas as pl
from jax.experimental.pallas import tpu as pltpu
from jax.sharding import PartitionSpec as P

MESH = pl.DeviceIdType.MESH
HEAD_DIM = 64
LEV = 2
WLAT = 12
WLON = 6
NX = 4
NZ = 8
TOK = LEV * WLAT * WLON
ROW = LEV * WLON
HALF_ROWS = WLAT // 2
HALF_COLS = WLON // 2
F32 = jnp.float32
BF16 = jnp.bfloat16


def nn(a, b):
    return lax.dot_general(a, b, (((1,), (0,)), ((), ())), preferred_element_type=F32)


def nt(a, b):
    return lax.dot_general(a, b, (((1,), (1,)), ((), ())), preferred_element_type=F32)


def tn(a, b):
    return lax.dot_general(a, b, (((0,), (0,)), ((), ())), preferred_element_type=F32)


def iota(shape, axis):
    return lax.broadcasted_iota(jnp.int32, shape, axis)


def by12(t):
    return (t * 342) >> 12


def kernel(
    sizes,
    band_ref,
    lat_ref,
    lon_ref,
    tok_hbm,
    gout_hbm,
    wqkv_hbm,
    wout_hbm,
    gtok_ref,
    gw_ref,
    wqkv,
    wout,
    tok_wide,
    gout_wide,
    tok_rows,
    gout_rows,
    lat_send,
    xo,
    xg,
    go,
    bias,
    qkv,
    ga,
    gall,
    own_qk,
    g_recv,
    gin,
    gin_recv,
    back_own,
    back_rows,
    back_send,
    side_own,
    side_cols,
    side_send,
    parts,
    psend,
    precv,
    rz,
    zsend,
    zrecv,
    rf,
    frecv,
    load_sem,
    halo_send_sem,
    halo_recv_sem,
    lat_send_sem,
    lat_recv_sem,
    core_send_sem,
    core_recv_sem,
    xg_send_sem,
    xg_recv_sem,
    relay_send_sem,
    relay_recv_sem,
    g_send_sem,
    g_recv_sem,
    p_send_sem,
    p_recv_sem,
    z_send_sem,
    z_recv_sem,
    f_send_sem,
    f_recv_sem,
):
    n_lon, n_lat, width, half = sizes
    n_ylo = n_lon // (NX * NZ)
    n_y = n_lat * n_ylo
    assert n_y == NX
    cut = half // NX
    lon = lax.axis_index("lon")
    lat = lax.axis_index("lat")
    core = lax.axis_index("head")
    x = lon % NX
    z = (lon // NX) % NZ
    ylo = lon // (NX * NZ)
    y = lat * n_ylo + ylo

    right = ((lon + 1) % n_lon, lat, core)
    left = ((lon + n_lon - 1) % n_lon, lat, core)
    across = (lon, (lat + 1) % n_lat, core)
    sibling = (lon, lat, 1 - core)

    def x_peer(d):
        return (lon - x + (x + d) % NX, lat, core)

    def y_peer(d):
        other = (y + d) % n_y
        return (lon + (other % n_ylo - ylo) * (NX * NZ), other // n_ylo, core)

    def z_peer(d):
        return (lon + ((z + d) % NZ - z) * NX, lat, core)

    def either(for_first, for_second):
        return for_first + core * (for_second - for_first)

    def wide_peer(d):
        return tuple(either(a, b) for a, b in zip(x_peer(d)[:2], y_peer(d)[:2])) + (core,)

    def slim_peer(d):
        return tuple(either(a, b) for a, b in zip(y_peer(d)[:2], x_peer(d)[:2])) + (core,)

    wide_at = either(x, y)
    slim_at = either(y, x)

    def x_block(i):
        return i * n_lat

    def y_block(i):
        return (i % n_ylo) * (NZ * NX * n_lat) + i // n_ylo

    def wide_block(i):
        return either(x_block(i), y_block(i))

    def slim_block(i):
        return either(y_block(i), x_block(i))

    partners = [right, left, across, sibling]
    partners += [x_peer(d) for d in range(1, NX)]
    partners += [y_peer(d) for d in range(1, n_y)]
    partners += [z_peer(d) for d in range(1, NZ)]

    def remote(src, dst, send_sem, recv_sem, device):
        return pltpu.make_async_remote_copy(
            src_ref=src,
            dst_ref=dst,
            send_sem=send_sem,
            recv_sem=recv_sem,
            device_id=device,
            device_id_type=MESH,
        )

    barrier = pltpu.get_barrier_semaphore()
    for partner in partners:
        pl.semaphore_signal(barrier, inc=1, device_id=partner, device_id_type=MESH)

    inputs = (tok_hbm, gout_hbm)
    wides = (tok_wide, gout_wide)
    rows_of = (tok_rows, gout_rows)
    loads = []
    for a in range(2):
        middle = wides[a].at[:, HALF_COLS : HALF_COLS + WLON]
        loads.append(pltpu.make_async_copy(inputs[a], middle, load_sem.at[a]))
    loads.append(pltpu.make_async_copy(wqkv_hbm, wqkv, load_sem.at[2]))
    loads.append(pltpu.make_async_copy(wout_hbm, wout, load_sem.at[3]))
    for load in loads:
        load.start()

    row_shift = lat_ref[0]
    col_shift = lon_ref[0]
    row_swap = jnp.where(row_shift > HALF_ROWS, 1, 0)
    col_swap = jnp.where(col_shift > HALF_COLS, 1, 0)
    f = row_shift - WLAT * row_swap
    e = col_shift - WLON * col_swap

    k_at = iota((TOK, TOK), 0)
    q_at = iota((TOK, TOK), 1)
    first_row = WLAT * ((lat + row_swap) % n_lat) + row_shift
    k_row = by12(k_at)
    q_row = by12(q_at)
    n_rows = WLAT * n_lat
    counts = jnp.zeros((TOK, TOK), jnp.int32)
    for r in range(WLAT):
        raw = first_row + r
        counts = jnp.where(k_row == r, band_ref[jnp.where(raw >= n_rows, raw - n_rows, raw)], counts)
    n_cols = WLON * n_lon
    k_col = ((k_at - ROW * k_row) >> 1) + (WLON * lon + e)
    k_col = jnp.where(k_col < 0, k_col + n_cols, k_col)
    k_col = jnp.where(k_col >= n_cols, k_col - n_cols, k_col)
    same_side = (k_row + first_row >= n_rows) == (q_row + first_row >= n_rows)
    allowed = ((k_col < counts) | (k_at == q_at)) & same_side
    bias[...] = jnp.where(allowed, 0.0, -1e30)

    pl.semaphore_wait(barrier, len(partners))

    halo = []
    for a in range(2):
        to_left = remote(
            inputs[a].at[:, 0:HALF_COLS],
            wides[a].at[:, HALF_COLS + WLON : 2 * WLON],
            halo_send_sem.at[a, 0],
            halo_recv_sem.at[a, 0],
            left,
        )
        to_right = remote(
            inputs[a].at[:, HALF_COLS:WLON],
            wides[a].at[:, 0:HALF_COLS],
            halo_send_sem.at[a, 1],
            halo_recv_sem.at[a, 1],
            right,
        )
        to_left.start()
        to_right.start()
        halo.append((to_left, to_right))

    sends = [copy for pair in halo for copy in pair]
    over_lat = []
    for a in range(2):
        loads[a].wait()
        for copy in halo[a]:
            copy.wait_recv()
        columns = pl.ds(e + HALF_COLS, WLON)
        lat_send[a] = wides[a][pl.ds(HALF_ROWS * row_swap, HALF_ROWS), columns]
        copy = remote(
            lat_send.at[a],
            rows_of[a].at[WLAT : WLAT + HALF_ROWS],
            lat_send_sem.at[a],
            lat_recv_sem.at[a],
            across,
        )
        copy.start()
        over_lat.append(copy)
        rows_of[a][0:WLAT] = wides[a][:, columns]
    sends += over_lat

    over_core = []
    over_plane = {}
    for a in range(2):
        over_lat[a].wait_recv()
        picked = []
        for r in range(WLAT):
            q = f + r
            place = jnp.where(q < 0, q + (WLAT + HALF_ROWS), q)
            picked.append(rows_of[a][place])
        window = jnp.stack(picked).reshape(TOK, half)
        if a == 0:
            xo[core] = window
            mine = xo.at[core]
        else:
            go[core] = window
            mine = go.at[core]
        copy = remote(mine, mine, core_send_sem.at[a], core_recv_sem.at[a], sibling)
        copy.start()
        over_core.append(copy)
        if a == 0:
            for d in range(1, NX):
                for axis, peer in ((0, x_peer(d)), (1, y_peer(d))):
                    copy = remote(
                        xo.at[core],
                        xg.at[axis, d, core],
                        xg_send_sem.at[axis, d],
                        xg_recv_sem.at[axis, d],
                        peer,
                    )
                    copy.start()
                    over_plane[axis, d] = copy
    sends += over_core + list(over_plane.values())

    loads[2].wait()
    over_core[0].wait_recv()
    for j in range(3):
        total = nn(xo[0], wqkv[j, :half]) + nn(xo[1], wqkv[j, half:])
        qkv[j] = total.astype(BF16)
    loads[3].wait()
    over_core[1].wait_recv()
    ga[...] = (nt(go[0], wout[:, :half]) + nt(go[1], wout[:, half:])).astype(BF16)

    def factor_peer(t, d):
        return wide_peer(d) if t < 2 else slim_peer(d)

    def sum_peer(t, d):
        return slim_peer(d) if t < 2 else wide_peer(d)

    scale = HEAD_DIM ** (-0.5)
    over_g = {}
    for t in range(2):
        at = slice(t * HEAD_DIM, (t + 1) * HEAD_DIM)
        for n in range(NX):
            d = (n + 1) % NX
            pair = (wide_at + d) % NX
            lanes = pl.ds(pl.multiple_of(pair * cut, cut), cut)
            q, k, v = (qkv[j, :, lanes][:, at] for j in range(3))
            g = ga[:, lanes][:, at]
            scores = jnp.where(bias[...] == 0.0, nt(k, q) * scale, -1e30)
            raised = jnp.exp(scores - jnp.max(scores, 0, keepdims=True))
            probs = raised * (1.0 / jnp.sum(raised, 0, keepdims=True))
            grad_probs = nt(v, g)
            inner = jnp.sum(probs * grad_probs, 0, keepdims=True)
            grad_scores = (probs * (grad_probs - inner) * scale).astype(BF16)
            grad_q = tn(grad_scores, k).astype(BF16)
            grad_k = nn(grad_scores, q).astype(BF16)
            gall[0, pair, :, at] = grad_q
            gall[1, pair, :, at] = grad_k
            gall[2, pair, :, at] = nn(probs.astype(BF16), g).astype(BF16)
            own_qk[t, d] = jnp.concatenate([grad_q, grad_k], 1)
            if d:
                copy = remote(
                    own_qk.at[t, d],
                    g_recv.at[t, d],
                    g_send_sem.at[t, d],
                    g_recv_sem.at[t, d],
                    factor_peer(t, d),
                )
                copy.start()
                over_g[t, d] = copy
    for d in range(1, NX):
        copy = remote(
            gall.at[2, (slim_at + d) % NX],
            g_recv.at[2, d],
            g_send_sem.at[2, d],
            g_recv_sem.at[2, d],
            factor_peer(2, d),
        )
        copy.start()
        over_g[2, d] = copy
    sends += list(over_g.values())

    def grad_in(which):
        rows = pl.ds(pl.multiple_of(which * half, half), half)
        total = 0.0
        for j in range(3):
            joined = jnp.concatenate([gall[j, pair] for pair in range(NX)], 1)
            total = total + nt(joined, wqkv[j, rows])
        return total

    gin[0] = grad_in(1 - core)
    to_sibling = remote(gin.at[0], gin_recv, core_send_sem.at[2], core_recv_sem.at[2], sibling)
    to_sibling.start()
    relays = {}
    for key, copy in over_plane.items():
        axis, d = key
        copy.wait_recv()
        mine = xg.at[axis, d, core]
        relay = remote(mine, mine, relay_send_sem.at[axis, d], relay_recv_sem.at[axis, d], sibling)
        relay.start()
        relays[key] = relay
    gin[1] = grad_in(core)

    to_sibling.wait_recv()
    window = (gin[1] + gin_recv[...]).astype(BF16).reshape(WLAT, WLON, LEV, half)
    back_own[...] = window
    back_rows[0:WLAT] = window
    for k in range(HALF_ROWS):
        from_row = k + jnp.where(f > 0, WLAT, -HALF_ROWS) - f
        back_send[k] = back_own[jnp.clip(from_row, 0, WLAT - 1)]
    over_lat_back = remote(
        back_send,
        back_rows.at[WLAT : WLAT + HALF_ROWS],
        lat_send_sem.at[2],
        lat_recv_sem.at[2],
        across,
    )
    over_lat_back.start()

    blocks = parts.shape[1]
    own = parts.shape[2]

    def make_product(t):
        axis = core if t < 2 else 1 - core
        halves = []
        for side in range(2):
            halves.append(tn(xo[side], own_qk[t, 0] if t < 2 else gall[2, slim_at]))
        for d in range(1, NX):
            if t == 0:
                relays[0, d].wait_recv()
                relays[1, d].wait_recv()
            over_g[t, d].wait_recv()
            for side in range(2):
                halves[side] = halves[side] + tn(xg[axis, d, side], g_recv[t, d])
        for side in range(2):
            rows = slice(side * (blocks // 2), (side + 1) * (blocks // 2))
            parts[t, rows] = halves[side].reshape(blocks // 2, own, cut)

    def owner_rows(t, i):
        base = slim_block(i) if t < 2 else wide_block(i)
        picked = []
        for k in range(NZ):
            for j in range(NX):
                along = wide_block(j) if t < 2 else slim_block(j)
                picked.append(parts[t, base + along + k * (NX * n_lat)])
        return jnp.concatenate(picked, 0)

    over_p = {}
    for t in range(3):
        make_product(t)
        place = slim_at if t < 2 else wide_at
        for d in range(1, NX):
            psend[t, d] = owner_rows(t, (place + d) % NX).astype(BF16)
            copy = remote(
                psend.at[t, d],
                precv.at[t, d],
                p_send_sem.at[t, d],
                p_recv_sem.at[t, d],
                sum_peer(t, d),
            )
            copy.start()
            over_p[t, d] = copy
    sends += list(over_p.values())

    over_lat_back.wait_recv()
    for b in range(WLAT):
        was = b - f
        home = (was >= 0) & (was < WLAT)
        row = back_rows[jnp.where(home, was, b + WLAT - HALF_ROWS * row_swap)]
        side_own[b] = row
        side_cols[b, 0:WLON] = row
    for s in range(HALF_COLS):
        side_send[0, :, s] = side_own[:, jnp.clip(s - HALF_COLS - e, 0, WLON - 1)]
        side_send[1, :, s] = side_own[:, jnp.clip(s + WLON - e, 0, WLON - 1)]
    side_left = remote(
        side_send.at[0],
        side_cols.at[:, WLON + HALF_COLS : 2 * WLON],
        halo_send_sem.at[2, 0],
        halo_recv_sem.at[2, 0],
        left,
    )
    side_right = remote(
        side_send.at[1],
        side_cols.at[:, WLON : WLON + HALF_COLS],
        halo_send_sem.at[2, 1],
        halo_recv_sem.at[2, 1],
        right,
    )
    side_left.start()
    side_right.start()
    sends += [to_sibling, over_lat_back, side_left, side_right] + list(relays.values())

    over_z = {}
    for t in range(3):
        total = owner_rows(t, slim_at if t < 2 else wide_at)
        for d in range(1, NX):
            over_p[t, d].wait_recv()
            total = total + precv[t, d].astype(F32)
        rz[t] = total.reshape(NZ, NX * own, cut)
        for d in range(1, NZ):
            zsend[t, d] = rz[t, (z + d) % NZ].astype(BF16)
            copy = remote(
                zsend.at[t, d],
                zrecv.at[t, d],
                z_send_sem.at[t, d],
                z_recv_sem.at[t, d],
                z_peer(d),
            )
            copy.start()
            over_z[t, d] = copy
    sends += list(over_z.values())

    side_left.wait_recv()
    side_right.wait_recv()
    for q in range(WLON):
        c = q - e
        home = (c >= 0) & (c < WLON)
        gtok_ref[:, q] = side_cols[:, jnp.where(home, c, q + WLON)]

    last = {}
    for t in range(3):
        total = rz[t, z]
        for d in range(1, NZ):
            over_z[t, d].wait_recv()
            total = total + zrecv[t, d].astype(F32)
        rf[:, t] = total.reshape(NX, own, cut)
        if t == 0:
            continue
        group = slice(0, 2) if t == 1 else slice(2, 3)
        place = wide_at if t == 1 else slim_at
        for d in range(1, NX):
            copy = remote(
                rf.at[(place + d) % NX, group],
                frecv.at[d, group],
                f_send_sem.at[t, d],
                f_recv_sem.at[t, d],
                factor_peer(t, d),
            )
            copy.start()
            last[t, d] = copy
    sends += list(last.values())
    for d in range(NX):
        if d:
            last[1, d].wait_recv()
            last[2, d].wait_recv()
            first, second, values = (frecv[d, t] for t in range(3))
        else:
            first, second, values = rf[wide_at, 0], rf[wide_at, 1], rf[slim_at, 2]
        lanes = pl.ds(pl.multiple_of(((wide_at + NX - d) % NX) * cut, cut), cut)
        for j in range(2):
            at = slice(j * HEAD_DIM, (j + 1) * HEAD_DIM)
            gw_ref[j, :, lanes] = jnp.concatenate([first[:, at], second[:, at]], 1)
        lanes = pl.ds(pl.multiple_of(((slim_at + NX - d) % NX) * cut, cut), cut)
        gw_ref[2, :, lanes] = values

    for copy in sends:
        copy.wait_send()


def solution(mesh):
    n_lon, n_lat = mesh.shape["lon"], mesh.shape["lat"]

    def shards(tokens, grad_out, w_qkv, w_out, band_count, lat_shift, lon_shift):
        half = tokens.shape[-1]
        width = w_qkv.shape[1]
        own = width // (n_lon * n_lat)
        cut = half // NX
        rest = NZ * NX * own
        vmem = pl.BlockSpec(memory_space=pltpu.VMEM)
        smem = pl.BlockSpec(memory_space=pltpu.SMEM)
        hbm = pl.BlockSpec(memory_space=pltpu.HBM)
        dma = pltpu.SemaphoreType.DMA
        gtok, gw = pl.pallas_call(
            functools.partial(kernel, (n_lon, n_lat, width, half)),
            out_shape=(
                jax.ShapeDtypeStruct((WLAT, WLON, LEV, half), BF16),
                jax.ShapeDtypeStruct((3, own, half), F32),
            ),
            in_specs=[smem, smem, smem, hbm, hbm, hbm, hbm],
            out_specs=(vmem, vmem),
            scratch_shapes=[
                pltpu.VMEM((3, width, half), BF16),
                pltpu.VMEM((half, width), BF16),
                pltpu.VMEM((WLAT, 2 * WLON, LEV, half), BF16),
                pltpu.VMEM((WLAT, 2 * WLON, LEV, half), BF16),
                pltpu.VMEM((WLAT + HALF_ROWS, WLON, LEV, half), BF16),
                pltpu.VMEM((WLAT + HALF_ROWS, WLON, LEV, half), BF16),
                pltpu.VMEM((2, HALF_ROWS, WLON, LEV, half), BF16),
                pltpu.VMEM((2, TOK, half), BF16),
                pltpu.VMEM((2, NX, 2, TOK, half), BF16),
                pltpu.VMEM((2, TOK, half), BF16),
                pltpu.VMEM((TOK, TOK), F32),
                pltpu.VMEM((3, TOK, half), BF16),
                pltpu.VMEM((TOK, half), BF16),
                pltpu.VMEM((3, NX, TOK, cut), BF16),
                pltpu.VMEM((2, NX, TOK, cut), BF16),
                pltpu.VMEM((3, NX, TOK, cut), BF16),
                pltpu.VMEM((2, TOK, half), F32),
                pltpu.VMEM((TOK, half), F32),
                pltpu.VMEM((WLAT, WLON, LEV, half), BF16),
                pltpu.VMEM((WLAT + HALF_ROWS, WLON, LEV, half), BF16),
                pltpu.VMEM((HALF_ROWS, WLON, LEV, half), BF16),
                pltpu.VMEM((WLAT, WLON, LEV, half), BF16),
                pltpu.VMEM((WLAT, 2 * WLON, LEV, half), BF16),
                pltpu.VMEM((2, WLAT, HALF_COLS, LEV, half), BF16),
                pltpu.VMEM((3, n_lon * n_lat, own, cut), F32),
                pltpu.VMEM((3, NX, rest, cut), BF16),
                pltpu.VMEM((3, NX, rest, cut), BF16),
                pltpu.VMEM((3, NZ, NX * own, cut), F32),
                pltpu.VMEM((3, NZ, NX * own, cut), BF16),
                pltpu.VMEM((3, NZ, NX * own, cut), BF16),
                pltpu.VMEM((NX, 3, own, cut), F32),
                pltpu.VMEM((NX, 3, own, cut), F32),
                dma((4,)),
                dma((3, 2)),
                dma((3, 2)),
                dma((3,)),
                dma((3,)),
                dma((3,)),
                dma((3,)),
                dma((2, NX)),
                dma((2, NX)),
                dma((2, NX)),
                dma((2, NX)),
                dma((3, NX)),
                dma((3, NX)),
                dma((3, NX)),
                dma((3, NX)),
                dma((3, NZ)),
                dma((3, NZ)),
                dma((3, NX)),
                dma((3, NX)),
            ],
            compiler_params=pltpu.CompilerParams(
                collective_id=0, has_side_effects=True, vmem_limit_bytes=60 * 2**20
            ),
        )(
            band_count,
            lat_shift,
            lon_shift,
            tokens.transpose(1, 2, 0, 3),
            grad_out.transpose(1, 2, 0, 3),
            w_qkv,
            w_out,
        )
        return gtok.transpose(2, 0, 1, 3), gw

    in_specs = (
        P(None, "lat", "lon", "head"),
        P(None, "lat", "lon", "head"),
        P(None, None, "head"),
        P("head", None),
        P(),
        P(),
        P(),
    )
    out_specs = (P(None, "lat", "lon", "head"), P(None, ("lon", "lat"), "head"))
    return jax.shard_map(shards, mesh=mesh, in_specs=in_specs, out_specs=out_specs, check_vma=False)
```

```python
import functools

import jax
import jax.numpy as jnp
from jax import lax
from jax.experimental import pallas as pl
from jax.experimental.pallas import tpu as pltpu
from jax.sharding import PartitionSpec as P

MESH = pl.DeviceIdType.MESH
HEAD_DIM = 64
LEV = 2
WLAT = 12
WLON = 6
NX = 4
NZ = 8
TOK = LEV * WLAT * WLON
ROW = LEV * WLON
HALF_ROWS = WLAT // 2
HALF_COLS = WLON // 2
F32 = jnp.float32
BF16 = jnp.bfloat16


def nn(a, b):
    return lax.dot_general(a, b, (((1,), (0,)), ((), ())), preferred_element_type=F32)


def nt(a, b):
    return lax.dot_general(a, b, (((1,), (1,)), ((), ())), preferred_element_type=F32)


def tn(a, b):
    return lax.dot_general(a, b, (((0,), (0,)), ((), ())), preferred_element_type=F32)


def iota(shape, axis):
    return lax.broadcasted_iota(jnp.int32, shape, axis)


def by12(t):
    return (t * 342) >> 12


def kernel(
    sizes,
    lat_ref,
    lon_ref,
    band_hbm,
    tok_hbm,
    gout_hbm,
    wqkv_hbm,
    wout_hbm,
    gtok_ref,
    gw_ref,
    wqkv,
    wout,
    band_ref,
    own_block,
    tok_wide,
    gout_wide,
    lat_send,
    xo,
    xg,
    go,
    bias,
    qkv,
    ga,
    gall,
    own_qk,
    g_recv,
    gin,
    gin_recv,
    back_own,
    back_rows,
    back_send,
    side_own,
    side_cols,
    side_send,
    parts,
    psend,
    precv,
    rz,
    zsend,
    zrecv,
    rf,
    frecv,
    load_sem,
    halo_send_sem,
    halo_recv_sem,
    core_send_sem,
    core_recv_sem,
    xg_send_sem,
    xg_recv_sem,
    relay_send_sem,
    relay_recv_sem,
    g_send_sem,
    g_recv_sem,
    p_send_sem,
    p_recv_sem,
    z_send_sem,
    z_recv_sem,
    f_send_sem,
    f_recv_sem,
):
    n_lon, n_lat, width, half = sizes
    n_ylo = n_lon // (NX * NZ)
    n_y = n_lat * n_ylo
    assert n_y == NX
    cut = half // NX
    lon = lax.axis_index("lon")
    lat = lax.axis_index("lat")
    core = lax.axis_index("head")
    x = lon % NX
    z = (lon // NX) % NZ
    ylo = lon // (NX * NZ)
    y = lat * n_ylo + ylo

    right = ((lon + 1) % n_lon, lat, core)
    left = ((lon + n_lon - 1) % n_lon, lat, core)
    across = (lon, (lat + 1) % n_lat, core)
    across_right = ((lon + 1) % n_lon, (lat + 1) % n_lat, core)
    across_left = ((lon + n_lon - 1) % n_lon, (lat + 1) % n_lat, core)
    sibling = (lon, lat, 1 - core)

    def x_peer(d):
        return (lon - x + (x + d) % NX, lat, core)

    def y_peer(d):
        other = (y + d) % n_y
        return (lon + (other % n_ylo - ylo) * (NX * NZ), other // n_ylo, core)

    def z_peer(d):
        return (lon + ((z + d) % NZ - z) * NX, lat, core)

    def either(for_first, for_second):
        return for_first + core * (for_second - for_first)

    def wide_peer(d):
        return tuple(either(a, b) for a, b in zip(x_peer(d)[:2], y_peer(d)[:2])) + (core,)

    def slim_peer(d):
        return tuple(either(a, b) for a, b in zip(y_peer(d)[:2], x_peer(d)[:2])) + (core,)

    wide_at = either(x, y)
    slim_at = either(y, x)

    def x_block(i):
        return i * n_lat

    def y_block(i):
        return (i % n_ylo) * (NZ * NX * n_lat) + i // n_ylo

    def wide_block(i):
        return either(x_block(i), y_block(i))

    def slim_block(i):
        return either(y_block(i), x_block(i))

    partners = [right, left, across, across_right, across_left, sibling]
    partners += [x_peer(d) for d in range(1, NX)]
    partners += [y_peer(d) for d in range(1, n_y)]
    partners += [z_peer(d) for d in range(1, NZ)]

    def remote(src, dst, send_sem, recv_sem, device):
        return pltpu.make_async_remote_copy(
            src_ref=src,
            dst_ref=dst,
            send_sem=send_sem,
            recv_sem=recv_sem,
            device_id=device,
            device_id_type=MESH,
        )

    barrier = pltpu.get_barrier_semaphore()
    for partner in partners:
        pl.semaphore_signal(barrier, inc=1, device_id=partner, device_id_type=MESH)

    load_band = pltpu.make_async_copy(band_hbm, band_ref, load_sem.at[0])
    load_band.start()
    inputs = (tok_hbm, gout_hbm)
    wides = (tok_wide, gout_wide)
    middle = slice(HALF_COLS, HALF_COLS + WLON)
    loads = []
    for a in range(2):
        loads.append(pltpu.make_async_copy(inputs[a], own_block.at[a], load_sem.at[1 + a]))
        loads.append(
            pltpu.make_async_copy(inputs[a], wides[a].at[0:WLAT, middle], load_sem.at[3 + a])
        )
    loads.append(pltpu.make_async_copy(wqkv_hbm, wqkv, load_sem.at[5]))
    loads.append(pltpu.make_async_copy(wout_hbm, wout, load_sem.at[6]))
    for load in loads:
        load.start()

    row_shift = lat_ref[0]
    col_shift = lon_ref[0]
    row_swap = jnp.where(row_shift > HALF_ROWS, 1, 0)
    col_swap = jnp.where(col_shift > HALF_COLS, 1, 0)
    f = row_shift - WLAT * row_swap
    e = col_shift - WLON * col_swap

    loads[0].wait()
    loads[2].wait()
    for a in range(2):
        lat_send[a] = own_block[a, pl.ds(HALF_ROWS * row_swap, HALF_ROWS)]

    load_band.wait()
    k_at = iota((TOK, TOK), 0)
    q_at = iota((TOK, TOK), 1)
    first_row = WLAT * ((lat + row_swap) % n_lat) + row_shift
    k_row = by12(k_at)
    q_row = by12(q_at)
    n_rows = WLAT * n_lat
    counts = jnp.zeros((TOK, TOK), jnp.int32)
    for r in range(WLAT):
        raw = first_row + r
        counts = jnp.where(k_row == r, band_ref[jnp.where(raw >= n_rows, raw - n_rows, raw)], counts)
    n_cols = WLON * n_lon
    k_col = ((k_at - ROW * k_row) >> 1) + (WLON * lon + e)
    k_col = jnp.where(k_col < 0, k_col + n_cols, k_col)
    k_col = jnp.where(k_col >= n_cols, k_col - n_cols, k_col)
    same_side = (k_row + first_row >= n_rows) == (q_row + first_row >= n_rows)
    allowed = ((k_col < counts) | (k_at == q_at)) & same_side
    bias[...] = jnp.where(allowed, 0.0, -1e30)

    pl.semaphore_wait(barrier, len(partners))

    halo = []
    before = slice(0, HALF_COLS)
    after = slice(HALF_COLS + WLON, 2 * WLON)
    left_half = slice(0, HALF_COLS)
    right_half = slice(HALF_COLS, WLON)
    kept = slice(0, WLAT)
    borrowed = slice(WLAT, WLAT + HALF_ROWS)
    for a in range(2):
        copies = []
        for n, (src, rows, columns, device) in enumerate(
            (
                (lat_send.at[a], borrowed, middle, across),
                (inputs[a].at[:, left_half], kept, after, left),
                (inputs[a].at[:, right_half], kept, before, right),
                (lat_send.at[a, :, left_half], borrowed, after, across_left),
                (lat_send.at[a, :, right_half], borrowed, before, across_right),
            )
        ):
            copy = remote(
                src, wides[a].at[rows, columns], halo_send_sem.at[a, n], halo_recv_sem.at[a, n], device
            )
            copy.start()
            copies.append(copy)
        halo.append(copies)
    sends = [copy for copies in halo for copy in copies]

    over_core = []
    over_plane = {}
    for a in range(2):
        loads[2 * a + 1].wait()
        for copy in halo[a]:
            copy.wait_recv()
        columns = pl.ds(e + HALF_COLS, WLON)
        picked = []
        for r in range(WLAT):
            q = f + r
            picked.append(wides[a][jnp.where(q < 0, q + (WLAT + HALF_ROWS), q), columns])
        window = jnp.stack(picked).reshape(TOK, half)
        if a == 0:
            xo[core] = window
            mine = xo.at[core]
        else:
            go[core] = window
            mine = go.at[core]
        copy = remote(mine, mine, core_send_sem.at[a], core_recv_sem.at[a], sibling)
        copy.start()
        over_core.append(copy)
        if a == 0:
            for d in range(1, NX):
                for axis, peer in ((0, x_peer(d)), (1, y_peer(d))):
                    copy = remote(
                        xo.at[core],
                        xg.at[axis, d, core],
                        xg_send_sem.at[axis, d],
                        xg_recv_sem.at[axis, d],
                        peer,
                    )
                    copy.start()
                    over_plane[axis, d] = copy
    sends += over_core + list(over_plane.values())

    loads[4].wait()
    over_core[0].wait_recv()
    for j in range(3):
        total = nn(xo[0], wqkv[j, :half]) + nn(xo[1], wqkv[j, half:])
        qkv[j] = total.astype(BF16)
    loads[5].wait()
    over_core[1].wait_recv()
    ga[...] = (nt(go[0], wout[:, :half]) + nt(go[1], wout[:, half:])).astype(BF16)

    def factor_peer(t, d):
        return wide_peer(d) if t < 2 else slim_peer(d)

    def sum_peer(t, d):
        return slim_peer(d) if t < 2 else wide_peer(d)

    relays = {}

    def relay(d):
        for axis in range(2):
            over_plane[axis, d].wait_recv()
            mine = xg.at[axis, d, core]
            copy = remote(
                mine, mine, relay_send_sem.at[axis, d], relay_recv_sem.at[axis, d], sibling
            )
            copy.start()
            relays[axis, d] = copy

    scale = HEAD_DIM ** (-0.5)
    over_g = {}
    for t in range(2):
        at = slice(t * HEAD_DIM, (t + 1) * HEAD_DIM)
        for n in range(NX):
            d = (n + 1) % NX
            pair = (wide_at + d) % NX
            lanes = pl.ds(pl.multiple_of(pair * cut, cut), cut)
            q, k, v = (qkv[j, :, lanes][:, at] for j in range(3))
            g = ga[:, lanes][:, at]
            scores = jnp.where(bias[...] == 0.0, nt(k, q) * scale, -1e30)
            raised = jnp.exp(scores - jnp.max(scores, 0, keepdims=True))
            probs = raised * (1.0 / jnp.sum(raised, 0, keepdims=True))
            grad_probs = nt(v, g)
            inner = jnp.sum(probs * grad_probs, 0, keepdims=True)
            grad_scores = (probs * (grad_probs - inner) * scale).astype(BF16)
            grad_q = tn(grad_scores, k).astype(BF16)
            grad_k = nn(grad_scores, q).astype(BF16)
            gall[0, pair, :, at] = grad_q
            gall[1, pair, :, at] = grad_k
            gall[2, pair, :, at] = nn(probs.astype(BF16), g).astype(BF16)
            own_qk[t, d] = jnp.concatenate([grad_q, grad_k], 1)
            if d:
                copy = remote(
                    own_qk.at[t, d],
                    g_recv.at[t, d],
                    g_send_sem.at[t, d],
                    g_recv_sem.at[t, d],
                    factor_peer(t, d),
                )
                copy.start()
                over_g[t, d] = copy
        if t == 0:
            for d in range(1, NX):
                if d != NX // 2:
                    relay(d)
    for d in range(1, NX):
        copy = remote(
            gall.at[2, (slim_at + d) % NX],
            g_recv.at[2, d],
            g_send_sem.at[2, d],
            g_recv_sem.at[2, d],
            factor_peer(2, d),
        )
        copy.start()
        over_g[2, d] = copy
    relay(NX // 2)
    sends += list(over_g.values()) + list(relays.values())

    blocks = parts.shape[1]
    own = parts.shape[2]

    def make_product(t):
        axis = core if t < 2 else 1 - core
        halves = []
        for side in range(2):
            halves.append(tn(xo[side], own_qk[t, 0] if t < 2 else gall[2, slim_at]))
        for d in range(1, NX):
            if t == 0:
                relays[0, d].wait_recv()
                relays[1, d].wait_recv()
            over_g[t, d].wait_recv()
            for side in range(2):
                halves[side] = halves[side] + tn(xg[axis, d, side], g_recv[t, d])
        for side in range(2):
            rows = slice(side * (blocks // 2), (side + 1) * (blocks // 2))
            parts[t, rows] = halves[side].reshape(blocks // 2, own, cut)

    def owner_rows(t, i):
        base = slim_block(i) if t < 2 else wide_block(i)
        picked = []
        for k in range(NZ):
            for j in range(NX):
                along = wide_block(j) if t < 2 else slim_block(j)
                picked.append(parts[t, base + along + k * (NX * n_lat)])
        return jnp.concatenate(picked, 0)

    over_p = {}
    for t in range(3):
        make_product(t)
        place = slim_at if t < 2 else wide_at
        for d in range(1, NX):
            psend[t, d] = owner_rows(t, (place + d) % NX).astype(BF16)
            copy = remote(
                psend.at[t, d],
                precv.at[t, d],
                p_send_sem.at[t, d],
                p_recv_sem.at[t, d],
                sum_peer(t, d),
            )
            copy.start()
            over_p[t, d] = copy
    sends += list(over_p.values())

    def grad_in(which):
        rows = pl.ds(pl.multiple_of(which * half, half), half)
        total = 0.0
        for j in range(3):
            joined = jnp.concatenate([gall[j, pair] for pair in range(NX)], 1)
            total = total + nt(joined, wqkv[j, rows])
        return total

    gin[0] = grad_in(1 - core)
    to_sibling = remote(gin.at[0], gin_recv, core_send_sem.at[2], core_recv_sem.at[2], sibling)
    to_sibling.start()
    gin[1] = grad_in(core)

    to_sibling.wait_recv()
    window = (gin[1] + gin_recv[...]).astype(BF16).reshape(WLAT, WLON, LEV, half)
    back_own[...] = window
    back_rows[0:WLAT] = window
    for k in range(HALF_ROWS):
        from_row = k + jnp.where(f > 0, WLAT, -HALF_ROWS) - f
        back_send[k] = back_own[jnp.clip(from_row, 0, WLAT - 1)]
    over_lat_back = remote(
        back_send,
        back_rows.at[WLAT : WLAT + HALF_ROWS],
        halo_send_sem.at[2, 0],
        halo_recv_sem.at[2, 0],
        across,
    )
    over_lat_back.start()

    over_z = {}
    for t in range(3):
        total = owner_rows(t, slim_at if t < 2 else wide_at)
        for d in range(1, NX):
            over_p[t, d].wait_recv()
            total = total + precv[t, d].astype(F32)
        rz[t] = total.reshape(NZ, NX * own, cut)
        for d in range(1, NZ):
            zsend[t, d] = rz[t, (z + d) % NZ].astype(BF16)
            copy = remote(
                zsend.at[t, d],
                zrecv.at[t, d],
                z_send_sem.at[t, d],
                z_recv_sem.at[t, d],
                z_peer(d),
            )
            copy.start()
            over_z[t, d] = copy
    sends += list(over_z.values())

    over_lat_back.wait_recv()
    for b in range(WLAT):
        was = b - f
        home = (was >= 0) & (was < WLAT)
        row = back_rows[jnp.where(home, was, b + WLAT - HALF_ROWS * row_swap)]
        side_own[b] = row
        side_cols[b, 0:WLON] = row
    for s in range(HALF_COLS):
        side_send[0, :, s] = side_own[:, jnp.clip(s - HALF_COLS - e, 0, WLON - 1)]
        side_send[1, :, s] = side_own[:, jnp.clip(s + WLON - e, 0, WLON - 1)]
    side_left = remote(
        side_send.at[0],
        side_cols.at[:, WLON + HALF_COLS : 2 * WLON],
        halo_send_sem.at[2, 1],
        halo_recv_sem.at[2, 1],
        left,
    )
    side_right = remote(
        side_send.at[1],
        side_cols.at[:, WLON : WLON + HALF_COLS],
        halo_send_sem.at[2, 2],
        halo_recv_sem.at[2, 2],
        right,
    )
    side_left.start()
    side_right.start()
    sends += [to_sibling, over_lat_back, side_left, side_right]

    side_left.wait_recv()
    side_right.wait_recv()
    for q in range(WLON):
        c = q - e
        home = (c >= 0) & (c < WLON)
        gtok_ref[:, q] = side_cols[:, jnp.where(home, c, q + WLON)]

    last = {}
    for t in range(3):
        total = rz[t, z]
        for d in range(1, NZ):
            over_z[t, d].wait_recv()
            total = total + zrecv[t, d].astype(F32)
        rf[:, t] = total.reshape(NX, own, cut)
        if t == 0:
            continue
        group = slice(0, 2) if t == 1 else slice(2, 3)
        place = wide_at if t == 1 else slim_at
        for d in range(1, NX):
            copy = remote(
                rf.at[(place + d) % NX, group],
                frecv.at[d, group],
                f_send_sem.at[t, d],
                f_recv_sem.at[t, d],
                factor_peer(t, d),
            )
            copy.start()
            last[t, d] = copy
    sends += list(last.values())
    for d in range(NX):
        if d:
            last[1, d].wait_recv()
            last[2, d].wait_recv()
            first, second, values = (frecv[d, t] for t in range(3))
        else:
            first, second, values = rf[wide_at, 0], rf[wide_at, 1], rf[slim_at, 2]
        lanes = pl.ds(pl.multiple_of(((wide_at + NX - d) % NX) * cut, cut), cut)
        for j in range(2):
            at = slice(j * HEAD_DIM, (j + 1) * HEAD_DIM)
            gw_ref[j, :, lanes] = jnp.concatenate([first[:, at], second[:, at]], 1)
        lanes = pl.ds(pl.multiple_of(((slim_at + NX - d) % NX) * cut, cut), cut)
        gw_ref[2, :, lanes] = values

    for copy in sends:
        copy.wait_send()


def solution(mesh):
    n_lon, n_lat = mesh.shape["lon"], mesh.shape["lat"]

    def shards(tokens, grad_out, w_qkv, w_out, band_count, lat_shift, lon_shift):
        half = tokens.shape[-1]
        width = w_qkv.shape[1]
        own = width // (n_lon * n_lat)
        cut = half // NX
        rest = NZ * NX * own
        vmem = pl.BlockSpec(memory_space=pltpu.VMEM)
        smem = pl.BlockSpec(memory_space=pltpu.SMEM)
        hbm = pl.BlockSpec(memory_space=pltpu.HBM)
        dma = pltpu.SemaphoreType.DMA
        gtok, gw = pl.pallas_call(
            functools.partial(kernel, (n_lon, n_lat, width, half)),
            out_shape=(
                pltpu.VMEM((WLAT, WLON, LEV, half), BF16),
                pltpu.VMEM((3, own, half), F32),
            ),
            in_specs=[smem] * 2 + [hbm] * 5,
            out_specs=(vmem, vmem),
            scratch_shapes=[
                pltpu.VMEM((3, width, half), BF16),
                pltpu.VMEM((half, width), BF16),
                pltpu.SMEM(band_count.shape, jnp.int32),
                pltpu.VMEM((2, WLAT, WLON, LEV, half), BF16),
                pltpu.VMEM((WLAT + HALF_ROWS, 2 * WLON, LEV, half), BF16),
                pltpu.VMEM((WLAT + HALF_ROWS, 2 * WLON, LEV, half), BF16),
                pltpu.VMEM((2, HALF_ROWS, WLON, LEV, half), BF16),
                pltpu.VMEM((2, TOK, half), BF16),
                pltpu.VMEM((2, NX, 2, TOK, half), BF16),
                pltpu.VMEM((2, TOK, half), BF16),
                pltpu.VMEM((TOK, TOK), F32),
                pltpu.VMEM((3, TOK, half), BF16),
                pltpu.VMEM((TOK, half), BF16),
                pltpu.VMEM((3, NX, TOK, cut), BF16),
                pltpu.VMEM((2, NX, TOK, cut), BF16),
                pltpu.VMEM((3, NX, TOK, cut), BF16),
                pltpu.VMEM((2, TOK, half), F32),
                pltpu.VMEM((TOK, half), F32),
                pltpu.VMEM((WLAT, WLON, LEV, half), BF16),
                pltpu.VMEM((WLAT + HALF_ROWS, WLON, LEV, half), BF16),
                pltpu.VMEM((HALF_ROWS, WLON, LEV, half), BF16),
                pltpu.VMEM((WLAT, WLON, LEV, half), BF16),
                pltpu.VMEM((WLAT, 2 * WLON, LEV, half), BF16),
                pltpu.VMEM((2, WLAT, HALF_COLS, LEV, half), BF16),
                pltpu.VMEM((3, n_lon * n_lat, own, cut), F32),
                pltpu.VMEM((3, NX, rest, cut), BF16),
                pltpu.VMEM((3, NX, rest, cut), BF16),
                pltpu.VMEM((3, NZ, NX * own, cut), F32),
                pltpu.VMEM((3, NZ, NX * own, cut), BF16),
                pltpu.VMEM((3, NZ, NX * own, cut), BF16),
                pltpu.VMEM((NX, 3, own, cut), F32),
                pltpu.VMEM((NX, 3, own, cut), F32),
                dma((7,)),
                dma((3, 5)),
                dma((3, 5)),
                dma((3,)),
                dma((3,)),
                dma((2, NX)),
                dma((2, NX)),
                dma((2, NX)),
                dma((2, NX)),
                dma((3, NX)),
                dma((3, NX)),
                dma((3, NX)),
                dma((3, NX)),
                dma((3, NZ)),
                dma((3, NZ)),
                dma((3, NX)),
                dma((3, NX)),
            ],
            compiler_params=pltpu.CompilerParams(
                collective_id=0, has_side_effects=True, vmem_limit_bytes=60 * 2**20
            ),
        )(
            lat_shift,
            lon_shift,
            *(
                pltpu.with_memory_space_constraint(array, pltpu.HBM)
                for array in (
                    band_count,
                    tokens.transpose(1, 2, 0, 3),
                    grad_out.transpose(1, 2, 0, 3),
                    w_qkv,
                    w_out,
                )
            )
        )
        return gtok.transpose(2, 0, 1, 3), gw

    in_specs = (
        P(None, "lat", "lon", "head"),
        P(None, "lat", "lon", "head"),
        P(None, None, "head"),
        P("head", None),
        P(),
        P(),
        P(),
    )
    out_specs = (P(None, "lat", "lon", "head"), P(None, ("lon", "lat"), "head"))
    return jax.shard_map(shards, mesh=mesh, in_specs=in_specs, out_specs=out_specs, check_vma=False)
```

```python
import functools

import jax
import jax.numpy as jnp
from jax import lax
from jax.experimental import pallas as pl
from jax.experimental.pallas import tpu as pltpu
from jax.sharding import PartitionSpec as P

MESH = pl.DeviceIdType.MESH
HEAD_DIM = 64
LEV = 2
WLAT = 12
WLON = 6
NX = 4
NZ = 8
TOK = LEV * WLAT * WLON
ROW = LEV * WLON
HALF_ROWS = WLAT // 2
HALF_COLS = WLON // 2
F32 = jnp.float32
BF16 = jnp.bfloat16


def nn(a, b):
    return lax.dot_general(a, b, (((1,), (0,)), ((), ())), preferred_element_type=F32)


def nt(a, b):
    return lax.dot_general(a, b, (((1,), (1,)), ((), ())), preferred_element_type=F32)


def tn(a, b):
    return lax.dot_general(a, b, (((0,), (0,)), ((), ())), preferred_element_type=F32)


def iota(shape, axis):
    return lax.broadcasted_iota(jnp.int32, shape, axis)


def by12(t):
    return (t * 342) >> 12


def kernel(
    sizes,
    lat_ref,
    lon_ref,
    band_hbm,
    tok_hbm,
    gout_hbm,
    wqkv_hbm,
    wout_hbm,
    gtok_ref,
    gw_ref,
    wqkv,
    wout,
    band_ref,
    own_block,
    tok_wide,
    gout_wide,
    lat_send,
    xo,
    xg,
    go,
    bias,
    probs_of,
    qkv,
    ga,
    gall,
    own_qk,
    g_recv,
    gin,
    gin_recv,
    back_own,
    back_rows,
    back_send,
    side_own,
    side_cols,
    side_send,
    parts,
    psend,
    precv,
    rz,
    zsend,
    zrecv,
    rf,
    frecv,
    load_sem,
    halo_send_sem,
    halo_recv_sem,
    core_send_sem,
    core_recv_sem,
    xg_send_sem,
    xg_recv_sem,
    relay_send_sem,
    relay_recv_sem,
    g_send_sem,
    g_recv_sem,
    p_send_sem,
    p_recv_sem,
    z_send_sem,
    z_recv_sem,
    f_send_sem,
    f_recv_sem,
):
    n_lon, n_lat, width, half = sizes
    n_ylo = n_lon // (NX * NZ)
    n_y = n_lat * n_ylo
    assert n_y == NX
    cut = half // NX
    lon = lax.axis_index("lon")
    lat = lax.axis_index("lat")
    core = lax.axis_index("head")
    x = lon % NX
    z = (lon // NX) % NZ
    ylo = lon // (NX * NZ)
    y = lat * n_ylo + ylo

    right = ((lon + 1) % n_lon, lat, core)
    left = ((lon + n_lon - 1) % n_lon, lat, core)
    across = (lon, (lat + 1) % n_lat, core)
    across_right = ((lon + 1) % n_lon, (lat + 1) % n_lat, core)
    across_left = ((lon + n_lon - 1) % n_lon, (lat + 1) % n_lat, core)
    sibling = (lon, lat, 1 - core)

    def x_peer(d):
        return (lon - x + (x + d) % NX, lat, core)

    def y_peer(d):
        other = (y + d) % n_y
        return (lon + (other % n_ylo - ylo) * (NX * NZ), other // n_ylo, core)

    def z_peer(d):
        return (lon + ((z + d) % NZ - z) * NX, lat, core)

    def either(for_first, for_second):
        return for_first + core * (for_second - for_first)

    def wide_peer(d):
        return tuple(either(a, b) for a, b in zip(x_peer(d)[:2], y_peer(d)[:2])) + (core,)

    def slim_peer(d):
        return tuple(either(a, b) for a, b in zip(y_peer(d)[:2], x_peer(d)[:2])) + (core,)

    wide_at = either(x, y)
    slim_at = either(y, x)

    def x_block(i):
        return i * n_lat

    def y_block(i):
        return (i % n_ylo) * (NZ * NX * n_lat) + i // n_ylo

    def wide_block(i):
        return either(x_block(i), y_block(i))

    def slim_block(i):
        return either(y_block(i), x_block(i))

    partners = [right, left, across, across_right, across_left, sibling]
    partners += [x_peer(d) for d in range(1, NX)]
    partners += [y_peer(d) for d in range(1, n_y)]
    partners += [z_peer(d) for d in range(1, NZ)]

    def remote(src, dst, send_sem, recv_sem, device):
        return pltpu.make_async_remote_copy(
            src_ref=src,
            dst_ref=dst,
            send_sem=send_sem,
            recv_sem=recv_sem,
            device_id=device,
            device_id_type=MESH,
        )

    barrier = pltpu.get_barrier_semaphore()
    for partner in partners:
        pl.semaphore_signal(barrier, inc=1, device_id=partner, device_id_type=MESH)

    load_band = pltpu.make_async_copy(band_hbm, band_ref, load_sem.at[0])
    load_band.start()
    inputs = (tok_hbm, gout_hbm)
    wides = (tok_wide, gout_wide)
    middle = slice(HALF_COLS, HALF_COLS + WLON)
    loads = []
    for a in range(2):
        loads.append(pltpu.make_async_copy(inputs[a], own_block.at[a], load_sem.at[1 + a]))
        loads.append(
            pltpu.make_async_copy(inputs[a], wides[a].at[0:WLAT, middle], load_sem.at[3 + a])
        )
    loads.append(pltpu.make_async_copy(wqkv_hbm, wqkv, load_sem.at[5]))
    loads.append(pltpu.make_async_copy(wout_hbm, wout, load_sem.at[6]))
    for load in loads:
        load.start()

    row_shift = lat_ref[0]
    col_shift = lon_ref[0]
    row_swap = jnp.where(row_shift > HALF_ROWS, 1, 0)
    col_swap = jnp.where(col_shift > HALF_COLS, 1, 0)
    f = row_shift - WLAT * row_swap
    e = col_shift - WLON * col_swap

    loads[0].wait()
    loads[2].wait()
    for a in range(2):
        lat_send[a] = own_block[a, pl.ds(HALF_ROWS * row_swap, HALF_ROWS)]

    load_band.wait()
    k_at = iota((TOK, TOK), 0)
    q_at = iota((TOK, TOK), 1)
    first_row = WLAT * ((lat + row_swap) % n_lat) + row_shift
    k_row = by12(k_at)
    q_row = by12(q_at)
    n_rows = WLAT * n_lat
    counts = jnp.zeros((TOK, TOK), jnp.int32)
    for r in range(WLAT):
        raw = first_row + r
        counts = jnp.where(k_row == r, band_ref[jnp.where(raw >= n_rows, raw - n_rows, raw)], counts)
    n_cols = WLON * n_lon
    k_col = ((k_at - ROW * k_row) >> 1) + (WLON * lon + e)
    k_col = jnp.where(k_col < 0, k_col + n_cols, k_col)
    k_col = jnp.where(k_col >= n_cols, k_col - n_cols, k_col)
    same_side = (k_row + first_row >= n_rows) == (q_row + first_row >= n_rows)
    allowed = ((k_col < counts) | (k_at == q_at)) & same_side
    bias[...] = jnp.where(allowed, 0.0, -1e30)

    pl.semaphore_wait(barrier, len(partners))

    halo = []
    before = slice(0, HALF_COLS)
    after = slice(HALF_COLS + WLON, 2 * WLON)
    left_half = slice(0, HALF_COLS)
    right_half = slice(HALF_COLS, WLON)
    kept = slice(0, WLAT)
    borrowed = slice(WLAT, WLAT + HALF_ROWS)
    for a in range(2):
        copies = []
        for n, (src, rows, columns, device) in enumerate(
            (
                (lat_send.at[a], borrowed, middle, across),
                (inputs[a].at[:, left_half], kept, after, left),
                (inputs[a].at[:, right_half], kept, before, right),
                (lat_send.at[a, :, left_half], borrowed, after, across_left),
                (lat_send.at[a, :, right_half], borrowed, before, across_right),
            )
        ):
            copy = remote(
                src, wides[a].at[rows, columns], halo_send_sem.at[a, n], halo_recv_sem.at[a, n], device
            )
            copy.start()
            copies.append(copy)
        halo.append(copies)
    sends = [copy for copies in halo for copy in copies]

    over_core = []
    over_plane = {}

    def make_window(a):
        loads[2 * a + 1].wait()
        for copy in halo[a]:
            copy.wait_recv()
        columns = pl.ds(e + HALF_COLS, WLON)
        picked = []
        for r in range(WLAT):
            q = f + r
            picked.append(wides[a][jnp.where(q < 0, q + (WLAT + HALF_ROWS), q), columns])
        held = (xo, go)[a]
        held[core] = jnp.stack(picked).reshape(TOK, half)
        mine = held.at[core]
        copy = remote(mine, mine, core_send_sem.at[a], core_recv_sem.at[a], sibling)
        copy.start()
        over_core.append(copy)

    make_window(0)
    for d in (1, NX - 1) + tuple(range(2, NX - 1)):
        for axis, peer in ((0, x_peer(d)), (1, y_peer(d))):
            if (axis, d) in over_plane:
                continue
            copy = remote(
                xo.at[core],
                xg.at[axis, d, core],
                xg_send_sem.at[axis, d],
                xg_recv_sem.at[axis, d],
                peer,
            )
            copy.start()
            over_plane[axis, d] = copy
    sends += list(over_plane.values())

    loads[4].wait()
    over_core[0].wait_recv()
    for j in range(3):
        total = nn(xo[0], wqkv[j, :half]) + nn(xo[1], wqkv[j, half:])
        qkv[j] = total.astype(BF16)

    scale = HEAD_DIM ** (-0.5)
    order = []
    for t in range(2):
        at = slice(t * HEAD_DIM, (t + 1) * HEAD_DIM)
        for n in range(NX):
            d = (n + 1) % NX
            pair = (wide_at + d) % NX
            lanes = pl.ds(pl.multiple_of(pair * cut, cut), cut)
            order.append((t, at, d, pair, lanes))
    for n, (t, at, d, pair, lanes) in enumerate(order):
        scores = nt(qkv[1, :, lanes][:, at], qkv[0, :, lanes][:, at]) * scale
        scores = jnp.where(bias[...] == 0.0, scores, -1e30)
        raised = jnp.exp(scores - jnp.max(scores, 0, keepdims=True))
        probs_of[n] = raised * (1.0 / jnp.sum(raised, 0, keepdims=True))

    make_window(1)
    sends += over_core
    loads[5].wait()
    over_core[1].wait_recv()
    ga[...] = (nt(go[0], wout[:, :half]) + nt(go[1], wout[:, half:])).astype(BF16)

    def factor_peer(t, d):
        return wide_peer(d) if t < 2 else slim_peer(d)

    def sum_peer(t, d):
        return slim_peer(d) if t < 2 else wide_peer(d)

    relays = {}

    def relay(d):
        for axis in range(2):
            over_plane[axis, d].wait_recv()
            mine = xg.at[axis, d, core]
            copy = remote(
                mine, mine, relay_send_sem.at[axis, d], relay_recv_sem.at[axis, d], sibling
            )
            copy.start()
            relays[axis, d] = copy

    over_g = {}
    for n, (t, at, d, pair, lanes) in enumerate(order):
        q, k, v = (qkv[j, :, lanes][:, at] for j in range(3))
        g = ga[:, lanes][:, at]
        probs = probs_of[n]
        grad_probs = nt(v, g)
        inner = jnp.sum(probs * grad_probs, 0, keepdims=True)
        grad_scores = (probs * (grad_probs - inner) * scale).astype(BF16)
        grad_q = tn(grad_scores, k).astype(BF16)
        grad_k = nn(grad_scores, q).astype(BF16)
        gall[0, pair, :, at] = grad_q
        gall[1, pair, :, at] = grad_k
        gall[2, pair, :, at] = nn(probs.astype(BF16), g).astype(BF16)
        own_qk[t, d] = jnp.concatenate([grad_q, grad_k], 1)
        if d:
            copy = remote(
                own_qk.at[t, d],
                g_recv.at[t, d],
                g_send_sem.at[t, d],
                g_recv_sem.at[t, d],
                factor_peer(t, d),
            )
            copy.start()
            over_g[t, d] = copy
    for d in range(1, NX):
        copy = remote(
            gall.at[2, (slim_at + d) % NX],
            g_recv.at[2, d],
            g_send_sem.at[2, d],
            g_recv_sem.at[2, d],
            factor_peer(2, d),
        )
        copy.start()
        over_g[2, d] = copy
    sends += list(over_g.values())

    def grad_in(which):
        rows = pl.ds(pl.multiple_of(which * half, half), half)
        total = 0.0
        for j in range(3):
            joined = jnp.concatenate([gall[j, pair] for pair in range(NX)], 1)
            total = total + nt(joined, wqkv[j, rows])
        return total

    gin[0] = grad_in(1 - core)
    to_sibling = remote(gin.at[0], gin_recv, core_send_sem.at[2], core_recv_sem.at[2], sibling)
    to_sibling.start()
    for d in (1, NX - 1) + tuple(range(2, NX - 1)):
        if (0, d) not in relays:
            relay(d)
    sends += list(relays.values())

    blocks = parts.shape[1]
    own = parts.shape[2]

    def make_product(t):
        axis = core if t < 2 else 1 - core
        halves = []
        for side in range(2):
            halves.append(tn(xo[side], own_qk[t, 0] if t < 2 else gall[2, slim_at]))
        for d in range(1, NX):
            if t == 0:
                relays[0, d].wait_recv()
                relays[1, d].wait_recv()
            over_g[t, d].wait_recv()
            for side in range(2):
                halves[side] = halves[side] + tn(xg[axis, d, side], g_recv[t, d])
        for side in range(2):
            rows = slice(side * (blocks // 2), (side + 1) * (blocks // 2))
            parts[t, rows] = halves[side].reshape(blocks // 2, own, cut)

    def owner_rows(t, i):
        base = slim_block(i) if t < 2 else wide_block(i)
        picked = []
        for k in range(NZ):
            for j in range(NX):
                along = wide_block(j) if t < 2 else slim_block(j)
                picked.append(parts[t, base + along + k * (NX * n_lat)])
        return jnp.concatenate(picked, 0)

    over_p = {}
    for t in range(3):
        make_product(t)
        place = slim_at if t < 2 else wide_at
        for d in range(1, NX):
            psend[t, d] = owner_rows(t, (place + d) % NX).astype(BF16)
            copy = remote(
                psend.at[t, d],
                precv.at[t, d],
                p_send_sem.at[t, d],
                p_recv_sem.at[t, d],
                sum_peer(t, d),
            )
            copy.start()
            over_p[t, d] = copy
    sends += list(over_p.values())

    gin[1] = grad_in(core)

    to_sibling.wait_recv()
    window = (gin[1] + gin_recv[...]).astype(BF16).reshape(WLAT, WLON, LEV, half)
    back_own[...] = window
    back_rows[0:WLAT] = window
    for k in range(HALF_ROWS):
        from_row = k + jnp.where(f > 0, WLAT, -HALF_ROWS) - f
        back_send[k] = back_own[jnp.clip(from_row, 0, WLAT - 1)]
    over_lat_back = remote(
        back_send,
        back_rows.at[WLAT : WLAT + HALF_ROWS],
        halo_send_sem.at[2, 0],
        halo_recv_sem.at[2, 0],
        across,
    )
    over_lat_back.start()

    over_z = {}
    for t in range(3):
        total = owner_rows(t, slim_at if t < 2 else wide_at)
        for d in range(1, NX):
            over_p[t, d].wait_recv()
            total = total + precv[t, d].astype(F32)
        rz[t] = total.reshape(NZ, NX * own, cut)
        for d in range(1, NZ):
            zsend[t, d] = rz[t, (z + d) % NZ].astype(BF16)
            copy = remote(
                zsend.at[t, d],
                zrecv.at[t, d],
                z_send_sem.at[t, d],
                z_recv_sem.at[t, d],
                z_peer(d),
            )
            copy.start()
            over_z[t, d] = copy
    sends += list(over_z.values())

    over_lat_back.wait_recv()
    for b in range(WLAT):
        was = b - f
        home = (was >= 0) & (was < WLAT)
        row = back_rows[jnp.where(home, was, b + WLAT - HALF_ROWS * row_swap)]
        side_own[b] = row
        side_cols[b, 0:WLON] = row
    for s in range(HALF_COLS):
        side_send[0, :, s] = side_own[:, jnp.clip(s - HALF_COLS - e, 0, WLON - 1)]
        side_send[1, :, s] = side_own[:, jnp.clip(s + WLON - e, 0, WLON - 1)]
    side_left = remote(
        side_send.at[0],
        side_cols.at[:, WLON + HALF_COLS : 2 * WLON],
        halo_send_sem.at[2, 1],
        halo_recv_sem.at[2, 1],
        left,
    )
    side_right = remote(
        side_send.at[1],
        side_cols.at[:, WLON : WLON + HALF_COLS],
        halo_send_sem.at[2, 2],
        halo_recv_sem.at[2, 2],
        right,
    )
    side_left.start()
    side_right.start()
    sends += [to_sibling, over_lat_back, side_left, side_right]

    side_left.wait_recv()
    side_right.wait_recv()
    for q in range(WLON):
        c = q - e
        home = (c >= 0) & (c < WLON)
        gtok_ref[:, q] = side_cols[:, jnp.where(home, c, q + WLON)]

    last = {}
    for t in range(3):
        total = rz[t, z]
        for d in range(1, NZ):
            over_z[t, d].wait_recv()
            total = total + zrecv[t, d].astype(F32)
        rf[:, t] = total.reshape(NX, own, cut)
        if t == 0:
            continue
        group = slice(0, 2) if t == 1 else slice(2, 3)
        place = wide_at if t == 1 else slim_at
        for d in range(1, NX):
            copy = remote(
                rf.at[(place + d) % NX, group],
                frecv.at[d, group],
                f_send_sem.at[t, d],
                f_recv_sem.at[t, d],
                factor_peer(t, d),
            )
            copy.start()
            last[t, d] = copy
    sends += list(last.values())
    for d in range(NX):
        if d:
            last[1, d].wait_recv()
            last[2, d].wait_recv()
            first, second, values = (frecv[d, t] for t in range(3))
        else:
            first, second, values = rf[wide_at, 0], rf[wide_at, 1], rf[slim_at, 2]
        lanes = pl.ds(pl.multiple_of(((wide_at + NX - d) % NX) * cut, cut), cut)
        for j in range(2):
            at = slice(j * HEAD_DIM, (j + 1) * HEAD_DIM)
            gw_ref[j, :, lanes] = jnp.concatenate([first[:, at], second[:, at]], 1)
        lanes = pl.ds(pl.multiple_of(((slim_at + NX - d) % NX) * cut, cut), cut)
        gw_ref[2, :, lanes] = values

    for copy in sends:
        copy.wait_send()


def solution(mesh):
    n_lon, n_lat = mesh.shape["lon"], mesh.shape["lat"]

    def shards(tokens, grad_out, w_qkv, w_out, band_count, lat_shift, lon_shift):
        half = tokens.shape[-1]
        width = w_qkv.shape[1]
        own = width // (n_lon * n_lat)
        cut = half // NX
        rest = NZ * NX * own
        vmem = pl.BlockSpec(memory_space=pltpu.VMEM)
        smem = pl.BlockSpec(memory_space=pltpu.SMEM)
        hbm = pl.BlockSpec(memory_space=pltpu.HBM)
        dma = pltpu.SemaphoreType.DMA
        gtok, gw = pl.pallas_call(
            functools.partial(kernel, (n_lon, n_lat, width, half)),
            out_shape=(
                pltpu.VMEM((WLAT, WLON, LEV, half), BF16),
                pltpu.VMEM((3, own, half), F32),
            ),
            in_specs=[smem] * 2 + [hbm] * 5,
            out_specs=(vmem, vmem),
            scratch_shapes=[
                pltpu.VMEM((3, width, half), BF16),
                pltpu.VMEM((half, width), BF16),
                pltpu.SMEM(band_count.shape, jnp.int32),
                pltpu.VMEM((2, WLAT, WLON, LEV, half), BF16),
                pltpu.VMEM((WLAT + HALF_ROWS, 2 * WLON, LEV, half), BF16),
                pltpu.VMEM((WLAT + HALF_ROWS, 2 * WLON, LEV, half), BF16),
                pltpu.VMEM((2, HALF_ROWS, WLON, LEV, half), BF16),
                pltpu.VMEM((2, TOK, half), BF16),
                pltpu.VMEM((2, NX, 2, TOK, half), BF16),
                pltpu.VMEM((2, TOK, half), BF16),
                pltpu.VMEM((TOK, TOK), F32),
                pltpu.VMEM((half // HEAD_DIM, TOK, TOK), F32),
                pltpu.VMEM((3, TOK, half), BF16),
                pltpu.VMEM((TOK, half), BF16),
                pltpu.VMEM((3, NX, TOK, cut), BF16),
                pltpu.VMEM((2, NX, TOK, cut), BF16),
                pltpu.VMEM((3, NX, TOK, cut), BF16),
                pltpu.VMEM((2, TOK, half), F32),
                pltpu.VMEM((TOK, half), F32),
                pltpu.VMEM((WLAT, WLON, LEV, half), BF16),
                pltpu.VMEM((WLAT + HALF_ROWS, WLON, LEV, half), BF16),
                pltpu.VMEM((HALF_ROWS, WLON, LEV, half), BF16),
                pltpu.VMEM((WLAT, WLON, LEV, half), BF16),
                pltpu.VMEM((WLAT, 2 * WLON, LEV, half), BF16),
                pltpu.VMEM((2, WLAT, HALF_COLS, LEV, half), BF16),
                pltpu.VMEM((3, n_lon * n_lat, own, cut), F32),
                pltpu.VMEM((3, NX, rest, cut), BF16),
                pltpu.VMEM((3, NX, rest, cut), BF16),
                pltpu.VMEM((3, NZ, NX * own, cut), F32),
                pltpu.VMEM((3, NZ, NX * own, cut), BF16),
                pltpu.VMEM((3, NZ, NX * own, cut), BF16),
                pltpu.VMEM((NX, 3, own, cut), F32),
                pltpu.VMEM((NX, 3, own, cut), F32),
                dma((7,)),
                dma((3, 5)),
                dma((3, 5)),
                dma((3,)),
                dma((3,)),
                dma((2, NX)),
                dma((2, NX)),
                dma((2, NX)),
                dma((2, NX)),
                dma((3, NX)),
                dma((3, NX)),
                dma((3, NX)),
                dma((3, NX)),
                dma((3, NZ)),
                dma((3, NZ)),
                dma((3, NX)),
                dma((3, NX)),
            ],
            compiler_params=pltpu.CompilerParams(
                collective_id=0, has_side_effects=True, vmem_limit_bytes=60 * 2**20
            ),
        )(
            lat_shift,
            lon_shift,
            *(
                pltpu.with_memory_space_constraint(array, pltpu.HBM)
                for array in (
                    band_count,
                    tokens.transpose(1, 2, 0, 3),
                    grad_out.transpose(1, 2, 0, 3),
                    w_qkv,
                    w_out,
                )
            )
        )
        return gtok.transpose(2, 0, 1, 3), gw

    in_specs = (
        P(None, "lat", "lon", "head"),
        P(None, "lat", "lon", "head"),
        P(None, None, "head"),
        P("head", None),
        P(),
        P(),
        P(),
    )
    out_specs = (P(None, "lat", "lon", "head"), P(None, ("lon", "lat"), "head"))
    return jax.shard_map(shards, mesh=mesh, in_specs=in_specs, out_specs=out_specs, check_vma=False)
```

```python
import functools

import jax
import jax.numpy as jnp
from jax import lax
from jax.experimental import pallas as pl
from jax.experimental.pallas import tpu as pltpu
from jax.sharding import PartitionSpec as P

MESH = pl.DeviceIdType.MESH
HEAD_DIM = 64
LEV = 2
WLAT = 12
WLON = 6
NX = 4
NZ = 8
TOK = LEV * WLAT * WLON
ROW = LEV * WLON
HALF_ROWS = WLAT // 2
HALF_COLS = WLON // 2
F32 = jnp.float32
BF16 = jnp.bfloat16


def nn(a, b):
    return lax.dot_general(a, b, (((1,), (0,)), ((), ())), preferred_element_type=F32)


def nt(a, b):
    return lax.dot_general(a, b, (((1,), (1,)), ((), ())), preferred_element_type=F32)


def tn(a, b):
    return lax.dot_general(a, b, (((0,), (0,)), ((), ())), preferred_element_type=F32)


def iota(shape, axis):
    return lax.broadcasted_iota(jnp.int32, shape, axis)


def by12(t):
    return (t * 342) >> 12


def kernel(
    sizes,
    lat_ref,
    lon_ref,
    band_hbm,
    tok_hbm,
    gout_hbm,
    wqkv_hbm,
    wout_hbm,
    gtok_ref,
    gw_ref,
    wqkv,
    wout,
    band_ref,
    own_block,
    tok_wide,
    gout_wide,
    lat_send,
    xo,
    xg,
    go,
    bias,
    probs_of,
    qkv,
    ga,
    gall,
    own_qk,
    g_recv,
    gin,
    gin_recv,
    back_own,
    back_rows,
    back_send,
    side_own,
    side_cols,
    side_send,
    parts,
    psend,
    precv,
    rz,
    zsend,
    zrecv,
    rf,
    frecv,
    load_sem,
    halo_send_sem,
    halo_recv_sem,
    core_send_sem,
    core_recv_sem,
    xg_send_sem,
    xg_recv_sem,
    relay_send_sem,
    relay_recv_sem,
    g_send_sem,
    g_recv_sem,
    p_send_sem,
    p_recv_sem,
    z_send_sem,
    z_recv_sem,
    f_send_sem,
    f_recv_sem,
):
    n_lon, n_lat, width, half = sizes
    n_ylo = n_lon // (NX * NZ)
    n_y = n_lat * n_ylo
    assert n_y == NX
    cut = half // NX
    lon = lax.axis_index("lon")
    lat = lax.axis_index("lat")
    core = lax.axis_index("head")
    x = lon % NX
    z = (lon // NX) % NZ
    ylo = lon // (NX * NZ)
    y = lat * n_ylo + ylo

    right = ((lon + 1) % n_lon, lat, core)
    left = ((lon + n_lon - 1) % n_lon, lat, core)
    across = (lon, (lat + 1) % n_lat, core)
    across_right = ((lon + 1) % n_lon, (lat + 1) % n_lat, core)
    across_left = ((lon + n_lon - 1) % n_lon, (lat + 1) % n_lat, core)
    sibling = (lon, lat, 1 - core)

    def x_peer(d):
        return (lon - x + (x + d) % NX, lat, core)

    def y_peer(d):
        other = (y + d) % n_y
        return (lon + (other % n_ylo - ylo) * (NX * NZ), other // n_ylo, core)

    def z_peer(d):
        return (lon + ((z + d) % NZ - z) * NX, lat, core)

    def either(for_first, for_second):
        return for_first + core * (for_second - for_first)

    def wide_peer(d):
        return tuple(either(a, b) for a, b in zip(x_peer(d)[:2], y_peer(d)[:2])) + (core,)

    def slim_peer(d):
        return tuple(either(a, b) for a, b in zip(y_peer(d)[:2], x_peer(d)[:2])) + (core,)

    wide_at = either(x, y)
    slim_at = either(y, x)

    def x_block(i):
        return i * n_lat

    def y_block(i):
        return (i % n_ylo) * (NZ * NX * n_lat) + i // n_ylo

    def wide_block(i):
        return either(x_block(i), y_block(i))

    def slim_block(i):
        return either(y_block(i), x_block(i))

    partners = [right, left, across, across_right, across_left, sibling]
    partners += [x_peer(d) for d in range(1, NX)]
    partners += [y_peer(d) for d in range(1, n_y)]
    partners += [z_peer(d) for d in range(1, NZ)]

    def remote(src, dst, send_sem, recv_sem, device):
        return pltpu.make_async_remote_copy(
            src_ref=src,
            dst_ref=dst,
            send_sem=send_sem,
            recv_sem=recv_sem,
            device_id=device,
            device_id_type=MESH,
        )

    barrier = pltpu.get_barrier_semaphore()
    for partner in partners:
        pl.semaphore_signal(barrier, inc=1, device_id=partner, device_id_type=MESH)

    load_band = pltpu.make_async_copy(band_hbm, band_ref, load_sem.at[0])
    load_band.start()
    inputs = (tok_hbm, gout_hbm)
    wides = (tok_wide, gout_wide)
    middle = slice(HALF_COLS, HALF_COLS + WLON)
    loads = []
    for a in range(2):
        loads.append(pltpu.make_async_copy(inputs[a], own_block.at[a], load_sem.at[1 + a]))
        loads.append(
            pltpu.make_async_copy(inputs[a], wides[a].at[0:WLAT, middle], load_sem.at[3 + a])
        )
    loads.append(pltpu.make_async_copy(wqkv_hbm, wqkv, load_sem.at[5]))
    loads.append(pltpu.make_async_copy(wout_hbm, wout, load_sem.at[6]))
    for load in loads:
        load.start()

    row_shift = lat_ref[0]
    col_shift = lon_ref[0]
    row_swap = jnp.where(row_shift > HALF_ROWS, 1, 0)
    col_swap = jnp.where(col_shift > HALF_COLS, 1, 0)
    f = row_shift - WLAT * row_swap
    e = col_shift - WLON * col_swap

    loads[0].wait()
    loads[2].wait()
    for a in range(2):
        lat_send[a] = own_block[a, pl.ds(HALF_ROWS * row_swap, HALF_ROWS)]

    load_band.wait()
    k_at = iota((TOK, TOK), 0)
    q_at = iota((TOK, TOK), 1)
    first_row = WLAT * ((lat + row_swap) % n_lat) + row_shift
    k_row = by12(k_at)
    q_row = by12(q_at)
    n_rows = WLAT * n_lat
    counts = jnp.zeros((TOK, TOK), jnp.int32)
    for r in range(WLAT):
        raw = first_row + r
        counts = jnp.where(k_row == r, band_ref[jnp.where(raw >= n_rows, raw - n_rows, raw)], counts)
    n_cols = WLON * n_lon
    k_col = ((k_at - ROW * k_row) >> 1) + (WLON * lon + e)
    k_col = jnp.where(k_col < 0, k_col + n_cols, k_col)
    k_col = jnp.where(k_col >= n_cols, k_col - n_cols, k_col)
    same_side = (k_row + first_row >= n_rows) == (q_row + first_row >= n_rows)
    allowed = ((k_col < counts) | (k_at == q_at)) & same_side
    bias[...] = jnp.where(allowed, 0.0, -1e30)

    pl.semaphore_wait(barrier, len(partners))

    halo = []
    before = slice(0, HALF_COLS)
    after = slice(HALF_COLS + WLON, 2 * WLON)
    left_half = slice(0, HALF_COLS)
    right_half = slice(HALF_COLS, WLON)
    kept = slice(0, WLAT)
    borrowed = slice(WLAT, WLAT + HALF_ROWS)
    for a in range(2):
        copies = []
        for n, (src, rows, columns, device) in enumerate(
            (
                (lat_send.at[a], borrowed, middle, across),
                (inputs[a].at[:, left_half], kept, after, left),
                (inputs[a].at[:, right_half], kept, before, right),
                (lat_send.at[a, :, left_half], borrowed, after, across_left),
                (lat_send.at[a, :, right_half], borrowed, before, across_right),
            )
        ):
            copy = remote(
                src, wides[a].at[rows, columns], halo_send_sem.at[a, n], halo_recv_sem.at[a, n], device
            )
            copy.start()
            copies.append(copy)
        halo.append(copies)
    sends = [copy for copies in halo for copy in copies]

    over_core = []
    over_plane = {}

    def make_window(a):
        loads[2 * a + 1].wait()
        for copy in halo[a]:
            copy.wait_recv()
        columns = pl.ds(e + HALF_COLS, WLON)
        picked = []
        for r in range(WLAT):
            q = f + r
            picked.append(wides[a][jnp.where(q < 0, q + (WLAT + HALF_ROWS), q), columns])
        held = (xo, go)[a]
        held[core] = jnp.stack(picked).reshape(TOK, half)
        mine = held.at[core]
        copy = remote(mine, mine, core_send_sem.at[a], core_recv_sem.at[a], sibling)
        copy.start()
        over_core.append(copy)

    make_window(0)
    for d in (1, NX - 1) + tuple(range(2, NX - 1)):
        for axis, peer in ((0, x_peer(d)), (1, y_peer(d))):
            if (axis, d) in over_plane:
                continue
            copy = remote(
                xo.at[core],
                xg.at[axis, d, core],
                xg_send_sem.at[axis, d],
                xg_recv_sem.at[axis, d],
                peer,
            )
            copy.start()
            over_plane[axis, d] = copy
    sends += list(over_plane.values())

    loads[4].wait()
    over_core[0].wait_recv()
    for j in range(3):
        total = nn(xo[0], wqkv[j, :half]) + nn(xo[1], wqkv[j, half:])
        qkv[j] = total.astype(BF16)

    scale = HEAD_DIM ** (-0.5)
    order = []
    for t in range(2):
        at = slice(t * HEAD_DIM, (t + 1) * HEAD_DIM)
        for n in range(NX):
            d = (n + 1) % NX
            pair = (wide_at + d) % NX
            lanes = pl.ds(pl.multiple_of(pair * cut, cut), cut)
            order.append((t, at, d, pair, lanes))
    for n, (t, at, d, pair, lanes) in enumerate(order):
        scores = nt(qkv[1, :, lanes][:, at], qkv[0, :, lanes][:, at]) * scale
        scores = jnp.where(bias[...] == 0.0, scores, -1e30)
        raised = jnp.exp(scores - jnp.max(scores, 0, keepdims=True))
        probs_of[n] = raised * (1.0 / jnp.sum(raised, 0, keepdims=True))

    make_window(1)
    sends += over_core
    loads[5].wait()
    over_core[1].wait_recv()
    ga[...] = (nt(go[0], wout[:, :half]) + nt(go[1], wout[:, half:])).astype(BF16)

    def factor_peer(t, d):
        return wide_peer(d) if t < 2 else slim_peer(d)

    def sum_peer(t, d):
        return slim_peer(d) if t < 2 else wide_peer(d)

    relays = {}

    def relay(d):
        for axis in range(2):
            over_plane[axis, d].wait_recv()
            mine = xg.at[axis, d, core]
            copy = remote(
                mine, mine, relay_send_sem.at[axis, d], relay_recv_sem.at[axis, d], sibling
            )
            copy.start()
            relays[axis, d] = copy

    over_g = {}
    for n, (t, at, d, pair, lanes) in enumerate(order):
        q, k, v = (qkv[j, :, lanes][:, at] for j in range(3))
        g = ga[:, lanes][:, at]
        probs = probs_of[n]
        grad_probs = nt(v, g)
        inner = jnp.sum(probs * grad_probs, 0, keepdims=True)
        grad_scores = (probs * (grad_probs - inner) * scale).astype(BF16)
        grad_q = tn(grad_scores, k).astype(BF16)
        grad_k = nn(grad_scores, q).astype(BF16)
        gall[0, pair, :, at] = grad_q
        gall[1, pair, :, at] = grad_k
        gall[2, pair, :, at] = nn(probs.astype(BF16), g).astype(BF16)
        own_qk[t, d] = jnp.concatenate([grad_q, grad_k], 1)
        if d:
            copy = remote(
                own_qk.at[t, d],
                g_recv.at[t, d],
                g_send_sem.at[t, d],
                g_recv_sem.at[t, d],
                factor_peer(t, d),
            )
            copy.start()
            over_g[t, d] = copy
    for d in range(1, NX):
        copy = remote(
            gall.at[2, (slim_at + d) % NX],
            g_recv.at[2, d],
            g_send_sem.at[2, d],
            g_recv_sem.at[2, d],
            factor_peer(2, d),
        )
        copy.start()
        over_g[2, d] = copy
    sends += list(over_g.values())

    def grad_in(which):
        rows = pl.ds(pl.multiple_of(which * half, half), half)
        total = 0.0
        for j in range(3):
            joined = jnp.concatenate([gall[j, pair] for pair in range(NX)], 1)
            total = total + nt(joined, wqkv[j, rows])
        return total

    gin[0] = grad_in(1 - core)
    to_sibling = remote(gin.at[0], gin_recv, core_send_sem.at[2], core_recv_sem.at[2], sibling)
    to_sibling.start()
    blocks = parts.shape[1]
    own = parts.shape[2]
    sides = [slice(0, blocks // 2), slice(blocks // 2, blocks)]
    for t in range(3):
        for side, rows in enumerate(sides):
            product = tn(xo[side], own_qk[t, 0] if t < 2 else gall[2, slim_at])
            parts[t, rows] = product.reshape(blocks // 2, own, cut)
    for d in (1, NX - 1) + tuple(range(2, NX - 1)):
        if (0, d) not in relays:
            relay(d)
    sends += list(relays.values())

    gin[1] = grad_in(core)

    to_sibling.wait_recv()
    window = (gin[1] + gin_recv[...]).astype(BF16).reshape(WLAT, WLON, LEV, half)
    back_own[...] = window
    back_rows[0:WLAT] = window
    for k in range(HALF_ROWS):
        from_row = k + jnp.where(f > 0, WLAT, -HALF_ROWS) - f
        back_send[k] = back_own[jnp.clip(from_row, 0, WLAT - 1)]
    over_lat_back = remote(
        back_send,
        back_rows.at[WLAT : WLAT + HALF_ROWS],
        halo_send_sem.at[2, 0],
        halo_recv_sem.at[2, 0],
        across,
    )
    over_lat_back.start()

    def make_product(t):
        axis = core if t < 2 else 1 - core
        halves = [parts[t, rows].reshape(half, cut) for rows in sides]
        for d in range(1, NX):
            if t == 0:
                relays[0, d].wait_recv()
                relays[1, d].wait_recv()
            over_g[t, d].wait_recv()
            for side in range(2):
                halves[side] = halves[side] + tn(xg[axis, d, side], g_recv[t, d])
        for side, rows in enumerate(sides):
            parts[t, rows] = halves[side].reshape(blocks // 2, own, cut)

    def owner_rows(t, i):
        base = slim_block(i) if t < 2 else wide_block(i)
        picked = []
        for k in range(NZ):
            for j in range(NX):
                along = wide_block(j) if t < 2 else slim_block(j)
                picked.append(parts[t, base + along + k * (NX * n_lat)])
        return jnp.concatenate(picked, 0)

    over_p = {}
    for t in range(3):
        make_product(t)
        place = slim_at if t < 2 else wide_at
        for d in range(1, NX):
            psend[t, d] = owner_rows(t, (place + d) % NX).astype(BF16)
            copy = remote(
                psend.at[t, d],
                precv.at[t, d],
                p_send_sem.at[t, d],
                p_recv_sem.at[t, d],
                sum_peer(t, d),
            )
            copy.start()
            over_p[t, d] = copy

    over_lat_back.wait_recv()
    for b in range(WLAT):
        was = b - f
        home = (was >= 0) & (was < WLAT)
        row = back_rows[jnp.where(home, was, b + WLAT - HALF_ROWS * row_swap)]
        side_own[b] = row
        side_cols[b, 0:WLON] = row
    for s in range(HALF_COLS):
        side_send[0, :, s] = side_own[:, jnp.clip(s - HALF_COLS - e, 0, WLON - 1)]
        side_send[1, :, s] = side_own[:, jnp.clip(s + WLON - e, 0, WLON - 1)]
    side_left = remote(
        side_send.at[0],
        side_cols.at[:, WLON + HALF_COLS : 2 * WLON],
        halo_send_sem.at[2, 1],
        halo_recv_sem.at[2, 1],
        left,
    )
    side_right = remote(
        side_send.at[1],
        side_cols.at[:, WLON : WLON + HALF_COLS],
        halo_send_sem.at[2, 2],
        halo_recv_sem.at[2, 2],
        right,
    )
    side_left.start()
    side_right.start()

    for copy in sends:
        copy.wait_send()

    over_z = {}
    for t in range(3):
        total = owner_rows(t, slim_at if t < 2 else wide_at)
        for d in range(1, NX):
            over_p[t, d].wait_recv()
            total = total + precv[t, d].astype(F32)
        rz[t] = total.reshape(NZ, NX * own, cut)
        for d in range(1, NZ):
            zsend[t, d] = rz[t, (z + d) % NZ].astype(BF16)
            copy = remote(
                zsend.at[t, d],
                zrecv.at[t, d],
                z_send_sem.at[t, d],
                z_recv_sem.at[t, d],
                z_peer(d),
            )
            copy.start()
            over_z[t, d] = copy
    for copy in list(over_p.values()) + [to_sibling, over_lat_back, side_left, side_right]:
        copy.wait_send()

    side_left.wait_recv()
    side_right.wait_recv()
    for q in range(WLON):
        c = q - e
        home = (c >= 0) & (c < WLON)
        gtok_ref[:, q] = side_cols[:, jnp.where(home, c, q + WLON)]

    last = {}
    for t in range(3):
        total = rz[t, z]
        for d in range(1, NZ):
            over_z[t, d].wait_recv()
            total = total + zrecv[t, d].astype(F32)
        rf[:, t] = total.reshape(NX, own, cut)
        if t == 0:
            continue
        group = slice(0, 2) if t == 1 else slice(2, 3)
        place = wide_at if t == 1 else slim_at
        for d in range(1, NX):
            copy = remote(
                rf.at[(place + d) % NX, group],
                frecv.at[d, group],
                f_send_sem.at[t, d],
                f_recv_sem.at[t, d],
                factor_peer(t, d),
            )
            copy.start()
            last[t, d] = copy
    for d in range(NX):
        if d:
            last[1, d].wait_recv()
            last[2, d].wait_recv()
            first, second, values = (frecv[d, t] for t in range(3))
        else:
            first, second, values = rf[wide_at, 0], rf[wide_at, 1], rf[slim_at, 2]
        lanes = pl.ds(pl.multiple_of(((wide_at + NX - d) % NX) * cut, cut), cut)
        for j in range(2):
            at = slice(j * HEAD_DIM, (j + 1) * HEAD_DIM)
            gw_ref[j, :, lanes] = jnp.concatenate([first[:, at], second[:, at]], 1)
        lanes = pl.ds(pl.multiple_of(((slim_at + NX - d) % NX) * cut, cut), cut)
        gw_ref[2, :, lanes] = values

    for copy in list(over_z.values()) + list(last.values()):
        copy.wait_send()


def solution(mesh):
    n_lon, n_lat = mesh.shape["lon"], mesh.shape["lat"]

    def shards(tokens, grad_out, w_qkv, w_out, band_count, lat_shift, lon_shift):
        half = tokens.shape[-1]
        width = w_qkv.shape[1]
        own = width // (n_lon * n_lat)
        cut = half // NX
        rest = NZ * NX * own
        vmem = pl.BlockSpec(memory_space=pltpu.VMEM)
        smem = pl.BlockSpec(memory_space=pltpu.SMEM)
        hbm = pl.BlockSpec(memory_space=pltpu.HBM)
        dma = pltpu.SemaphoreType.DMA
        gtok, gw = pl.pallas_call(
            functools.partial(kernel, (n_lon, n_lat, width, half)),
            out_shape=(
                pltpu.VMEM((WLAT, WLON, LEV, half), BF16),
                pltpu.VMEM((3, own, half), F32),
            ),
            in_specs=[smem] * 2 + [hbm] * 5,
            out_specs=(vmem, vmem),
            scratch_shapes=[
                pltpu.VMEM((3, width, half), BF16),
                pltpu.VMEM((half, width), BF16),
                pltpu.SMEM(band_count.shape, jnp.int32),
                pltpu.VMEM((2, WLAT, WLON, LEV, half), BF16),
                pltpu.VMEM((WLAT + HALF_ROWS, 2 * WLON, LEV, half), BF16),
                pltpu.VMEM((WLAT + HALF_ROWS, 2 * WLON, LEV, half), BF16),
                pltpu.VMEM((2, HALF_ROWS, WLON, LEV, half), BF16),
                pltpu.VMEM((2, TOK, half), BF16),
                pltpu.VMEM((2, NX, 2, TOK, half), BF16),
                pltpu.VMEM((2, TOK, half), BF16),
                pltpu.VMEM((TOK, TOK), F32),
                pltpu.VMEM((half // HEAD_DIM, TOK, TOK), F32),
                pltpu.VMEM((3, TOK, half), BF16),
                pltpu.VMEM((TOK, half), BF16),
                pltpu.VMEM((3, NX, TOK, cut), BF16),
                pltpu.VMEM((2, NX, TOK, cut), BF16),
                pltpu.VMEM((3, NX, TOK, cut), BF16),
                pltpu.VMEM((2, TOK, half), F32),
                pltpu.VMEM((TOK, half), F32),
                pltpu.VMEM((WLAT, WLON, LEV, half), BF16),
                pltpu.VMEM((WLAT + HALF_ROWS, WLON, LEV, half), BF16),
                pltpu.VMEM((HALF_ROWS, WLON, LEV, half), BF16),
                pltpu.VMEM((WLAT, WLON, LEV, half), BF16),
                pltpu.VMEM((WLAT, 2 * WLON, LEV, half), BF16),
                pltpu.VMEM((2, WLAT, HALF_COLS, LEV, half), BF16),
                pltpu.VMEM((3, n_lon * n_lat, own, cut), F32),
                pltpu.VMEM((3, NX, rest, cut), BF16),
                pltpu.VMEM((3, NX, rest, cut), BF16),
                pltpu.VMEM((3, NZ, NX * own, cut), F32),
                pltpu.VMEM((3, NZ, NX * own, cut), BF16),
                pltpu.VMEM((3, NZ, NX * own, cut), BF16),
                pltpu.VMEM((NX, 3, own, cut), F32),
                pltpu.VMEM((NX, 3, own, cut), F32),
                dma((7,)),
                dma((3, 5)),
                dma((3, 5)),
                dma((3,)),
                dma((3,)),
                dma((2, NX)),
                dma((2, NX)),
                dma((2, NX)),
                dma((2, NX)),
                dma((3, NX)),
                dma((3, NX)),
                dma((3, NX)),
                dma((3, NX)),
                dma((3, NZ)),
                dma((3, NZ)),
                dma((3, NX)),
                dma((3, NX)),
            ],
            compiler_params=pltpu.CompilerParams(
                collective_id=0, has_side_effects=True, vmem_limit_bytes=60 * 2**20
            ),
        )(
            lat_shift,
            lon_shift,
            *(
                pltpu.with_memory_space_constraint(array, pltpu.HBM)
                for array in (
                    band_count,
                    tokens.transpose(1, 2, 0, 3),
                    grad_out.transpose(1, 2, 0, 3),
                    w_qkv,
                    w_out,
                )
            )
        )
        return gtok.transpose(2, 0, 1, 3), gw

    in_specs = (
        P(None, "lat", "lon", "head"),
        P(None, "lat", "lon", "head"),
        P(None, None, "head"),
        P("head", None),
        P(),
        P(),
        P(),
    )
    out_specs = (P(None, "lat", "lon", "head"), P(None, ("lon", "lat"), "head"))
    return jax.shard_map(shards, mesh=mesh, in_specs=in_specs, out_specs=out_specs, check_vma=False)
```

```python
import functools

import jax
import jax.numpy as jnp
from jax import lax
from jax.experimental import pallas as pl
from jax.experimental.pallas import tpu as pltpu
from jax.sharding import PartitionSpec as P

MESH = pl.DeviceIdType.MESH
HEAD_DIM = 64
LEV = 2
WLAT = 12
WLON = 6
NX = 4
NZ = 8
TOK = LEV * WLAT * WLON
ROW = LEV * WLON
HALF_ROWS = WLAT // 2
HALF_COLS = WLON // 2
F32 = jnp.float32
BF16 = jnp.bfloat16


def nn(a, b):
    return lax.dot_general(a, b, (((1,), (0,)), ((), ())), preferred_element_type=F32)


def nt(a, b):
    return lax.dot_general(a, b, (((1,), (1,)), ((), ())), preferred_element_type=F32)


def tn(a, b):
    return lax.dot_general(a, b, (((0,), (0,)), ((), ())), preferred_element_type=F32)


def iota(shape, axis):
    return lax.broadcasted_iota(jnp.int32, shape, axis)


def by12(t):
    return (t * 342) >> 12


def kernel(
    sizes,
    lat_ref,
    lon_ref,
    band_hbm,
    tok_hbm,
    gout_hbm,
    wqkv_hbm,
    wout_hbm,
    gtok_ref,
    gw_ref,
    wqkv,
    wout,
    band_ref,
    own_block,
    tok_wide,
    gout_wide,
    lat_send,
    xo,
    xg,
    go,
    bias,
    probs_of,
    qkv,
    ga,
    gall,
    own_qk,
    g_recv,
    gin,
    gin_recv,
    back_own,
    back_rows,
    back_send,
    side_own,
    side_cols,
    side_send,
    parts,
    psend,
    precv,
    rz,
    zsend,
    zrecv,
    rf,
    frecv,
    load_sem,
    halo_send_sem,
    halo_recv_sem,
    core_send_sem,
    core_recv_sem,
    xg_send_sem,
    xg_recv_sem,
    relay_send_sem,
    relay_recv_sem,
    g_send_sem,
    g_recv_sem,
    p_send_sem,
    p_recv_sem,
    z_send_sem,
    z_recv_sem,
    f_send_sem,
    f_recv_sem,
):
    n_lon, n_lat, width, half = sizes
    n_ylo = n_lon // (NX * NZ)
    n_y = n_lat * n_ylo
    assert n_y == NX
    cut = half // NX
    lon = lax.axis_index("lon")
    lat = lax.axis_index("lat")
    core = lax.axis_index("head")
    x = lon % NX
    z = (lon // NX) % NZ
    ylo = lon // (NX * NZ)
    y = lat * n_ylo + ylo

    right = ((lon + 1) % n_lon, lat, core)
    left = ((lon + n_lon - 1) % n_lon, lat, core)
    across = (lon, (lat + 1) % n_lat, core)
    across_right = ((lon + 1) % n_lon, (lat + 1) % n_lat, core)
    across_left = ((lon + n_lon - 1) % n_lon, (lat + 1) % n_lat, core)
    sibling = (lon, lat, 1 - core)

    def x_peer(d):
        return (lon - x + (x + d) % NX, lat, core)

    def y_peer(d):
        other = (y + d) % n_y
        return (lon + (other % n_ylo - ylo) * (NX * NZ), other // n_ylo, core)

    def z_peer(d):
        return (lon + ((z + d) % NZ - z) * NX, lat, core)

    far_x = sorted(range(1, NX), key=lambda d: -min(d, NX - d))
    far_z = sorted(range(1, NZ), key=lambda d: -min(d, NZ - d))

    def either(for_first, for_second):
        return for_first + core * (for_second - for_first)

    def wide_peer(d):
        return tuple(either(a, b) for a, b in zip(x_peer(d)[:2], y_peer(d)[:2])) + (core,)

    def slim_peer(d):
        return tuple(either(a, b) for a, b in zip(y_peer(d)[:2], x_peer(d)[:2])) + (core,)

    wide_at = either(x, y)
    slim_at = either(y, x)

    def x_block(i):
        return i * n_lat

    def y_block(i):
        return (i % n_ylo) * (NZ * NX * n_lat) + i // n_ylo

    def wide_block(i):
        return either(x_block(i), y_block(i))

    def slim_block(i):
        return either(y_block(i), x_block(i))

    partners = [right, left, across, across_right, across_left, sibling]
    partners += [x_peer(d) for d in range(1, NX)]
    partners += [y_peer(d) for d in range(1, n_y)]
    partners += [z_peer(d) for d in range(1, NZ)]

    def remote(src, dst, send_sem, recv_sem, device):
        return pltpu.make_async_remote_copy(
            src_ref=src,
            dst_ref=dst,
            send_sem=send_sem,
            recv_sem=recv_sem,
            device_id=device,
            device_id_type=MESH,
        )

    barrier = pltpu.get_barrier_semaphore()
    for partner in partners:
        pl.semaphore_signal(barrier, inc=1, device_id=partner, device_id_type=MESH)

    load_band = pltpu.make_async_copy(band_hbm, band_ref, load_sem.at[0])
    load_band.start()
    inputs = (tok_hbm, gout_hbm)
    wides = (tok_wide, gout_wide)
    middle = slice(HALF_COLS, HALF_COLS + WLON)
    loads = []
    for a in range(2):
        loads.append(pltpu.make_async_copy(inputs[a], own_block.at[a], load_sem.at[1 + a]))
        loads.append(
            pltpu.make_async_copy(inputs[a], wides[a].at[0:WLAT, middle], load_sem.at[3 + a])
        )
    for load in loads:
        load.start()
    loads.append(pltpu.make_async_copy(wqkv_hbm, wqkv, load_sem.at[5]))
    loads.append(pltpu.make_async_copy(wout_hbm, wout, load_sem.at[6]))

    row_shift = lat_ref[0]
    col_shift = lon_ref[0]
    row_swap = jnp.where(row_shift > HALF_ROWS, 1, 0)
    col_swap = jnp.where(col_shift > HALF_COLS, 1, 0)
    f = row_shift - WLAT * row_swap
    e = col_shift - WLON * col_swap

    pl.semaphore_wait(barrier, len(partners))

    halo = []
    before = slice(0, HALF_COLS)
    after = slice(HALF_COLS + WLON, 2 * WLON)
    left_half = slice(0, HALF_COLS)
    right_half = slice(HALF_COLS, WLON)
    kept = slice(0, WLAT)
    borrowed = slice(WLAT, WLAT + HALF_ROWS)
    for a in range(2):
        routes = (
            (inputs[a].at[:, left_half], kept, after, left),
            (inputs[a].at[:, right_half], kept, before, right),
            (lat_send.at[a], borrowed, middle, across),
            (lat_send.at[a, :, left_half], borrowed, after, across_left),
            (lat_send.at[a, :, right_half], borrowed, before, across_right),
        )
        halo.append(
            [
                remote(
                    src,
                    wides[a].at[rows, columns],
                    halo_send_sem.at[a, n],
                    halo_recv_sem.at[a, n],
                    device,
                )
                for n, (src, rows, columns, device) in enumerate(routes)
            ]
        )
    for copies in halo:
        copies[0].start()
        copies[1].start()
    loads[0].wait()
    loads[2].wait()
    for a, copies in enumerate(halo):
        lat_send[a] = own_block[a, pl.ds(HALF_ROWS * row_swap, HALF_ROWS)]
        for copy in copies[2:]:
            copy.start()
    loads[4].start()
    loads[5].start()
    sends = [copy for copies in halo for copy in copies]

    load_band.wait()
    k_at = iota((TOK, TOK), 0)
    q_at = iota((TOK, TOK), 1)
    first_row = WLAT * ((lat + row_swap) % n_lat) + row_shift
    k_row = by12(k_at)
    q_row = by12(q_at)
    n_rows = WLAT * n_lat
    counts = jnp.zeros((TOK, TOK), jnp.int32)
    for r in range(WLAT):
        raw = first_row + r
        counts = jnp.where(k_row == r, band_ref[jnp.where(raw >= n_rows, raw - n_rows, raw)], counts)
    n_cols = WLON * n_lon
    k_col = ((k_at - ROW * k_row) >> 1) + (WLON * lon + e)
    k_col = jnp.where(k_col < 0, k_col + n_cols, k_col)
    k_col = jnp.where(k_col >= n_cols, k_col - n_cols, k_col)
    same_side = (k_row + first_row >= n_rows) == (q_row + first_row >= n_rows)
    allowed = ((k_col < counts) | (k_at == q_at)) & same_side
    bias[...] = jnp.where(allowed, 0.0, -1e30)

    over_core = []
    over_plane = {}

    def make_window(a):
        loads[2 * a + 1].wait()
        for copy in halo[a]:
            copy.wait_recv()
        columns = pl.ds(e + HALF_COLS, WLON)
        picked = []
        for r in range(WLAT):
            q = f + r
            picked.append(wides[a][jnp.where(q < 0, q + (WLAT + HALF_ROWS), q), columns])
        held = (xo, go)[a]
        held[core] = jnp.stack(picked).reshape(TOK, half)
        mine = held.at[core]
        copy = remote(mine, mine, core_send_sem.at[a], core_recv_sem.at[a], sibling)
        copy.start()
        over_core.append(copy)

    make_window(0)
    for d in far_x:
        for axis, peer in ((0, x_peer(d)), (1, y_peer(d))):
            copy = remote(
                xo.at[core],
                xg.at[axis, d, core],
                xg_send_sem.at[axis, d],
                xg_recv_sem.at[axis, d],
                peer,
            )
            copy.start()
            over_plane[axis, d] = copy
    sends += list(over_plane.values())

    loads[4].wait()
    over_core[0].wait_recv()
    for j in range(3):
        total = nn(xo[0], wqkv[j, :half]) + nn(xo[1], wqkv[j, half:])
        qkv[j] = total.astype(BF16)

    scale = HEAD_DIM ** (-0.5)
    order = []
    for t in range(2):
        at = slice(t * HEAD_DIM, (t + 1) * HEAD_DIM)
        for d in far_x + [0]:
            pair = (wide_at + d) % NX
            lanes = pl.ds(pl.multiple_of(pair * cut, cut), cut)
            order.append((t, at, d, pair, lanes))
    for n, (t, at, d, pair, lanes) in enumerate(order):
        scores = nt(qkv[1, :, lanes][:, at], qkv[0, :, lanes][:, at]) * scale
        scores = jnp.where(bias[...] == 0.0, scores, -1e30)
        raised = jnp.exp(scores - jnp.max(scores, 0, keepdims=True))
        probs_of[n] = raised * (1.0 / jnp.sum(raised, 0, keepdims=True))

    make_window(1)
    sends += over_core
    loads[5].wait()
    over_core[1].wait_recv()
    ga[...] = (nt(go[0], wout[:, :half]) + nt(go[1], wout[:, half:])).astype(BF16)

    def factor_peer(t, d):
        return wide_peer(d) if t < 2 else slim_peer(d)

    def sum_peer(t, d):
        return slim_peer(d) if t < 2 else wide_peer(d)

    relays = {}

    def relay(d):
        for axis in range(2):
            over_plane[axis, d].wait_recv()
            mine = xg.at[axis, d, core]
            copy = remote(
                mine, mine, relay_send_sem.at[axis, d], relay_recv_sem.at[axis, d], sibling
            )
            copy.start()
            relays[axis, d] = copy

    over_g = {}
    for n, (t, at, d, pair, lanes) in enumerate(order):
        q, k, v = (qkv[j, :, lanes][:, at] for j in range(3))
        g = ga[:, lanes][:, at]
        probs = probs_of[n]
        grad_probs = nt(v, g)
        inner = jnp.sum(probs * grad_probs, 0, keepdims=True)
        grad_scores = (probs * (grad_probs - inner) * scale).astype(BF16)
        grad_q = tn(grad_scores, k).astype(BF16)
        grad_k = nn(grad_scores, q).astype(BF16)
        gall[0, pair, :, at] = grad_q
        gall[1, pair, :, at] = grad_k
        gall[2, pair, :, at] = nn(probs.astype(BF16), g).astype(BF16)
        own_qk[t, d] = jnp.concatenate([grad_q, grad_k], 1)
        if d:
            copy = remote(
                own_qk.at[t, d],
                g_recv.at[t, d],
                g_send_sem.at[t, d],
                g_recv_sem.at[t, d],
                factor_peer(t, d),
            )
            copy.start()
            over_g[t, d] = copy
    for d in far_x:
        copy = remote(
            gall.at[2, (slim_at + d) % NX],
            g_recv.at[2, d],
            g_send_sem.at[2, d],
            g_recv_sem.at[2, d],
            factor_peer(2, d),
        )
        copy.start()
        over_g[2, d] = copy
    sends += list(over_g.values())

    def grad_in(which):
        rows = pl.ds(pl.multiple_of(which * half, half), half)
        total = 0.0
        for j in range(3):
            joined = jnp.concatenate([gall[j, pair] for pair in range(NX)], 1)
            total = total + nt(joined, wqkv[j, rows])
        return total

    gin[0] = grad_in(1 - core)
    to_sibling = remote(gin.at[0], gin_recv, core_send_sem.at[2], core_recv_sem.at[2], sibling)
    to_sibling.start()
    blocks = parts.shape[1]
    own = parts.shape[2]
    sides = [slice(0, blocks // 2), slice(blocks // 2, blocks)]
    for t in range(3):
        for side, rows in enumerate(sides):
            product = tn(xo[side], own_qk[t, 0] if t < 2 else gall[2, slim_at])
            parts[t, rows] = product.reshape(blocks // 2, own, cut)
    for d in reversed(far_x):
        relay(d)
    sends += list(relays.values())

    gin[1] = grad_in(core)

    to_sibling.wait_recv()
    window = (gin[1] + gin_recv[...]).astype(BF16).reshape(WLAT, WLON, LEV, half)
    back_own[...] = window
    back_rows[0:WLAT] = window
    for k in range(HALF_ROWS):
        from_row = k + jnp.where(f > 0, WLAT, -HALF_ROWS) - f
        back_send[k] = back_own[jnp.clip(from_row, 0, WLAT - 1)]
    over_lat_back = remote(
        back_send,
        back_rows.at[WLAT : WLAT + HALF_ROWS],
        halo_send_sem.at[2, 0],
        halo_recv_sem.at[2, 0],
        across,
    )
    over_lat_back.start()

    def make_product(t):
        axis = core if t < 2 else 1 - core
        halves = [parts[t, rows].reshape(half, cut) for rows in sides]
        for d in reversed(far_x):
            if t == 0:
                relays[0, d].wait_recv()
                relays[1, d].wait_recv()
            over_g[t, d].wait_recv()
            for side in range(2):
                halves[side] = halves[side] + tn(xg[axis, d, side], g_recv[t, d])
        for side, rows in enumerate(sides):
            parts[t, rows] = halves[side].reshape(blocks // 2, own, cut)

    def owner_rows(t, i):
        base = slim_block(i) if t < 2 else wide_block(i)
        picked = []
        for k in range(NZ):
            for j in range(NX):
                along = wide_block(j) if t < 2 else slim_block(j)
                picked.append(parts[t, base + along + k * (NX * n_lat)])
        return jnp.concatenate(picked, 0)

    over_p = {}
    for t in range(3):
        make_product(t)
        place = slim_at if t < 2 else wide_at
        for d in far_x:
            psend[t, d] = owner_rows(t, (place + d) % NX).astype(BF16)
            copy = remote(
                psend.at[t, d],
                precv.at[t, d],
                p_send_sem.at[t, d],
                p_recv_sem.at[t, d],
                sum_peer(t, d),
            )
            copy.start()
            over_p[t, d] = copy

    over_lat_back.wait_recv()
    for b in range(WLAT):
        was = b - f
        home = (was >= 0) & (was < WLAT)
        row = back_rows[jnp.where(home, was, b + WLAT - HALF_ROWS * row_swap)]
        side_own[b] = row
        side_cols[b, 0:WLON] = row
    for s in range(HALF_COLS):
        side_send[0, :, s] = side_own[:, jnp.clip(s - HALF_COLS - e, 0, WLON - 1)]
        side_send[1, :, s] = side_own[:, jnp.clip(s + WLON - e, 0, WLON - 1)]
    side_left = remote(
        side_send.at[0],
        side_cols.at[:, WLON + HALF_COLS : 2 * WLON],
        halo_send_sem.at[2, 1],
        halo_recv_sem.at[2, 1],
        left,
    )
    side_right = remote(
        side_send.at[1],
        side_cols.at[:, WLON : WLON + HALF_COLS],
        halo_send_sem.at[2, 2],
        halo_recv_sem.at[2, 2],
        right,
    )
    side_left.start()
    side_right.start()

    for copy in sends:
        copy.wait_send()

    over_z = {}
    for t in range(3):
        total = owner_rows(t, slim_at if t < 2 else wide_at)
        for d in range(1, NX):
            over_p[t, d].wait_recv()
            total = total + precv[t, d].astype(F32)
        rz[t] = total.reshape(NZ, NX * own, cut)
        for d in far_z:
            zsend[t, d] = rz[t, (z + d) % NZ].astype(BF16)
            copy = remote(
                zsend.at[t, d],
                zrecv.at[t, d],
                z_send_sem.at[t, d],
                z_recv_sem.at[t, d],
                z_peer(d),
            )
            copy.start()
            over_z[t, d] = copy
    for copy in list(over_p.values()) + [to_sibling, over_lat_back, side_left, side_right]:
        copy.wait_send()

    side_left.wait_recv()
    side_right.wait_recv()
    for q in range(WLON):
        c = q - e
        home = (c >= 0) & (c < WLON)
        gtok_ref[:, q] = side_cols[:, jnp.where(home, c, q + WLON)]

    last = {}
    for t in range(3):
        total = rz[t, z]
        for d in range(1, NZ):
            over_z[t, d].wait_recv()
            total = total + zrecv[t, d].astype(F32)
        rf[:, t] = total.reshape(NX, own, cut)
        if t == 0:
            continue
        group = slice(0, 2) if t == 1 else slice(2, 3)
        place = wide_at if t == 1 else slim_at
        for d in far_x:
            copy = remote(
                rf.at[(place + d) % NX, group],
                frecv.at[d, group],
                f_send_sem.at[t, d],
                f_recv_sem.at[t, d],
                factor_peer(t, d),
            )
            copy.start()
            last[t, d] = copy
    for d in range(NX):
        if d:
            last[1, d].wait_recv()
            last[2, d].wait_recv()
            first, second, values = (frecv[d, t] for t in range(3))
        else:
            first, second, values = rf[wide_at, 0], rf[wide_at, 1], rf[slim_at, 2]
        lanes = pl.ds(pl.multiple_of(((wide_at + NX - d) % NX) * cut, cut), cut)
        for j in range(2):
            at = slice(j * HEAD_DIM, (j + 1) * HEAD_DIM)
            gw_ref[j, :, lanes] = jnp.concatenate([first[:, at], second[:, at]], 1)
        lanes = pl.ds(pl.multiple_of(((slim_at + NX - d) % NX) * cut, cut), cut)
        gw_ref[2, :, lanes] = values

    for copy in list(over_z.values()) + list(last.values()):
        copy.wait_send()


def write_out(gtok_vmem, gw_vmem, gtok_hbm, gw_hbm, sem):
    copies = [
        pltpu.make_async_copy(gtok_vmem, gtok_hbm, sem.at[0]),
        pltpu.make_async_copy(gw_vmem, gw_hbm, sem.at[1]),
    ]
    for copy in copies:
        copy.start()
    for copy in copies:
        copy.wait()


def solution(mesh):
    n_lon, n_lat = mesh.shape["lon"], mesh.shape["lat"]

    def shards(tokens, grad_out, w_qkv, w_out, band_count, lat_shift, lon_shift):
        half = tokens.shape[-1]
        width = w_qkv.shape[1]
        own = width // (n_lon * n_lat)
        cut = half // NX
        rest = NZ * NX * own
        vmem = pl.BlockSpec(memory_space=pltpu.VMEM)
        smem = pl.BlockSpec(memory_space=pltpu.SMEM)
        hbm = pl.BlockSpec(memory_space=pltpu.HBM)
        dma = pltpu.SemaphoreType.DMA
        gtok, gw = pl.pallas_call(
            functools.partial(kernel, (n_lon, n_lat, width, half)),
            out_shape=(
                pltpu.VMEM((WLAT, WLON, LEV, half), BF16),
                pltpu.VMEM((3, own, half), F32),
            ),
            in_specs=[smem] * 2 + [hbm] * 5,
            out_specs=(vmem, vmem),
            scratch_shapes=[
                pltpu.VMEM((3, width, half), BF16),
                pltpu.VMEM((half, width), BF16),
                pltpu.SMEM(band_count.shape, jnp.int32),
                pltpu.VMEM((2, WLAT, WLON, LEV, half), BF16),
                pltpu.VMEM((WLAT + HALF_ROWS, 2 * WLON, LEV, half), BF16),
                pltpu.VMEM((WLAT + HALF_ROWS, 2 * WLON, LEV, half), BF16),
                pltpu.VMEM((2, HALF_ROWS, WLON, LEV, half), BF16),
                pltpu.VMEM((2, TOK, half), BF16),
                pltpu.VMEM((2, NX, 2, TOK, half), BF16),
                pltpu.VMEM((2, TOK, half), BF16),
                pltpu.VMEM((TOK, TOK), F32),
                pltpu.VMEM((half // HEAD_DIM, TOK, TOK), F32),
                pltpu.VMEM((3, TOK, half), BF16),
                pltpu.VMEM((TOK, half), BF16),
                pltpu.VMEM((3, NX, TOK, cut), BF16),
                pltpu.VMEM((2, NX, TOK, cut), BF16),
                pltpu.VMEM((3, NX, TOK, cut), BF16),
                pltpu.VMEM((2, TOK, half), F32),
                pltpu.VMEM((TOK, half), F32),
                pltpu.VMEM((WLAT, WLON, LEV, half), BF16),
                pltpu.VMEM((WLAT + HALF_ROWS, WLON, LEV, half), BF16),
                pltpu.VMEM((HALF_ROWS, WLON, LEV, half), BF16),
                pltpu.VMEM((WLAT, WLON, LEV, half), BF16),
                pltpu.VMEM((WLAT, 2 * WLON, LEV, half), BF16),
                pltpu.VMEM((2, WLAT, HALF_COLS, LEV, half), BF16),
                pltpu.VMEM((3, n_lon * n_lat, own, cut), F32),
                pltpu.VMEM((3, NX, rest, cut), BF16),
                pltpu.VMEM((3, NX, rest, cut), BF16),
                pltpu.VMEM((3, NZ, NX * own, cut), F32),
                pltpu.VMEM((3, NZ, NX * own, cut), BF16),
                pltpu.VMEM((3, NZ, NX * own, cut), BF16),
                pltpu.VMEM((NX, 3, own, cut), F32),
                pltpu.VMEM((NX, 3, own, cut), F32),
                dma((7,)),
                dma((3, 5)),
                dma((3, 5)),
                dma((3,)),
                dma((3,)),
                dma((2, NX)),
                dma((2, NX)),
                dma((2, NX)),
                dma((2, NX)),
                dma((3, NX)),
                dma((3, NX)),
                dma((3, NX)),
                dma((3, NX)),
                dma((3, NZ)),
                dma((3, NZ)),
                dma((3, NX)),
                dma((3, NX)),
            ],
            compiler_params=pltpu.CompilerParams(
                collective_id=0, has_side_effects=True, vmem_limit_bytes=60 * 2**20
            ),
        )(
            lat_shift,
            lon_shift,
            *(
                pltpu.with_memory_space_constraint(array, pltpu.HBM)
                for array in (
                    band_count,
                    tokens.transpose(1, 2, 0, 3),
                    grad_out.transpose(1, 2, 0, 3),
                    w_qkv,
                    w_out,
                )
            )
        )
        gtok, gw = pl.pallas_call(
            write_out,
            out_shape=(
                jax.ShapeDtypeStruct(gtok.shape, BF16),
                jax.ShapeDtypeStruct(gw.shape, F32),
            ),
            in_specs=[vmem, vmem],
            out_specs=(hbm, hbm),
            scratch_shapes=[dma((2,))],
        )(gtok, gw)
        return gtok.transpose(2, 0, 1, 3), gw

    in_specs = (
        P(None, "lat", "lon", "head"),
        P(None, "lat", "lon", "head"),
        P(None, None, "head"),
        P("head", None),
        P(),
        P(),
        P(),
    )
    out_specs = (P(None, "lat", "lon", "head"), P(None, ("lon", "lat"), "head"))
    return jax.shard_map(shards, mesh=mesh, in_specs=in_specs, out_specs=out_specs, check_vma=False)
```

```python
import functools

import jax
import jax.numpy as jnp
from jax import lax
from jax.experimental import pallas as pl
from jax.experimental.pallas import tpu as pltpu
from jax.sharding import PartitionSpec as P

MESH = pl.DeviceIdType.MESH
HEAD_DIM = 64
LEV = 2
WLAT = 12
WLON = 6
NX = 4
NZ = 8
TOK = LEV * WLAT * WLON
ROW = LEV * WLON
HALF_ROWS = WLAT // 2
HALF_COLS = WLON // 2
F32 = jnp.float32
BF16 = jnp.bfloat16


def nn(a, b):
    return lax.dot_general(a, b, (((1,), (0,)), ((), ())), preferred_element_type=F32)


def nt(a, b):
    return lax.dot_general(a, b, (((1,), (1,)), ((), ())), preferred_element_type=F32)


def tn(a, b):
    return lax.dot_general(a, b, (((0,), (0,)), ((), ())), preferred_element_type=F32)


def iota(shape, axis):
    return lax.broadcasted_iota(jnp.int32, shape, axis)


def by12(t):
    return (t * 342) >> 12


def kernel(
    sizes,
    lat_ref,
    lon_ref,
    band_hbm,
    tok_hbm,
    gout_hbm,
    wqkv_hbm,
    wout_hbm,
    gtok_ref,
    gw_ref,
    wqkv,
    wout,
    band_ref,
    own_block,
    tok_wide,
    gout_wide,
    lat_send,
    xo,
    xg,
    go,
    bias,
    probs_of,
    qkv,
    ga,
    gall,
    own_qk,
    g_recv,
    gin,
    gin_recv,
    back_own,
    back_rows,
    back_send,
    side_own,
    side_cols,
    side_send,
    parts,
    psend,
    precv,
    rz,
    zsend,
    zrecv,
    rf,
    frecv,
    load_sem,
    halo_send_sem,
    halo_recv_sem,
    core_send_sem,
    core_recv_sem,
    xg_send_sem,
    xg_recv_sem,
    relay_send_sem,
    relay_recv_sem,
    g_send_sem,
    g_recv_sem,
    p_send_sem,
    p_recv_sem,
    z_send_sem,
    z_recv_sem,
    f_send_sem,
    f_recv_sem,
):
    n_lon, n_lat, width, half = sizes
    n_ylo = n_lon // (NX * NZ)
    n_y = n_lat * n_ylo
    assert n_y == NX
    cut = half // NX
    lon = lax.axis_index("lon")
    lat = lax.axis_index("lat")
    core = lax.axis_index("head")
    x = lon % NX
    z = (lon // NX) % NZ
    ylo = lon // (NX * NZ)
    y = lat * n_ylo + ylo

    right = ((lon + 1) % n_lon, lat, core)
    left = ((lon + n_lon - 1) % n_lon, lat, core)
    across = (lon, (lat + 1) % n_lat, core)
    across_right = ((lon + 1) % n_lon, (lat + 1) % n_lat, core)
    across_left = ((lon + n_lon - 1) % n_lon, (lat + 1) % n_lat, core)
    sibling = (lon, lat, 1 - core)

    def x_peer(d):
        return (lon - x + (x + d) % NX, lat, core)

    def y_peer(d):
        other = (y + d) % n_y
        return (lon + (other % n_ylo - ylo) * (NX * NZ), other // n_ylo, core)

    def z_peer(d):
        return (lon + ((z + d) % NZ - z) * NX, lat, core)

    far_x = sorted(range(1, NX), key=lambda d: -min(d, NX - d))
    far_z = sorted(range(1, NZ), key=lambda d: -min(d, NZ - d))

    def either(for_first, for_second):
        return for_first + core * (for_second - for_first)

    def wide_peer(d):
        return tuple(either(a, b) for a, b in zip(x_peer(d)[:2], y_peer(d)[:2])) + (core,)

    def slim_peer(d):
        return tuple(either(a, b) for a, b in zip(y_peer(d)[:2], x_peer(d)[:2])) + (core,)

    wide_at = either(x, y)
    slim_at = either(y, x)

    def x_block(i):
        return i * n_lat

    def y_block(i):
        return (i % n_ylo) * (NZ * NX * n_lat) + i // n_ylo

    def wide_block(i):
        return either(x_block(i), y_block(i))

    def slim_block(i):
        return either(y_block(i), x_block(i))

    partners = [right, left, across, across_right, across_left, sibling]
    partners += [x_peer(d) for d in range(1, NX)]
    partners += [y_peer(d) for d in range(1, n_y)]
    partners += [z_peer(d) for d in range(1, NZ)]

    def remote(src, dst, send_sem, recv_sem, device):
        return pltpu.make_async_remote_copy(
            src_ref=src,
            dst_ref=dst,
            send_sem=send_sem,
            recv_sem=recv_sem,
            device_id=device,
            device_id_type=MESH,
        )

    barrier = pltpu.get_barrier_semaphore()
    for partner in partners:
        pl.semaphore_signal(barrier, inc=1, device_id=partner, device_id_type=MESH)

    load_band = pltpu.make_async_copy(band_hbm, band_ref, load_sem.at[0])
    load_band.start()
    inputs = (tok_hbm, gout_hbm)
    wides = (tok_wide, gout_wide)
    middle = slice(HALF_COLS, HALF_COLS + WLON)
    loads = []
    for a in range(2):
        loads.append(pltpu.make_async_copy(inputs[a], own_block.at[a], load_sem.at[1 + a]))
        loads.append(
            pltpu.make_async_copy(inputs[a], wides[a].at[0:WLAT, middle], load_sem.at[3 + a])
        )
    for load in loads:
        load.start()
    loads.append(pltpu.make_async_copy(wqkv_hbm, wqkv, load_sem.at[5]))
    loads.append(pltpu.make_async_copy(wout_hbm, wout, load_sem.at[6]))

    row_shift = lat_ref[0]
    col_shift = lon_ref[0]
    row_swap = jnp.where(row_shift > HALF_ROWS, 1, 0)
    col_swap = jnp.where(col_shift > HALF_COLS, 1, 0)
    f = row_shift - WLAT * row_swap
    e = col_shift - WLON * col_swap

    pl.semaphore_wait(barrier, len(partners))

    halo = []
    before = slice(1, HALF_COLS)
    after = slice(HALF_COLS + WLON, 2 * WLON)
    left_half = slice(0, HALF_COLS)
    right_half = slice(HALF_COLS + 1, WLON)
    kept = slice(0, WLAT)
    borrowed = slice(WLAT, WLAT + HALF_ROWS)
    for a in range(2):
        routes = (
            (inputs[a].at[:, left_half], kept, after, left),
            (inputs[a].at[:, right_half], kept, before, right),
            (lat_send.at[a], borrowed, middle, across),
            (lat_send.at[a, :, left_half], borrowed, after, across_left),
            (lat_send.at[a, :, right_half], borrowed, before, across_right),
        )
        halo.append(
            [
                remote(
                    src,
                    wides[a].at[rows, columns],
                    halo_send_sem.at[a, n],
                    halo_recv_sem.at[a, n],
                    device,
                )
                for n, (src, rows, columns, device) in enumerate(routes)
            ]
        )
    for copies in halo:
        copies[0].start()
        copies[1].start()
    loads[0].wait()
    loads[2].wait()
    for a, copies in enumerate(halo):
        lat_send[a] = own_block[a, pl.ds(HALF_ROWS * row_swap, HALF_ROWS)]
        for copy in copies[2:]:
            copy.start()
    loads[4].start()
    loads[5].start()
    sends = [copy for copies in halo for copy in copies]

    load_band.wait()
    k_at = iota((TOK, TOK), 0)
    q_at = iota((TOK, TOK), 1)
    first_row = WLAT * ((lat + row_swap) % n_lat) + row_shift
    k_row = by12(k_at)
    q_row = by12(q_at)
    n_rows = WLAT * n_lat
    counts = jnp.zeros((TOK, TOK), jnp.int32)
    for r in range(WLAT):
        raw = first_row + r
        counts = jnp.where(k_row == r, band_ref[jnp.where(raw >= n_rows, raw - n_rows, raw)], counts)
    n_cols = WLON * n_lon
    k_col = ((k_at - ROW * k_row) >> 1) + (WLON * lon + e)
    k_col = jnp.where(k_col < 0, k_col + n_cols, k_col)
    k_col = jnp.where(k_col >= n_cols, k_col - n_cols, k_col)
    same_side = (k_row + first_row >= n_rows) == (q_row + first_row >= n_rows)
    allowed = ((k_col < counts) | (k_at == q_at)) & same_side
    bias[...] = jnp.where(allowed, 0.0, -1e30)

    over_core = []
    over_plane = {}

    def make_window(a):
        loads[2 * a + 1].wait()
        for copy in halo[a]:
            copy.wait_recv()
        columns = pl.ds(e + HALF_COLS, WLON)
        picked = []
        for r in range(WLAT):
            q = f + r
            picked.append(wides[a][jnp.where(q < 0, q + (WLAT + HALF_ROWS), q), columns])
        held = (xo, go)[a]
        held[core] = jnp.stack(picked).reshape(TOK, half)
        mine = held.at[core]
        copy = remote(mine, mine, core_send_sem.at[a], core_recv_sem.at[a], sibling)
        copy.start()
        over_core.append(copy)

    make_window(0)
    for d in far_x:
        for role, peer in enumerate((wide_peer(d), slim_peer(d))):
            copy = remote(
                xo.at[core],
                xg.at[role, d, core],
                xg_send_sem.at[role, d],
                xg_recv_sem.at[role, d],
                peer,
            )
            copy.start()
            over_plane[role, d] = copy
    sends += list(over_plane.values())

    loads[4].wait()
    over_core[0].wait_recv()
    for j in range(3):
        total = nn(xo[0], wqkv[j, :half]) + nn(xo[1], wqkv[j, half:])
        qkv[j] = total.astype(BF16)

    scale = HEAD_DIM ** (-0.5)
    order = []
    for t in range(2):
        at = slice(t * HEAD_DIM, (t + 1) * HEAD_DIM)
        for d in far_x + [0]:
            pair = (wide_at + d) % NX
            lanes = pl.ds(pl.multiple_of(pair * cut, cut), cut)
            order.append((t, at, d, pair, lanes))
    for n, (t, at, d, pair, lanes) in enumerate(order):
        scores = nt(qkv[1, :, lanes][:, at], qkv[0, :, lanes][:, at]) * scale
        scores = jnp.where(bias[...] == 0.0, scores, -1e30)
        raised = jnp.exp(scores - jnp.max(scores, 0, keepdims=True))
        probs_of[n] = raised * (1.0 / jnp.sum(raised, 0, keepdims=True))

    make_window(1)
    sends += over_core
    loads[5].wait()
    over_core[1].wait_recv()
    ga[...] = (nt(go[0], wout[:, :half]) + nt(go[1], wout[:, half:])).astype(BF16)

    def factor_peer(t, d):
        return wide_peer(d) if t < 2 else slim_peer(d)

    def sum_peer(t, d):
        return slim_peer(d) if t < 2 else wide_peer(d)

    relays = {}

    def relay(role, d):
        over_plane[role, d].wait_recv()
        copy = remote(
            xg.at[role, d, core],
            xg.at[1 - role, d, core],
            relay_send_sem.at[role, d],
            relay_recv_sem.at[1 - role, d],
            sibling,
        )
        copy.start()
        relays[1 - role, d] = copy

    over_g = {}
    for n, (t, at, d, pair, lanes) in enumerate(order):
        q, k, v = (qkv[j, :, lanes][:, at] for j in range(3))
        g = ga[:, lanes][:, at]
        probs = probs_of[n]
        grad_probs = nt(v, g)
        inner = jnp.sum(probs * grad_probs, 0, keepdims=True)
        grad_scores = (probs * (grad_probs - inner) * scale).astype(BF16)
        grad_q = tn(grad_scores, k).astype(BF16)
        grad_k = nn(grad_scores, q).astype(BF16)
        gall[0, pair, :, at] = grad_q
        gall[1, pair, :, at] = grad_k
        gall[2, pair, :, at] = nn(probs.astype(BF16), g).astype(BF16)
        own_qk[t, d] = jnp.concatenate([grad_q, grad_k], 1)
        if d:
            copy = remote(
                own_qk.at[t, d],
                g_recv.at[t, d],
                g_send_sem.at[t, d],
                g_recv_sem.at[t, d],
                factor_peer(t, d),
            )
            copy.start()
            over_g[t, d] = copy
    for d in far_x:
        copy = remote(
            gall.at[2, (slim_at + d) % NX],
            g_recv.at[2, d],
            g_send_sem.at[2, d],
            g_recv_sem.at[2, d],
            factor_peer(2, d),
        )
        copy.start()
        over_g[2, d] = copy
    sends += list(over_g.values())

    def grad_in(which):
        rows = pl.ds(pl.multiple_of(which * half, half), half)
        total = 0.0
        for j in range(3):
            joined = jnp.concatenate([gall[j, pair] for pair in range(NX)], 1)
            total = total + nt(joined, wqkv[j, rows])
        return total

    gin[0] = grad_in(1 - core)
    to_sibling = remote(gin.at[0], gin_recv, core_send_sem.at[2], core_recv_sem.at[2], sibling)
    to_sibling.start()
    blocks = parts.shape[1]
    own = parts.shape[2]
    sides = [slice(0, blocks // 2), slice(blocks // 2, blocks)]
    for t in range(3):
        for side, rows in enumerate(sides):
            product = tn(xo[side], own_qk[t, 0] if t < 2 else gall[2, slim_at])
            parts[t, rows] = product.reshape(blocks // 2, own, cut)
    for role in (1, 0):
        for d in reversed(far_x):
            relay(role, d)
    sends += list(relays.values())

    gin[1] = grad_in(core)

    to_sibling.wait_recv()
    window = (gin[1] + gin_recv[...]).astype(BF16).reshape(WLAT, WLON, LEV, half)
    back_own[...] = window
    back_rows[0:WLAT] = window
    for k in range(HALF_ROWS):
        from_row = k + jnp.where(f > 0, WLAT, -HALF_ROWS) - f
        back_send[k] = back_own[jnp.clip(from_row, 0, WLAT - 1)]
    over_lat_back = remote(
        back_send,
        back_rows.at[WLAT : WLAT + HALF_ROWS],
        halo_send_sem.at[2, 0],
        halo_recv_sem.at[2, 0],
        across,
    )
    over_lat_back.start()

    def make_product(t):
        role = 0 if t < 2 else 1
        halves = [parts[t, rows].reshape(half, cut) for rows in sides]
        for d in reversed(far_x):
            if t != 1:
                relays[role, d].wait_recv()
            over_g[t, d].wait_recv()
            for side in range(2):
                halves[side] = halves[side] + tn(xg[role, d, side], g_recv[t, d])
        for side, rows in enumerate(sides):
            parts[t, rows] = halves[side].reshape(blocks // 2, own, cut)

    def owner_rows(t, i):
        base = slim_block(i) if t < 2 else wide_block(i)
        picked = []
        for k in range(NZ):
            for j in range(NX):
                along = wide_block(j) if t < 2 else slim_block(j)
                picked.append(parts[t, base + along + k * (NX * n_lat)])
        return jnp.concatenate(picked, 0)

    over_p = {}
    for t in range(3):
        make_product(t)
        place = slim_at if t < 2 else wide_at
        for d in far_x:
            psend[t, d] = owner_rows(t, (place + d) % NX).astype(BF16)
            copy = remote(
                psend.at[t, d],
                precv.at[t, d],
                p_send_sem.at[t, d],
                p_recv_sem.at[t, d],
                sum_peer(t, d),
            )
            copy.start()
            over_p[t, d] = copy

    over_lat_back.wait_recv()
    for b in range(WLAT):
        was = b - f
        home = (was >= 0) & (was < WLAT)
        row = back_rows[jnp.where(home, was, b + WLAT - HALF_ROWS * row_swap)]
        side_own[b] = row
        side_cols[b, 0:WLON] = row
    for s in range(HALF_COLS):
        side_send[0, :, s] = side_own[:, jnp.clip(s - HALF_COLS - e, 0, WLON - 1)]
        side_send[1, :, s] = side_own[:, jnp.clip(s + WLON - e, 0, WLON - 1)]
    side_left = remote(
        side_send.at[0],
        side_cols.at[:, WLON + HALF_COLS : 2 * WLON],
        halo_send_sem.at[2, 1],
        halo_recv_sem.at[2, 1],
        left,
    )
    side_right = remote(
        side_send.at[1],
        side_cols.at[:, WLON : WLON + HALF_COLS],
        halo_send_sem.at[2, 2],
        halo_recv_sem.at[2, 2],
        right,
    )
    side_left.start()
    side_right.start()

    for copy in sends:
        copy.wait_send()

    over_z = {}
    for t in range(3):
        total = owner_rows(t, slim_at if t < 2 else wide_at)
        for d in range(1, NX):
            over_p[t, d].wait_recv()
            total = total + precv[t, d].astype(F32)
        rz[t] = total.reshape(NZ, NX * own, cut)
        for d in far_z:
            zsend[t, d] = rz[t, (z + d) % NZ].astype(BF16)
            copy = remote(
                zsend.at[t, d],
                zrecv.at[t, d],
                z_send_sem.at[t, d],
                z_recv_sem.at[t, d],
                z_peer(d),
            )
            copy.start()
            over_z[t, d] = copy
    for copy in list(over_p.values()) + [to_sibling, over_lat_back, side_left, side_right]:
        copy.wait_send()

    side_left.wait_recv()
    side_right.wait_recv()
    for q in range(WLON):
        c = q - e
        home = (c >= 0) & (c < WLON)
        gtok_ref[:, q] = side_cols[:, jnp.where(home, c, q + WLON)]

    last = {}
    for t in range(3):
        total = rz[t, z]
        for d in range(1, NZ):
            over_z[t, d].wait_recv()
            total = total + zrecv[t, d].astype(F32)
        rf[:, t] = total.reshape(NX, own, cut)
        if t == 0:
            continue
        group = slice(0, 2) if t == 1 else slice(2, 3)
        place = wide_at if t == 1 else slim_at
        for d in far_x:
            copy = remote(
                rf.at[(place + d) % NX, group],
                frecv.at[d, group],
                f_send_sem.at[t, d],
                f_recv_sem.at[t, d],
                factor_peer(t, d),
            )
            copy.start()
            last[t, d] = copy
    for d in range(NX):
        if d:
            last[1, d].wait_recv()
            last[2, d].wait_recv()
            first, second, values = (frecv[d, t] for t in range(3))
        else:
            first, second, values = rf[wide_at, 0], rf[wide_at, 1], rf[slim_at, 2]
        lanes = pl.ds(pl.multiple_of(((wide_at + NX - d) % NX) * cut, cut), cut)
        for j in range(2):
            at = slice(j * HEAD_DIM, (j + 1) * HEAD_DIM)
            gw_ref[j, :, lanes] = jnp.concatenate([first[:, at], second[:, at]], 1)
        lanes = pl.ds(pl.multiple_of(((slim_at + NX - d) % NX) * cut, cut), cut)
        gw_ref[2, :, lanes] = values

    for copy in list(over_z.values()) + list(last.values()):
        copy.wait_send()


def solution(mesh):
    n_lon, n_lat = mesh.shape["lon"], mesh.shape["lat"]

    def shards(tokens, grad_out, w_qkv, w_out, band_count, lat_shift, lon_shift):
        half = tokens.shape[-1]
        width = w_qkv.shape[1]
        own = width // (n_lon * n_lat)
        cut = half // NX
        rest = NZ * NX * own
        vmem = pl.BlockSpec(memory_space=pltpu.VMEM)
        smem = pl.BlockSpec(memory_space=pltpu.SMEM)
        hbm = pl.BlockSpec(memory_space=pltpu.HBM)
        dma = pltpu.SemaphoreType.DMA
        gtok, gw = pl.pallas_call(
            functools.partial(kernel, (n_lon, n_lat, width, half)),
            out_shape=(
                pltpu.VMEM((WLAT, WLON, LEV, half), BF16),
                pltpu.VMEM((3, own, half), F32),
            ),
            in_specs=[smem] * 2 + [hbm] * 5,
            out_specs=(vmem, vmem),
            scratch_shapes=[
                pltpu.VMEM((3, width, half), BF16),
                pltpu.VMEM((half, width), BF16),
                pltpu.SMEM(band_count.shape, jnp.int32),
                pltpu.VMEM((2, WLAT, WLON, LEV, half), BF16),
                pltpu.VMEM((WLAT + HALF_ROWS, 2 * WLON, LEV, half), BF16),
                pltpu.VMEM((WLAT + HALF_ROWS, 2 * WLON, LEV, half), BF16),
                pltpu.VMEM((2, HALF_ROWS, WLON, LEV, half), BF16),
                pltpu.VMEM((2, TOK, half), BF16),
                pltpu.VMEM((2, NX, 2, TOK, half), BF16),
                pltpu.VMEM((2, TOK, half), BF16),
                pltpu.VMEM((TOK, TOK), F32),
                pltpu.VMEM((half // HEAD_DIM, TOK, TOK), F32),
                pltpu.VMEM((3, TOK, half), BF16),
                pltpu.VMEM((TOK, half), BF16),
                pltpu.VMEM((3, NX, TOK, cut), BF16),
                pltpu.VMEM((2, NX, TOK, cut), BF16),
                pltpu.VMEM((3, NX, TOK, cut), BF16),
                pltpu.VMEM((2, TOK, half), F32),
                pltpu.VMEM((TOK, half), F32),
                pltpu.VMEM((WLAT, WLON, LEV, half), BF16),
                pltpu.VMEM((WLAT + HALF_ROWS, WLON, LEV, half), BF16),
                pltpu.VMEM((HALF_ROWS, WLON, LEV, half), BF16),
                pltpu.VMEM((WLAT, WLON, LEV, half), BF16),
                pltpu.VMEM((WLAT, 2 * WLON, LEV, half), BF16),
                pltpu.VMEM((2, WLAT, HALF_COLS, LEV, half), BF16),
                pltpu.VMEM((3, n_lon * n_lat, own, cut), F32),
                pltpu.VMEM((3, NX, rest, cut), BF16),
                pltpu.VMEM((3, NX, rest, cut), BF16),
                pltpu.VMEM((3, NZ, NX * own, cut), F32),
                pltpu.VMEM((3, NZ, NX * own, cut), BF16),
                pltpu.VMEM((3, NZ, NX * own, cut), BF16),
                pltpu.VMEM((NX, 3, own, cut), F32),
                pltpu.VMEM((NX, 3, own, cut), F32),
                dma((7,)),
                dma((3, 5)),
                dma((3, 5)),
                dma((3,)),
                dma((3,)),
                dma((2, NX)),
                dma((2, NX)),
                dma((2, NX)),
                dma((2, NX)),
                dma((3, NX)),
                dma((3, NX)),
                dma((3, NX)),
                dma((3, NX)),
                dma((3, NZ)),
                dma((3, NZ)),
                dma((3, NX)),
                dma((3, NX)),
            ],
            compiler_params=pltpu.CompilerParams(
                collective_id=0, has_side_effects=True, vmem_limit_bytes=60 * 2**20
            ),
        )(
            lat_shift,
            lon_shift,
            *(
                pltpu.with_memory_space_constraint(array, pltpu.HBM)
                for array in (
                    band_count,
                    tokens.transpose(1, 2, 0, 3),
                    grad_out.transpose(1, 2, 0, 3),
                    w_qkv,
                    w_out,
                )
            )
        )
        return gtok.transpose(2, 0, 1, 3), gw

    in_specs = (
        P(None, "lat", "lon", "head"),
        P(None, "lat", "lon", "head"),
        P(None, None, "head"),
        P("head", None),
        P(),
        P(),
        P(),
    )
    out_specs = (P(None, "lat", "lon", "head"), P(None, ("lon", "lat"), "head"))
    return jax.shard_map(shards, mesh=mesh, in_specs=in_specs, out_specs=out_specs, check_vma=False)
```

```python
import functools

import jax
import jax.numpy as jnp
from jax import lax
from jax.experimental import pallas as pl
from jax.experimental.pallas import tpu as pltpu
from jax.sharding import PartitionSpec as P

MESH = pl.DeviceIdType.MESH
HEAD_DIM = 64
LEV = 2
WLAT = 12
WLON = 6
NX = 4
NZ = 8
TOK = LEV * WLAT * WLON
ROW = LEV * WLON
HALF_ROWS = WLAT // 2
HALF_COLS = WLON // 2
F32 = jnp.float32
BF16 = jnp.bfloat16


def nn(a, b):
    return lax.dot_general(a, b, (((1,), (0,)), ((), ())), preferred_element_type=F32)


def nt(a, b):
    return lax.dot_general(a, b, (((1,), (1,)), ((), ())), preferred_element_type=F32)


def tn(a, b):
    return lax.dot_general(a, b, (((0,), (0,)), ((), ())), preferred_element_type=F32)


def iota(shape, axis):
    return lax.broadcasted_iota(jnp.int32, shape, axis)


def by12(t):
    return (t * 342) >> 12


def kernel(
    sizes,
    lat_ref,
    lon_ref,
    band_hbm,
    tok_hbm,
    gout_hbm,
    wqkv_hbm,
    wout_hbm,
    gtok_ref,
    gw_ref,
    wqkv,
    wout,
    band_ref,
    own_block,
    tok_wide,
    gout_wide,
    lat_send,
    xo,
    xg,
    go,
    bias,
    probs_of,
    qkv,
    ga,
    gall,
    own_qk,
    g_recv,
    gin,
    gin_recv,
    back_own,
    back_rows,
    back_send,
    side_own,
    side_cols,
    side_send,
    parts,
    psend,
    precv,
    rz,
    zsend,
    zrecv,
    rf,
    frecv,
    load_sem,
    halo_send_sem,
    halo_recv_sem,
    core_send_sem,
    core_recv_sem,
    xg_send_sem,
    xg_recv_sem,
    relay_send_sem,
    relay_recv_sem,
    g_send_sem,
    g_recv_sem,
    p_send_sem,
    p_recv_sem,
    z_send_sem,
    z_recv_sem,
    f_send_sem,
    f_recv_sem,
):
    n_lon, n_lat, width, half = sizes
    n_ylo = n_lon // (NX * NZ)
    n_y = n_lat * n_ylo
    assert n_y == NX
    cut = half // NX
    lon = lax.axis_index("lon")
    lat = lax.axis_index("lat")
    core = lax.axis_index("head")
    x = lon % NX
    z = (lon // NX) % NZ
    ylo = lon // (NX * NZ)
    y = lat * n_ylo + ylo

    right = ((lon + 1) % n_lon, lat, core)
    left = ((lon + n_lon - 1) % n_lon, lat, core)
    across = (lon, (lat + 1) % n_lat, core)
    across_right = ((lon + 1) % n_lon, (lat + 1) % n_lat, core)
    across_left = ((lon + n_lon - 1) % n_lon, (lat + 1) % n_lat, core)
    sibling = (lon, lat, 1 - core)

    def x_peer(d):
        return (lon - x + (x + d) % NX, lat, core)

    def y_peer(d):
        other = (y + d) % n_y
        return (lon + (other % n_ylo - ylo) * (NX * NZ), other // n_ylo, core)

    def z_peer(d):
        return (lon + ((z + d) % NZ - z) * NX, lat, core)

    far_x = sorted(range(1, NX), key=lambda d: -min(d, NX - d))
    far_z = sorted(range(1, NZ), key=lambda d: -min(d, NZ - d))

    def either(for_first, for_second):
        return for_first + core * (for_second - for_first)

    def wide_peer(d):
        return tuple(either(a, b) for a, b in zip(x_peer(d)[:2], y_peer(d)[:2])) + (core,)

    def slim_peer(d):
        return tuple(either(a, b) for a, b in zip(y_peer(d)[:2], x_peer(d)[:2])) + (core,)

    wide_at = either(x, y)
    slim_at = either(y, x)

    def x_block(i):
        return i * n_lat

    def y_block(i):
        return (i % n_ylo) * (NZ * NX * n_lat) + i // n_ylo

    def wide_block(i):
        return either(x_block(i), y_block(i))

    def slim_block(i):
        return either(y_block(i), x_block(i))

    partners = [right, left, across, across_right, across_left, sibling]
    partners += [x_peer(d) for d in range(1, NX)]
    partners += [y_peer(d) for d in range(1, n_y)]
    partners += [z_peer(d) for d in range(1, NZ)]

    def remote(src, dst, send_sem, recv_sem, device):
        return pltpu.make_async_remote_copy(
            src_ref=src,
            dst_ref=dst,
            send_sem=send_sem,
            recv_sem=recv_sem,
            device_id=device,
            device_id_type=MESH,
        )

    barrier = pltpu.get_barrier_semaphore()
    for partner in partners:
        pl.semaphore_signal(barrier, inc=1, device_id=partner, device_id_type=MESH)

    load_band = pltpu.make_async_copy(band_hbm, band_ref, load_sem.at[0])
    load_band.start()
    inputs = (tok_hbm, gout_hbm)
    wides = (tok_wide, gout_wide)
    middle = slice(HALF_COLS, HALF_COLS + WLON)
    loads = []
    for a in range(2):
        loads.append(pltpu.make_async_copy(inputs[a], own_block.at[a], load_sem.at[1 + a]))
        loads.append(
            pltpu.make_async_copy(inputs[a], wides[a].at[0:WLAT, middle], load_sem.at[3 + a])
        )
    for load in loads:
        load.start()
    loads.append(pltpu.make_async_copy(wqkv_hbm, wqkv, load_sem.at[5]))
    loads.append(pltpu.make_async_copy(wout_hbm, wout, load_sem.at[6]))
    loads[4].start()
    loads[5].start()

    row_shift = lat_ref[0]
    col_shift = lon_ref[0]
    row_swap = jnp.where(row_shift > HALF_ROWS, 1, 0)
    col_swap = jnp.where(col_shift > HALF_COLS, 1, 0)
    f = row_shift - WLAT * row_swap
    e = col_shift - WLON * col_swap

    pl.semaphore_wait(barrier, len(partners))

    halo = []
    before = slice(1, HALF_COLS)
    after = slice(HALF_COLS + WLON, 2 * WLON)
    left_half = slice(0, HALF_COLS)
    right_half = slice(HALF_COLS + 1, WLON)
    kept = slice(0, WLAT)
    borrowed = slice(WLAT, WLAT + HALF_ROWS)
    for a in range(2):
        routes = (
            (own_block.at[a, :, left_half], kept, after, left),
            (own_block.at[a, :, right_half], kept, before, right),
            (lat_send.at[a], borrowed, middle, across),
            (lat_send.at[a, :, left_half], borrowed, after, across_left),
            (lat_send.at[a, :, right_half], borrowed, before, across_right),
        )
        halo.append(
            [
                remote(
                    src,
                    wides[a].at[rows, columns],
                    halo_send_sem.at[a, n],
                    halo_recv_sem.at[a, n],
                    device,
                )
                for n, (src, rows, columns, device) in enumerate(routes)
            ]
        )
    loads[0].wait()
    loads[2].wait()
    for copies in halo:
        copies[0].start()
        copies[1].start()
    for a, copies in enumerate(halo):
        lat_send[a] = own_block[a, pl.ds(HALF_ROWS * row_swap, HALF_ROWS)]
        for copy in copies[2:]:
            copy.start()
    sends = [copy for copies in halo for copy in copies]

    load_band.wait()
    k_at = iota((TOK, TOK), 0)
    q_at = iota((TOK, TOK), 1)
    first_row = WLAT * ((lat + row_swap) % n_lat) + row_shift
    k_row = by12(k_at)
    q_row = by12(q_at)
    n_rows = WLAT * n_lat
    counts = jnp.zeros((TOK, TOK), jnp.int32)
    for r in range(WLAT):
        raw = first_row + r
        counts = jnp.where(k_row == r, band_ref[jnp.where(raw >= n_rows, raw - n_rows, raw)], counts)
    n_cols = WLON * n_lon
    k_col = ((k_at - ROW * k_row) >> 1) + (WLON * lon + e)
    k_col = jnp.where(k_col < 0, k_col + n_cols, k_col)
    k_col = jnp.where(k_col >= n_cols, k_col - n_cols, k_col)
    same_side = (k_row + first_row >= n_rows) == (q_row + first_row >= n_rows)
    allowed = ((k_col < counts) | (k_at == q_at)) & same_side
    bias[...] = jnp.where(allowed, 0.0, -1e30)

    over_core = []
    over_plane = {}

    def make_window(a):
        loads[2 * a + 1].wait()
        for copy in halo[a]:
            copy.wait_recv()
        columns = pl.ds(e + HALF_COLS, WLON)
        picked = []
        for r in range(WLAT):
            q = f + r
            picked.append(wides[a][jnp.where(q < 0, q + (WLAT + HALF_ROWS), q), columns])
        held = (xo, go)[a]
        held[core] = jnp.stack(picked).reshape(TOK, half)
        mine = held.at[core]
        copy = remote(mine, mine, core_send_sem.at[a], core_recv_sem.at[a], sibling)
        copy.start()
        over_core.append(copy)

    make_window(0)
    for d in far_x:
        for role, peer in enumerate((wide_peer(d), slim_peer(d))):
            copy = remote(
                xo.at[core],
                xg.at[role, d, core],
                xg_send_sem.at[role, d],
                xg_recv_sem.at[role, d],
                peer,
            )
            copy.start()
            over_plane[role, d] = copy
    sends += list(over_plane.values())

    loads[4].wait()
    over_core[0].wait_recv()
    for j in range(3):
        total = nn(xo[0], wqkv[j, :half]) + nn(xo[1], wqkv[j, half:])
        qkv[j] = total.astype(BF16)

    scale = HEAD_DIM ** (-0.5)
    order = []
    for t in range(2):
        at = slice(t * HEAD_DIM, (t + 1) * HEAD_DIM)
        for d in far_x + [0]:
            pair = (wide_at + d) % NX
            lanes = pl.ds(pl.multiple_of(pair * cut, cut), cut)
            order.append((t, at, d, pair, lanes))
    for n, (t, at, d, pair, lanes) in enumerate(order):
        scores = nt(qkv[1, :, lanes][:, at], qkv[0, :, lanes][:, at]) * scale
        scores = jnp.where(bias[...] == 0.0, scores, -1e30)
        raised = jnp.exp(scores - jnp.max(scores, 0, keepdims=True))
        probs_of[n] = raised * (1.0 / jnp.sum(raised, 0, keepdims=True))

    make_window(1)
    sends += over_core
    loads[5].wait()
    over_core[1].wait_recv()
    ga[...] = (nt(go[0], wout[:, :half]) + nt(go[1], wout[:, half:])).astype(BF16)

    def factor_peer(t, d):
        return wide_peer(d) if t < 2 else slim_peer(d)

    def sum_peer(t, d):
        return slim_peer(d) if t < 2 else wide_peer(d)

    relays = {}

    def relay(role, d):
        over_plane[role, d].wait_recv()
        copy = remote(
            xg.at[role, d, core],
            xg.at[1 - role, d, core],
            relay_send_sem.at[role, d],
            relay_recv_sem.at[1 - role, d],
            sibling,
        )
        copy.start()
        relays[1 - role, d] = copy

    over_g = {}
    for n, (t, at, d, pair, lanes) in enumerate(order):
        q, k, v = (qkv[j, :, lanes][:, at] for j in range(3))
        g = ga[:, lanes][:, at]
        probs = probs_of[n]
        grad_probs = nt(v, g)
        inner = jnp.sum(probs * grad_probs, 0, keepdims=True)
        grad_scores = (probs * (grad_probs - inner) * scale).astype(BF16)
        grad_q = tn(grad_scores, k).astype(BF16)
        grad_k = nn(grad_scores, q).astype(BF16)
        gall[0, pair, :, at] = grad_q
        gall[1, pair, :, at] = grad_k
        gall[2, pair, :, at] = nn(probs.astype(BF16), g).astype(BF16)
        own_qk[t, d] = jnp.concatenate([grad_q, grad_k], 1)
        if d:
            copy = remote(
                own_qk.at[t, d],
                g_recv.at[t, d],
                g_send_sem.at[t, d],
                g_recv_sem.at[t, d],
                factor_peer(t, d),
            )
            copy.start()
            over_g[t, d] = copy
    for d in far_x:
        copy = remote(
            gall.at[2, (slim_at + d) % NX],
            g_recv.at[2, d],
            g_send_sem.at[2, d],
            g_recv_sem.at[2, d],
            factor_peer(2, d),
        )
        copy.start()
        over_g[2, d] = copy
    sends += list(over_g.values())

    def grad_in(which):
        rows = pl.ds(pl.multiple_of(which * half, half), half)
        total = 0.0
        for j in range(3):
            joined = jnp.concatenate([gall[j, pair] for pair in range(NX)], 1)
            total = total + nt(joined, wqkv[j, rows])
        return total

    gin[0] = grad_in(1 - core)
    to_sibling = remote(gin.at[0], gin_recv, core_send_sem.at[2], core_recv_sem.at[2], sibling)
    to_sibling.start()
    blocks = parts.shape[1]
    own = parts.shape[2]
    sides = [slice(0, blocks // 2), slice(blocks // 2, blocks)]
    for t in range(3):
        for side, rows in enumerate(sides):
            product = tn(xo[side], own_qk[t, 0] if t < 2 else gall[2, slim_at])
            parts[t, rows] = product.reshape(blocks // 2, own, cut)
    for role in (1, 0):
        for d in reversed(far_x):
            relay(role, d)
    sends += list(relays.values())

    gin[1] = grad_in(core)

    to_sibling.wait_recv()
    window = (gin[1] + gin_recv[...]).astype(BF16).reshape(WLAT, WLON, LEV, half)
    back_own[...] = window
    back_rows[0:WLAT] = window
    for k in range(HALF_ROWS):
        from_row = k + jnp.where(f > 0, WLAT, -HALF_ROWS) - f
        back_send[k] = back_own[jnp.clip(from_row, 0, WLAT - 1)]
    over_lat_back = remote(
        back_send,
        back_rows.at[WLAT : WLAT + HALF_ROWS],
        halo_send_sem.at[2, 0],
        halo_recv_sem.at[2, 0],
        across,
    )
    over_lat_back.start()

    def make_product(t):
        role = 0 if t < 2 else 1
        halves = [parts[t, rows].reshape(half, cut) for rows in sides]
        for d in reversed(far_x):
            if t != 1:
                relays[role, d].wait_recv()
            over_g[t, d].wait_recv()
            for side in range(2):
                halves[side] = halves[side] + tn(xg[role, d, side], g_recv[t, d])
        for side, rows in enumerate(sides):
            parts[t, rows] = halves[side].reshape(blocks // 2, own, cut)

    def owner_rows(t, i):
        base = slim_block(i) if t < 2 else wide_block(i)
        picked = []
        for k in range(NZ):
            for j in range(NX):
                along = wide_block(j) if t < 2 else slim_block(j)
                picked.append(parts[t, base + along + k * (NX * n_lat)])
        return jnp.concatenate(picked, 0)

    over_p = {}
    for t in range(3):
        make_product(t)
        place = slim_at if t < 2 else wide_at
        for d in far_x:
            psend[t, d] = owner_rows(t, (place + d) % NX).astype(BF16)
            copy = remote(
                psend.at[t, d],
                precv.at[t, d],
                p_send_sem.at[t, d],
                p_recv_sem.at[t, d],
                sum_peer(t, d),
            )
            copy.start()
            over_p[t, d] = copy

    over_lat_back.wait_recv()
    for b in range(WLAT):
        was = b - f
        home = (was >= 0) & (was < WLAT)
        row = back_rows[jnp.where(home, was, b + WLAT - HALF_ROWS * row_swap)]
        side_own[b] = row
        side_cols[b, 0:WLON] = row
    for s in range(HALF_COLS):
        side_send[0, :, s] = side_own[:, jnp.clip(s - HALF_COLS - e, 0, WLON - 1)]
        side_send[1, :, s] = side_own[:, jnp.clip(s + WLON - e, 0, WLON - 1)]
    side_left = remote(
        side_send.at[0],
        side_cols.at[:, WLON + HALF_COLS : 2 * WLON],
        halo_send_sem.at[2, 1],
        halo_recv_sem.at[2, 1],
        left,
    )
    side_right = remote(
        side_send.at[1],
        side_cols.at[:, WLON : WLON + HALF_COLS],
        halo_send_sem.at[2, 2],
        halo_recv_sem.at[2, 2],
        right,
    )
    side_left.start()
    side_right.start()

    for copy in sends:
        copy.wait_send()

    over_z = {}
    for t in range(3):
        total = owner_rows(t, slim_at if t < 2 else wide_at)
        for d in range(1, NX):
            over_p[t, d].wait_recv()
            total = total + precv[t, d].astype(F32)
        rz[t] = total.reshape(NZ, NX * own, cut)
        for d in far_z:
            zsend[t, d] = rz[t, (z + d) % NZ].astype(BF16)
            copy = remote(
                zsend.at[t, d],
                zrecv.at[t, d],
                z_send_sem.at[t, d],
                z_recv_sem.at[t, d],
                z_peer(d),
            )
            copy.start()
            over_z[t, d] = copy
    for copy in list(over_p.values()) + [to_sibling, over_lat_back, side_left, side_right]:
        copy.wait_send()

    side_left.wait_recv()
    side_right.wait_recv()
    for q in range(WLON):
        c = q - e
        home = (c >= 0) & (c < WLON)
        gtok_ref[:, q] = side_cols[:, jnp.where(home, c, q + WLON)]

    last = {}
    for t in range(3):
        total = rz[t, z]
        for d in range(1, NZ):
            over_z[t, d].wait_recv()
            total = total + zrecv[t, d].astype(F32)
        rf[:, t] = total.reshape(NX, own, cut)
        if t == 0:
            continue
        group = slice(0, 2) if t == 1 else slice(2, 3)
        place = wide_at if t == 1 else slim_at
        for d in far_x:
            copy = remote(
                rf.at[(place + d) % NX, group],
                frecv.at[d, group],
                f_send_sem.at[t, d],
                f_recv_sem.at[t, d],
                factor_peer(t, d),
            )
            copy.start()
            last[t, d] = copy
    for copy in over_z.values():
        copy.wait_send()
    for d in range(NX):
        if d:
            last[1, d].wait_recv()
            last[2, d].wait_recv()
            first, second, values = (frecv[d, t] for t in range(3))
        else:
            first, second, values = rf[wide_at, 0], rf[wide_at, 1], rf[slim_at, 2]
        lanes = pl.ds(pl.multiple_of(((wide_at + NX - d) % NX) * cut, cut), cut)
        for j in range(2):
            at = slice(j * HEAD_DIM, (j + 1) * HEAD_DIM)
            gw_ref[j, :, lanes] = jnp.concatenate([first[:, at], second[:, at]], 1)
        lanes = pl.ds(pl.multiple_of(((slim_at + NX - d) % NX) * cut, cut), cut)
        gw_ref[2, :, lanes] = values

    for copy in last.values():
        copy.wait_send()


def solution(mesh):
    n_lon, n_lat = mesh.shape["lon"], mesh.shape["lat"]

    def shards(tokens, grad_out, w_qkv, w_out, band_count, lat_shift, lon_shift):
        half = tokens.shape[-1]
        width = w_qkv.shape[1]
        own = width // (n_lon * n_lat)
        cut = half // NX
        rest = NZ * NX * own
        vmem = pl.BlockSpec(memory_space=pltpu.VMEM)
        smem = pl.BlockSpec(memory_space=pltpu.SMEM)
        hbm = pl.BlockSpec(memory_space=pltpu.HBM)
        dma = pltpu.SemaphoreType.DMA
        gtok, gw = pl.pallas_call(
            functools.partial(kernel, (n_lon, n_lat, width, half)),
            out_shape=(
                pltpu.VMEM((WLAT, WLON, LEV, half), BF16),
                pltpu.VMEM((3, own, half), F32),
            ),
            in_specs=[smem] * 2 + [hbm] * 5,
            out_specs=(vmem, vmem),
            scratch_shapes=[
                pltpu.VMEM((3, width, half), BF16),
                pltpu.VMEM((half, width), BF16),
                pltpu.SMEM(band_count.shape, jnp.int32),
                pltpu.VMEM((2, WLAT, WLON, LEV, half), BF16),
                pltpu.VMEM((WLAT + HALF_ROWS, 2 * WLON, LEV, half), BF16),
                pltpu.VMEM((WLAT + HALF_ROWS, 2 * WLON, LEV, half), BF16),
                pltpu.VMEM((2, HALF_ROWS, WLON, LEV, half), BF16),
                pltpu.VMEM((2, TOK, half), BF16),
                pltpu.VMEM((2, NX, 2, TOK, half), BF16),
                pltpu.VMEM((2, TOK, half), BF16),
                pltpu.VMEM((TOK, TOK), F32),
                pltpu.VMEM((half // HEAD_DIM, TOK, TOK), F32),
                pltpu.VMEM((3, TOK, half), BF16),
                pltpu.VMEM((TOK, half), BF16),
                pltpu.VMEM((3, NX, TOK, cut), BF16),
                pltpu.VMEM((2, NX, TOK, cut), BF16),
                pltpu.VMEM((3, NX, TOK, cut), BF16),
                pltpu.VMEM((2, TOK, half), F32),
                pltpu.VMEM((TOK, half), F32),
                pltpu.VMEM((WLAT, WLON, LEV, half), BF16),
                pltpu.VMEM((WLAT + HALF_ROWS, WLON, LEV, half), BF16),
                pltpu.VMEM((HALF_ROWS, WLON, LEV, half), BF16),
                pltpu.VMEM((WLAT, WLON, LEV, half), BF16),
                pltpu.VMEM((WLAT, 2 * WLON, LEV, half), BF16),
                pltpu.VMEM((2, WLAT, HALF_COLS, LEV, half), BF16),
                pltpu.VMEM((3, n_lon * n_lat, own, cut), F32),
                pltpu.VMEM((3, NX, rest, cut), BF16),
                pltpu.VMEM((3, NX, rest, cut), BF16),
                pltpu.VMEM((3, NZ, NX * own, cut), F32),
                pltpu.VMEM((3, NZ, NX * own, cut), BF16),
                pltpu.VMEM((3, NZ, NX * own, cut), BF16),
                pltpu.VMEM((NX, 3, own, cut), F32),
                pltpu.VMEM((NX, 3, own, cut), F32),
                dma((7,)),
                dma((3, 5)),
                dma((3, 5)),
                dma((3,)),
                dma((3,)),
                dma((2, NX)),
                dma((2, NX)),
                dma((2, NX)),
                dma((2, NX)),
                dma((3, NX)),
                dma((3, NX)),
                dma((3, NX)),
                dma((3, NX)),
                dma((3, NZ)),
                dma((3, NZ)),
                dma((3, NX)),
                dma((3, NX)),
            ],
            compiler_params=pltpu.CompilerParams(
                collective_id=0, has_side_effects=True, vmem_limit_bytes=60 * 2**20
            ),
        )(
            lat_shift,
            lon_shift,
            *(
                pltpu.with_memory_space_constraint(array, pltpu.HBM)
                for array in (
                    band_count,
                    tokens.transpose(1, 2, 0, 3),
                    grad_out.transpose(1, 2, 0, 3),
                    w_qkv,
                    w_out,
                )
            )
        )
        return gtok.transpose(2, 0, 1, 3), gw

    in_specs = (
        P(None, "lat", "lon", "head"),
        P(None, "lat", "lon", "head"),
        P(None, None, "head"),
        P("head", None),
        P(),
        P(),
        P(),
    )
    out_specs = (P(None, "lat", "lon", "head"), P(None, ("lon", "lat"), "head"))
    return jax.shard_map(shards, mesh=mesh, in_specs=in_specs, out_specs=out_specs, check_vma=False)
```
